256 devices in a mesh: section: 8 (over x_hi, y), dp: 32 (over x_lo, z, core).
Axes of the slice: x: 4 (x_hi: 2, x_lo: 2; x = x_hi * 2 + x_lo), y: 4, z: 8, core: 2. Of those that a mesh axis runs over, the one named last changes fastest.
Arguments:
- section_rows: bfloat16 [8, 8192, 2048], P('section', 'dp'), may hold values from -160 to 160
- kv_weight: bfloat16 [8, 2048, 4096], P('section', 'dp'), may hold values from -0.125 to 0.125
- cotangent: bfloat16 [8, 8192, 2048], P('section', 'dp'), may hold values from -6 to 6
- gain: float32 [2048], replicated, may hold values from 0.1 to 1.9
- section_map: int32 [8], replicated, may hold values from 0 to 31, as said below
Outputs:
- section_out: bfloat16 [8, 8192, 2048], P('section', 'dp')
- section_grad: bfloat16 [8, 8192, 2048], P('section', 'dp')
- gain_grad: float32 [2048], replicated
The draws below stay inside these ranges and needn't reach their ends.
Inputs may be any that keep to these rules, and one draw needn't show every extreme that they name: `section_map`: the entries are distinct; exactly one is 0 and marks the section of the encoder's last layer, every other section holds one decoder layer.
All inputs are finite; a program needn't handle non-finite values.
Results may differ from the reference program's by a relative error of at most 0.01.
The reference program's roundings to bfloat16 on the way count: a program that leaves them out, or rounds other values in their place, can miss the bound.
Values may be sent and summed in bfloat16 or wider, within the bound.
No kernel may reach another device: no remote copies, remote signals or barrier semaphores. Data moves between devices by JAX's collectives and lax.ppermute only.
A program may use at most 128 MiB of HBM per device.

```python
import math
import jax
import jax.numpy as jnp
from jax import lax

D = 2048
HEADS = 8
HEAD = 256
LEN = 256
HD = 2048
TOKENS = 8192
N_SECTION = 8


def draw_section_rows(key, part):
    key = jax.random.fold_in(key, 11)
    base = jax.random.normal(key, (N_SECTION, TOKENS, D), jnp.float32)
    return jnp.clip(base, -5.0, 5.0).astype(jnp.bfloat16)


def draw_section_map(key, part):
    key = jax.random.fold_in(key, 23)
    first_key, second_key = jax.random.split(key)
    highest = 4 * N_SECTION - 1
    middle = jax.random.permutation(first_key, highest - 1)[:N_SECTION - 2].astype(jnp.int32) + 1
    values = jnp.concatenate([jnp.zeros((1,), jnp.int32), jnp.full((1,), highest, jnp.int32), middle])
    placing = jax.random.permutation(second_key, N_SECTION).astype(jnp.int32)
    return values[placing].astype(jnp.int32)


def shard_levels(own_key, dims, shards, low, top_value):
    level, own = 1.0, jax.random.fold_in(own_key, 6)
    for position, blocks in shards:
        steps = jnp.exp(jax.random.uniform(jax.random.fold_in(own, position), (blocks,), jnp.float32, low / len(shards), top_value / len(shards)))
        level = level * jnp.repeat(steps, dims[position] // blocks).reshape([-1 if axis == position else 1 for axis in range(len(dims))])
    return level


def normal_values(stream_key, extent, deviation, bound, pieces=(), held_as=jnp.bfloat16):
    array = jax.random.normal(stream_key, extent, jnp.float32) * deviation
    if len(pieces) > 0:
        array = shard_levels(stream_key, extent, pieces, -0.22, 0.18) * array
    return jnp.clip(array, min=-bound, max=bound).astype(held_as)


def setup_inputs(seed: int = 0) -> dict:
    arg_keys = jax.random.split(jax.random.key(seed), 6)
    return {
        "section_rows": draw_section_rows(jax.random.fold_in(arg_keys[5], 71), 0),
        "kv_weight": normal_values(arg_keys[1], (N_SECTION, D, 2 * HD), D ** -0.5, 0.125, ((0, 8), (1, 32))),
        "cotangent": normal_values(arg_keys[2], (N_SECTION, TOKENS, HD), 1.0, 6.0, ((0, 8), (1, 32))),
        "gain": jnp.clip(1.0 + 0.18 * jax.random.normal(arg_keys[3], (D,), jnp.float32), 0.1, 1.9),
        "section_map": draw_section_map(jax.random.fold_in(arg_keys[5], 71), 0),
    }


eps = 1e-06

def cross_block(queries, keys, values, grads):
    rows = queries.shape[0]
    shape = (rows // LEN, LEN, HEADS, HEAD)
    scale = 1.0 / math.sqrt(HEAD)
    q = queries.reshape(shape).astype(jnp.float32)
    k = keys.reshape(shape).astype(jnp.float32)
    v = values.reshape(shape).astype(jnp.float32)
    g = grads.reshape(shape).astype(jnp.float32)
    scores = jnp.einsum('sqhd,skhd->shqk', q, k) * scale
    probs = jax.nn.softmax(scores, axis=-1)
    rounded = lax.optimization_barrier(probs.astype(jnp.bfloat16)).astype(jnp.float32)
    context = jnp.einsum('shqk,skhd->sqhd', rounded, v)
    dprobs = jnp.einsum('sqhd,skhd->shqk', g, v)
    delta = jnp.einsum('sqhd,sqhd->shq', g, context)[..., None]
    dscores = lax.optimization_barrier((probs * (dprobs - delta)).astype(jnp.bfloat16)).astype(jnp.float32)
    dq = jnp.einsum('shqk,skhd->sqhd', dscores, k) * scale
    dk = jnp.einsum('shqk,sqhd->skhd', dscores, q) * scale
    dv = jnp.einsum('shqk,sqhd->skhd', rounded, g)
    dkv = jnp.concatenate([dk.reshape(rows, -1), dv.reshape(rows, -1)], axis=1).astype(jnp.bfloat16)
    return (context.reshape(rows, -1), dq.reshape(rows, -1), dkv)

def reference(section_rows, kv_weight, cotangent, gain, section_map):
    order = jnp.arange(N_SECTION, dtype=jnp.int32)
    root = jnp.sum(jnp.where(section_map == 0, order, 0)).astype(jnp.int32)
    hidden = lax.dynamic_index_in_dim(section_rows, root, 0, keepdims=False).astype(jnp.float32)
    inv = lax.rsqrt(lax.optimization_barrier(jnp.mean(hidden * hidden, axis=1, keepdims=True)) + eps)
    enc_out = (hidden * inv * gain).astype(jnp.bfloat16)
    total = lax.dynamic_index_in_dim(cotangent, root, 0, keepdims=False).astype(jnp.float32)
    contexts = []
    query_grads = []
    for index in range(N_SECTION):
        weight = kv_weight[index]
        projected = jnp.dot(enc_out, weight, preferred_element_type=jnp.float32).astype(jnp.bfloat16)
        context, dq, dkv = cross_block(section_rows[index], projected[:, :HD], projected[:, HD:], cotangent[index])
        d_enc = jnp.dot(dkv, weight.T, preferred_element_type=jnp.float32)
        total = total + jnp.where(section_map[index] != 0, d_enc, jnp.float32(0.0))
        contexts.append(context.astype(jnp.bfloat16))
        query_grads.append(dq.astype(jnp.bfloat16))
    gain_grad = lax.optimization_barrier(jnp.sum(total * hidden * inv, axis=0))
    mean_term = lax.optimization_barrier(jnp.mean(hidden * gain * total, axis=1, keepdims=True))
    d_hidden = (inv * gain * total - hidden * inv * inv * inv * mean_term).astype(jnp.bfloat16)
    section_out = jnp.stack([jnp.where(section_map[i] == 0, enc_out, contexts[i]) for i in range(N_SECTION)])
    section_grad = jnp.stack([jnp.where(section_map[i] == 0, d_hidden, query_grads[i]) for i in range(N_SECTION)])
    return (section_out, section_grad, gain_grad)
```

```python
import functools
import math

import jax
import jax.numpy as jnp
from jax import lax
from jax.experimental import pallas as pl
from jax.experimental.pallas import tpu as pltpu
from jax.sharding import PartitionSpec as P

HEAD = 256
LEN = 256
D = 2048
HALF = 4
F = HALF * HEAD
QUARTER = LEN // 4

eps = 1e-06
bf16 = jnp.bfloat16
f32 = jnp.float32

SLOTS = (
    (0, 0), (0, 1), (0, -1), (1, 0), (0, 2), (0, -2), (1, 1), (0, 3),
    (0, -3), (1, 2), (1, 3), (0, 4), (1, -2), (1, 4), (1, -3), (1, -1),
)
N_SLOT = len(SLOTS)
SLOT = D // N_SLOT

ANY = pl.BlockSpec(memory_space=pl.ANY)
VMEM = pl.BlockSpec(memory_space=pltpu.VMEM)
LIMIT = 56 * 1024 * 1024


def dp_swap(x, move):
    pairs = []
    for index in range(32):
        column, place, core = index // 16, (index // 2) % 8, index % 2
        column, place, core = move(column, place, core)
        pairs.append((index, (column % 2) * 16 + (place % 8) * 2 + core % 2))
    return lax.ppermute(x, "dp", pairs)


def section_swap(x, move):
    pairs = []
    for index in range(8):
        high, y = move(index // 4, index % 4)
        pairs.append((index, (high % 2) * 4 + y % 4))
    return lax.ppermute(x, "section", pairs)


def other_core(x):
    return dp_swap(x, lambda c, z, k: (c, z, k + 1))


def other_column(x):
    return dp_swap(x, lambda c, z, k: (c + 1, z, k))


def from_above(x):
    return dp_swap(x, lambda c, z, k: (c, z - 1, k))


def from_below(x):
    return dp_swap(x, lambda c, z, k: (c, z + 1, k))


def other_high(x):
    return section_swap(x, lambda h, y: (h + 1, y))


def to_y(x, step):
    return section_swap(x, lambda h, y: (h, y + step))


def gather_slots(unit):
    a, b = {0: unit}, {}
    a[1], a[-1], b[0] = from_above(a[0]), from_below(a[0]), other_column(a[0])
    a[2], a[-2], b[1] = from_above(a[1]), from_below(a[-1]), other_column(a[1])
    a[3], a[-3], b[2] = from_above(a[2]), from_below(a[-2]), other_column(a[2])
    b[3], a[4], b[-2] = from_above(b[2]), from_below(a[-3]), other_column(a[-2])
    b[4], b[-3], b[-1] = from_above(b[3]), from_below(b[-2]), other_column(a[-1])
    return [(a, b)[column][offset] for column, offset in SLOTS]


def slot_start(slot):
    dp = lax.axis_index("dp")
    column, offset = SLOTS[slot]
    column = (dp // 16 + column) % 2
    place = ((dp // 2) % 8 + offset + 8) % 8
    return pl.multiple_of((column * 8 + place) * SLOT, SLOT)


def norm_kernel(own_ref, oth_ref, gain_ref, cot_ref, enc_ref, hid_ref, gain_out, inv_ref, dh_ref, gp_ref):
    y = lax.axis_index("section") % 4
    gain = gain_ref[...]
    for seq, ref in enumerate((own_ref, oth_ref)):
        rows = pl.ds(seq * LEN, LEN)
        hidden = ref[...].astype(f32)
        inv = lax.rsqrt(jnp.mean(hidden * hidden, axis=1, keepdims=True) + eps)
        inv_ref[rows, :] = jnp.broadcast_to(inv, (LEN, 128))
        for slot in range(N_SLOT):
            start = slot_start(slot)
            to = pl.ds(slot * SLOT, SLOT)
            part = ref[:, pl.ds(start, SLOT)]
            scale = gain_ref[:, pl.ds(start, SLOT)]
            hid_ref[rows, to] = part
            enc_ref[rows, to] = (part.astype(f32) * inv * scale).astype(bf16)
            gain_out[:, to] = scale
    total = jnp.zeros((1, D), f32)
    for quarter in range(4):
        rows = pl.ds(quarter * QUARTER, QUARTER)
        cot = cot_ref[pl.ds(pl.multiple_of(((y + quarter) % 4) * QUARTER, QUARTER), QUARTER), :].astype(f32)
        hidden = own_ref[rows, :].astype(f32)
        inv = inv_ref[rows, :1]
        mean = jnp.mean(hidden * gain * cot, axis=1, keepdims=True)
        dh_ref[rows, :] = (inv * gain * cot - hidden * (inv * inv * inv * mean)).astype(bf16)
        total = total + jnp.sum(cot * hidden * inv, axis=0, keepdims=True)
    gp_ref[...] = total


def normalise(own, oth, gain, cot):
    return pl.pallas_call(
        norm_kernel,
        in_specs=[VMEM] * 4,
        out_specs=[VMEM] * 6,
        out_shape=[
            jax.ShapeDtypeStruct((2 * LEN, D), bf16),
            jax.ShapeDtypeStruct((2 * LEN, D), bf16),
            jax.ShapeDtypeStruct((1, D), f32),
            jax.ShapeDtypeStruct((2 * LEN, 128), f32),
            jax.ShapeDtypeStruct((LEN, D), bf16),
            jax.ShapeDtypeStruct((1, D), f32),
        ],
        compiler_params=pltpu.CompilerParams(vmem_limit_bytes=LIMIT),
        cost_estimate=pl.CostEstimate(flops=20_000_000, bytes_accessed=8_000_000, transcendentals=0),
        name="norm",
    )(own, oth, gain, cot)


NT = (((1,), (1,)), ((), ()))
TN = (((0,), (0,)), ((), ()))
SCALE = 1.0 / math.sqrt(HEAD)


def main_kernel(*refs):
    pieces = refs[: 2 * N_SLOT]
    (flag_ref, q_own, q_oth, g_own, g_oth, enc_in, hid_in, inv_in, gain_in, dh_enc, gp_enc,
     ctx_own, ctx_oth, dq_own, dq_oth, dh_own, dh_oth, gp_ref,
     w, enc, hid, inv_ref, gain_ref, q, g, kv, dkv, mean_ref, sems, in_sems) = refs[2 * N_SLOT:]
    core = lax.axis_index("dp") % 2
    copies = []
    small = [
        pltpu.make_async_copy(enc_in, enc, in_sems.at[0]),
        pltpu.make_async_copy(q_own, q.at[pl.ds(0, LEN), :], in_sems.at[1]),
        pltpu.make_async_copy(q_oth, q.at[pl.ds(LEN, LEN), :], in_sems.at[2]),
        pltpu.make_async_copy(g_own, g.at[pl.ds(0, LEN), :], in_sems.at[3]),
        pltpu.make_async_copy(g_oth, g.at[pl.ds(LEN, LEN), :], in_sems.at[4]),
        pltpu.make_async_copy(hid_in, hid, in_sems.at[5]),
        pltpu.make_async_copy(inv_in, inv_ref, in_sems.at[6]),
        pltpu.make_async_copy(gain_in, gain_ref, in_sems.at[7]),
    ]
    small[0].start()
    for slot in range(N_SLOT):
        for half in range(2):
            place = core if half == 0 else 1 - core
            start = pl.multiple_of(slot * SLOT + place * (SLOT // 2), SLOT // 2)
            copy = pltpu.make_async_copy(
                pieces[2 * slot + half], w.at[pl.ds(start, SLOT // 2), :], sems.at[2 * slot + half]
            )
            copy.start()
            copies.append(copy)
    for copy in small[1:]:
        copy.start()
    small[0].wait()
    for copy in copies:
        copy.wait()

    @pl.loop(0, 2 * HALF)
    def _(block):
        cols = pl.ds(pl.multiple_of(block * HEAD, HEAD), HEAD)
        kv[:, cols] = jnp.dot(enc[...], w[:, cols], preferred_element_type=f32).astype(bf16)

    for copy in small[1:]:
        copy.wait()
    mean_ref[...] = jnp.zeros_like(mean_ref)

    @pl.loop(0, HALF)
    def _(head):
        cols = pl.ds(pl.multiple_of(head * HEAD, HEAD), HEAD)
        vcols = pl.ds(pl.multiple_of(F + head * HEAD, HEAD), HEAD)
        for seq, (ctx_ref, dq_ref) in enumerate(((ctx_own, dq_own), (ctx_oth, dq_oth))):
            rows = pl.ds(seq * LEN, LEN)
            qb, gb = q[rows, cols], g[rows, cols]
            kb, vb = kv[rows, cols], kv[rows, vcols]
            scores = lax.dot_general(kb, qb, NT, preferred_element_type=f32) * SCALE
            dprobs = lax.dot_general(vb, gb, NT, preferred_element_type=f32)
            top = jnp.max(scores, axis=0, keepdims=True)
            e = jnp.exp(scores - top)
            probs = e * (1.0 / jnp.sum(e, axis=0, keepdims=True))
            rounded = probs.astype(bf16)
            delta = jnp.sum(rounded.astype(f32) * dprobs, axis=0, keepdims=True)
            dscores = (probs * (dprobs - delta)).astype(bf16)
            ctx_ref[:, cols] = lax.dot_general(rounded, vb, TN, preferred_element_type=f32).astype(bf16)
            dq_ref[:, cols] = (lax.dot_general(dscores, kb, TN, preferred_element_type=f32) * SCALE).astype(bf16)
            dk = (jnp.dot(dscores, qb, preferred_element_type=f32) * SCALE).astype(bf16)
            dv = jnp.dot(rounded, gb, preferred_element_type=f32).astype(bf16)
            dkv[rows, cols] = dk
            dkv[rows, vcols] = dv
            term = dk.astype(f32) * kb.astype(f32) + dv.astype(f32) * vb.astype(f32)
            mean_ref[rows, :] += term[:, :128] + term[:, 128:]

    inv = inv_ref[:, :1]
    mean = jnp.sum(mean_ref[...], axis=1, keepdims=True) * (1.0 / D)
    factor = inv * inv * mean

    @pl.loop(0, N_SLOT // 2)
    def _(block):
        cols = pl.ds(pl.multiple_of(block * 2 * SLOT, 2 * SLOT), 2 * SLOT)
        denc = lax.dot_general(dkv[...], w[cols, :], NT, preferred_element_type=f32)
        hidden = hid[:, cols].astype(f32)
        dh = (inv * gain_ref[:, cols] * denc - hidden * factor).astype(bf16)
        part = jnp.sum(denc * hidden * inv, axis=0, keepdims=True)
        for side in range(2):
            lanes = slice(side * SLOT, (side + 1) * SLOT)
            start = slot_column(block, side)
            to = pl.ds(start, SLOT)
            dh_own[:, to] = dh[:LEN, lanes]
            dh_oth[:, to] = dh[LEN:, lanes]
            gp_ref[:, to] = part[:, lanes]

    @pl.when(flag_ref[0] != 0)
    def _():
        dh_oth[...] = jnp.zeros_like(dh_oth)
        pltpu.sync_copy(dh_enc, dh_own)
        pltpu.sync_copy(gp_enc, gp_ref)


def slot_column(block, side):
    column, offset = jnp.int32(0), jnp.int32(0)
    for index in range(N_SLOT // 2):
        here = block == index
        column = jnp.where(here, SLOTS[2 * index + side][0], column)
        offset = jnp.where(here, SLOTS[2 * index + side][1], offset)
    dp = lax.axis_index("dp")
    column = (dp // 16 + column) % 2
    place = ((dp // 2) % 8 + offset + 8) % 8
    return pl.multiple_of((column * 8 + place) * SLOT, SLOT)


def attend(pieces, flag, q_own, q_oth, g_own, g_oth, enc, hid, inv, gain, dh_enc, gp_enc):
    SMEM = pl.BlockSpec(memory_space=pltpu.SMEM)
    part = jax.ShapeDtypeStruct((LEN, F), bf16)
    rows = jax.ShapeDtypeStruct((LEN, D), bf16)
    return pl.pallas_call(
        main_kernel,
        in_specs=[ANY] * (2 * N_SLOT) + [SMEM] + [ANY] * 10,
        out_specs=[VMEM] * 7,
        out_shape=[part, part, part, part, rows, rows, jax.ShapeDtypeStruct((1, D), f32)],
        scratch_shapes=[
            pltpu.VMEM((D, 2 * F), bf16),
            pltpu.VMEM((2 * LEN, D), bf16),
            pltpu.VMEM((2 * LEN, D), bf16),
            pltpu.VMEM((2 * LEN, 128), f32),
            pltpu.VMEM((1, D), f32),
            pltpu.VMEM((2 * LEN, F), bf16),
            pltpu.VMEM((2 * LEN, F), bf16),
            pltpu.VMEM((2 * LEN, 2 * F), bf16),
            pltpu.VMEM((2 * LEN, 2 * F), bf16),
            pltpu.VMEM((2 * LEN, 128), f32),
            pltpu.SemaphoreType.DMA((2 * N_SLOT,)),
            pltpu.SemaphoreType.DMA((8,)),
        ],
        compiler_params=pltpu.CompilerParams(vmem_limit_bytes=LIMIT),
        cost_estimate=pl.CostEstimate(flops=10_000_000_000, bytes_accessed=20_000_000, transcendentals=600_000),
        name="attend",
    )(*pieces, flag, q_own, q_oth, g_own, g_oth, enc, hid, inv, gain, dh_enc, gp_enc)


def butterfly(x, swaps):
    parts = [x] + [swap(x) for swap in swaps]
    while len(parts) > 1:
        parts = [parts[i] + parts[i + 1] for i in range(0, len(parts), 2)]
    return parts[0]


def sum_everywhere(x):
    x = x + other_core(x)
    x = x + other_column(x)
    x = x + other_high(x)
    x = butterfly(x, [lambda v, i=i: section_swap(v, lambda h, y: (h, y ^ i)) for i in (1, 2, 3)])
    x = butterfly(x, [lambda v, i=i: dp_swap(v, lambda c, z, k: (c, z ^ i, k)) for i in (1, 2, 3)])
    return x + dp_swap(x, lambda c, z, k: (c, z ^ 4, k))


def on_device(section_rows, kv_weight, cotangent, gain, section_map):
    section = lax.axis_index("section")
    core = lax.axis_index("dp") % 2
    high, y = section // 4, section % 4
    order = jnp.arange(8, dtype=jnp.int32)
    root = jnp.sum(jnp.where(section_map == 0, order, 0))
    root_high, root_y = root // 4, root % 4
    is_encoder = root == section
    rows, cot, weight = section_rows[0], cotangent[0], kv_weight[0]

    def heads(x, which):
        return lax.dynamic_slice_in_dim(x, which * F, F, 1)

    def columns(which):
        return jnp.concatenate(
            [heads(weight, which), lax.dynamic_slice_in_dim(weight, 2 * F + which * F, F, 1)], axis=1
        )

    keep = columns(core)
    recv = other_core(columns(1 - core))
    first, second = gather_slots(keep), gather_slots(recv)
    pieces = [piece for pair in zip(first, second) for piece in pair]

    def quarter(step):
        return lax.dynamic_slice_in_dim(rows, ((y + step) % 4) * QUARTER, QUARTER, 0)

    mine = quarter(0)
    for step in (1, 3, 2):
        got = to_y(quarter(step), step)
        mine = jnp.where((y + 4 - step) % 4 == root_y, got, mine)
    crossed = other_high(mine)
    mine = jnp.where(high == root_high, mine, crossed)
    hidden = jnp.concatenate([mine, to_y(mine, 3), to_y(mine, 2), to_y(mine, 1)], axis=0)
    hidden_oth = other_core(hidden)

    q_own, g_own = heads(rows, core), heads(cot, core)
    q_oth, g_oth = other_core(heads(rows, 1 - core)), other_core(heads(cot, 1 - core))

    enc, hid, gain_slots, inv, dh_enc, gp_enc = normalise(hidden, hidden_oth, gain[None], cot)
    ctx_own, ctx_oth, dq_own, dq_oth, dh_own, dh_oth, gp = attend(
        pieces, is_encoder.astype(jnp.int32)[None], q_own, q_oth, g_own, g_oth, enc, hid, inv, gain_slots,
        dh_enc, gp_enc,
    )

    got = other_core(dh_oth)

    def part(step):
        at = slice(step * QUARTER, (step + 1) * QUARTER)
        return dh_own[at].astype(f32) + got[at].astype(f32)

    sums = [to_y(part(step).astype(bf16), step) for step in (1, 2, 3)]
    total = part(0)
    for other in sums:
        total = total + other.astype(f32)
    crossed = other_high(total.astype(bf16))
    dh = (total + crossed.astype(f32)).astype(bf16)
    dh = jnp.concatenate([dh, to_y(dh, 3), to_y(dh, 2), to_y(dh, 1)], axis=0)
    dh = lax.dynamic_slice_in_dim(jnp.concatenate([dh, dh], axis=0), ((4 - y) % 4) * QUARTER, LEN, 0)

    gain_grad = sum_everywhere(gp.reshape(D // 128, 128)).reshape(D)

    ctx_got, dq_got = other_core(ctx_oth), other_core(dq_oth)

    def whole(own, got):
        return jnp.where(core == 0, jnp.concatenate([own, got], 1), jnp.concatenate([got, own], 1))

    own_rows = rows.astype(f32)
    own_inv = lax.rsqrt(jnp.mean(own_rows * own_rows, axis=1, keepdims=True) + eps)
    enc_out = (own_rows * own_inv * gain).astype(bf16)
    section_out = jnp.where(is_encoder, enc_out, whole(ctx_own, ctx_got))[None]
    section_grad = jnp.where(is_encoder, dh, whole(dq_own, dq_got))[None]
    return (section_out, section_grad, gain_grad)


def solution(mesh):
    return jax.shard_map(
        on_device,
        mesh=mesh,
        in_specs=(
            P("section", "dp", None),
            P("section", "dp", None),
            P("section", "dp", None),
            P(),
            P(),
        ),
        out_specs=(P("section", "dp", None), P("section", "dp", None), P()),
        check_vma=False,
    )
```

```python
import functools
import math

import jax
import jax.numpy as jnp
from jax import lax
from jax.experimental import pallas as pl
from jax.experimental.pallas import tpu as pltpu
from jax.sharding import PartitionSpec as P

HEAD = 256
LEN = 256
D = 2048
HALF = 4
F = HALF * HEAD
QUARTER = LEN // 4

eps = 1e-06
bf16 = jnp.bfloat16
f32 = jnp.float32

SLOTS = (
    (0, 0), (0, 1), (0, -1), (1, 0), (0, 2), (0, -2), (1, 1), (0, 3),
    (0, -3), (1, 2), (1, 3), (0, 4), (1, -2), (1, 4), (1, -3), (1, -1),
)
N_SLOT = len(SLOTS)
SLOT = D // N_SLOT
EARLY = 10

ANY = pl.BlockSpec(memory_space=pl.ANY)
VMEM = pl.BlockSpec(memory_space=pltpu.VMEM)
SMEM = pl.BlockSpec(memory_space=pltpu.SMEM)
LIMIT = 28 * 1024 * 1024


def dp_swap(x, move):
    pairs = []
    for index in range(32):
        column, place, core = index // 16, (index // 2) % 8, index % 2
        column, place, core = move(column, place, core)
        pairs.append((index, (column % 2) * 16 + (place % 8) * 2 + core % 2))
    return lax.ppermute(x, "dp", pairs)


def section_swap(x, move):
    pairs = []
    for index in range(8):
        high, y = move(index // 4, index % 4)
        pairs.append((index, (high % 2) * 4 + y % 4))
    return lax.ppermute(x, "section", pairs)


def other_core(x):
    return dp_swap(x, lambda c, z, k: (c, z, k + 1))


def other_column(x):
    return dp_swap(x, lambda c, z, k: (c + 1, z, k))


def from_above(x):
    return dp_swap(x, lambda c, z, k: (c, z - 1, k))


def from_below(x):
    return dp_swap(x, lambda c, z, k: (c, z + 1, k))


def other_high(x):
    return section_swap(x, lambda h, y: (h + 1, y))


def to_y(x, step):
    return section_swap(x, lambda h, y: (h, y + step))


def join_kernel(*refs):
    del refs


def join(*arrays):
    count = len(arrays)
    return pl.pallas_call(
        join_kernel,
        in_specs=[ANY] * count,
        out_specs=[ANY] * count,
        out_shape=[jax.ShapeDtypeStruct(x.shape, x.dtype) for x in arrays],
        input_output_aliases={i: i for i in range(count)},
        compiler_params=pltpu.CompilerParams(vmem_limit_bytes=1024 * 1024),
        cost_estimate=pl.CostEstimate(flops=0, bytes_accessed=1024, transcendentals=0),
        name="join",
    )(*arrays)


def slot_column(column, offset):
    dp = lax.axis_index("dp")
    column = (dp // 16 + column) % 2
    place = ((dp // 2) % 8 + offset + 8) % 8
    return pl.multiple_of((column * 8 + place) * SLOT, SLOT)


def project_kernel(*refs):
    units = refs[:EARLY]
    (flag_ref, own_ref, oth_ref, gain_ref, cot_ref,
     acc_ref, enc_out, inv_ref, dh_ref, gp_ref, full_ref, enc, cot, cot_sem) = refs[EARLY:]
    for seq, ref in enumerate((own_ref, oth_ref)):
        rows = pl.ds(seq * LEN, LEN)
        hidden = ref[...].astype(f32)
        inv = lax.rsqrt(jnp.mean(hidden * hidden, axis=1, keepdims=True) + eps)
        inv_ref[rows, :] = jnp.broadcast_to(inv, (LEN, 128))
        for slot in range(N_SLOT):
            start = slot_column(*SLOTS[slot])
            part = ref[:, pl.ds(start, SLOT)].astype(f32)
            enc[rows, slot * SLOT:(slot + 1) * SLOT] = (part * inv * gain_ref[:, pl.ds(start, SLOT)]).astype(bf16)
    enc_out[...] = enc[:, EARLY * SLOT:]

    @pl.loop(0, 2 * F // HEAD)
    def _(block):
        cols = pl.ds(pl.multiple_of(block * HEAD, HEAD), HEAD)
        w = jnp.concatenate([unit[:, cols] for unit in units], axis=0)
        acc_ref[:, cols] = jnp.dot(enc[:, : EARLY * SLOT], w, preferred_element_type=f32)

    @pl.when(flag_ref[0] != 0)
    def _():
        fetch = pltpu.make_async_copy(cot_ref, cot, cot_sem)
        fetch.start()
        fetch.wait()
        y = lax.axis_index("section") % 4
        gain = gain_ref[...]
        total = jnp.zeros((1, D), f32)
        for quarter in range(4):
            rows = pl.ds(quarter * QUARTER, QUARTER)
            place = pl.ds(pl.multiple_of(((y + quarter) % 4) * QUARTER, QUARTER), QUARTER)
            g = cot[place, :].astype(f32)
            hidden = own_ref[rows, :].astype(f32)
            inv = inv_ref[rows, :1]
            full_ref[place, :] = (hidden * inv * gain).astype(bf16)
            mean = jnp.mean(hidden * gain * g, axis=1, keepdims=True)
            dh_ref[rows, :] = (inv * gain * g - hidden * (inv * inv * inv * mean)).astype(bf16)
            total = total + jnp.sum(g * hidden * inv, axis=0, keepdims=True)
        gp_ref[...] = total


def project(units, flag, own, oth, gain, cot):
    return pl.pallas_call(
        project_kernel,
        in_specs=[VMEM] * EARLY + [SMEM, VMEM, VMEM, VMEM, ANY],
        out_specs=[VMEM] * 6,
        out_shape=[
            jax.ShapeDtypeStruct((2 * LEN, 2 * F), f32),
            jax.ShapeDtypeStruct((2 * LEN, (N_SLOT - EARLY) * SLOT), bf16),
            jax.ShapeDtypeStruct((2 * LEN, 128), f32),
            jax.ShapeDtypeStruct((LEN, D), bf16),
            jax.ShapeDtypeStruct((1, D), f32),
            jax.ShapeDtypeStruct((LEN, D), bf16),
        ],
        scratch_shapes=[
            pltpu.VMEM((2 * LEN, D), bf16),
            pltpu.VMEM((LEN, D), bf16),
            pltpu.SemaphoreType.DMA,
        ],
        compiler_params=pltpu.CompilerParams(vmem_limit_bytes=LIMIT),
        cost_estimate=pl.CostEstimate(flops=3_000_000_000, bytes_accessed=14_000_000, transcendentals=0),
        name="project",
    )(*units, flag, own, oth, gain, cot)


NT = (((1,), (1,)), ((), ()))
TN = (((0,), (0,)), ((), ()))
SCALE = 1.0 / math.sqrt(HEAD)


def main_kernel(*refs):
    units = refs[:N_SLOT]
    (flag_ref, acc, q_own, q_oth, g_own, g_oth, enc, own_ref, oth_ref, inv_ref, gain_ref, dh_enc, gp_enc,
     own_out, oth_out, dh_own, dh_oth, gp_ref, kv, dkv, mean_ref) = refs[N_SLOT:]
    for head in range(HALF):
        cols = slice(head * HEAD, (head + 1) * HEAD)
        vcols = slice(F + head * HEAD, F + (head + 1) * HEAD)
        for at in (cols, vcols):
            w = jnp.concatenate([unit[:, at] for unit in units[EARLY:]], axis=0)
            kv[:, at] = (acc[:, at] + jnp.dot(enc[...], w, preferred_element_type=f32)).astype(bf16)
        for seq, (q, g, out) in enumerate(((q_own, g_own, own_out), (q_oth, g_oth, oth_out))):
            rows = slice(seq * LEN, (seq + 1) * LEN)
            qb, gb = q[:, cols], g[:, cols]
            kb, vb = kv[rows, cols], kv[rows, vcols]
            scores = lax.dot_general(kb, qb, NT, preferred_element_type=f32) * SCALE
            dprobs = lax.dot_general(vb, gb, NT, preferred_element_type=f32)
            peak = jnp.max(scores, axis=0, keepdims=True)
            e = jnp.exp(scores - peak)
            probs = e * (1.0 / jnp.sum(e, axis=0, keepdims=True))
            rounded = probs.astype(bf16)
            delta = jnp.sum(rounded.astype(f32) * dprobs, axis=0, keepdims=True)
            dscores = (probs * (dprobs - delta)).astype(bf16)
            context = lax.dot_general(rounded, vb, TN, preferred_element_type=f32)
            dq = lax.dot_general(dscores, kb, TN, preferred_element_type=f32) * SCALE
            out[:, cols] = context.astype(bf16)
            out[:, vcols] = dq.astype(bf16)
            dk = (jnp.dot(dscores, qb, preferred_element_type=f32) * SCALE).astype(bf16)
            dv = jnp.dot(rounded, gb, preferred_element_type=f32).astype(bf16)
            dkv[rows, cols] = dk
            dkv[rows, vcols] = dv
            term = dk.astype(f32) * kb.astype(f32) + dv.astype(f32) * vb.astype(f32)
            term = term[:, :128] + term[:, 128:]
            if head:
                term = term + mean_ref[rows, :]
            mean_ref[rows, :] = term

    top, low = slice(0, LEN), slice(LEN, 2 * LEN)
    inv = inv_ref[:, :1]
    factor = inv * inv * (jnp.sum(mean_ref[...], axis=1, keepdims=True) * (1.0 / D))

    @pl.when(flag_ref[0] == 0)
    def _():
        for block in range(N_SLOT // 2):
            w = jnp.concatenate([units[2 * block][...], units[2 * block + 1][...]], axis=0)
            denc = lax.dot_general(dkv[...], w, NT, preferred_element_type=f32)
            for side in range(2):
                cols = pl.ds(slot_column(*SLOTS[2 * block + side]), SLOT)
                total = jnp.zeros((1, SLOT), f32)
                for rows, hid, out in ((top, own_ref, dh_own), (low, oth_ref, dh_oth)):
                    hidden = hid[:, cols].astype(f32)
                    scaled = inv[rows] * denc[rows, side * SLOT:(side + 1) * SLOT]
                    out[:LEN, cols] = (gain_ref[:, cols] * scaled - hidden * factor[rows]).astype(bf16)
                    total = total + jnp.sum(scaled * hidden, axis=0, keepdims=True)
                gp_ref[:, cols] = total

    @pl.when(flag_ref[0] != 0)
    def _():
        dh_oth[...] = jnp.zeros_like(dh_oth)
        dh_own[...] = dh_enc[...]
        gp_ref[...] = gp_enc[...]

    dh_oth[LEN:, :] = two_rows(gp_ref[...])


def two_rows(x):
    high = x.astype(bf16).astype(f32)
    index = lax.broadcasted_iota(jnp.int32, (16, x.shape[1]), 0)
    rows = jnp.where(index == 0, high, jnp.where(index == 1, x - high, 0.0))
    return rows.astype(bf16)


def one_row(rows):
    return rows[0:1, :].astype(f32) + rows[1:2, :].astype(f32)


def attend(units, flag, acc, q_own, q_oth, g_own, g_oth, enc, own, oth, inv, gain, dh_enc, gp_enc):
    rows = jax.ShapeDtypeStruct((LEN, D), bf16)
    return pl.pallas_call(
        main_kernel,
        in_specs=[VMEM] * N_SLOT + [SMEM] + [VMEM] * 12,
        out_specs=[VMEM] * 5,
        out_shape=[
            rows, rows, rows, jax.ShapeDtypeStruct((LEN + 16, D), bf16), jax.ShapeDtypeStruct((1, D), f32)
        ],
        scratch_shapes=[
            pltpu.VMEM((2 * LEN, 2 * F), bf16),
            pltpu.VMEM((2 * LEN, 2 * F), bf16),
            pltpu.VMEM((2 * LEN, 128), f32),
        ],
        compiler_params=pltpu.CompilerParams(vmem_limit_bytes=LIMIT),
        cost_estimate=pl.CostEstimate(flops=7_000_000_000, bytes_accessed=20_000_000, transcendentals=600_000),
        name="attend",
    )(*units, flag, acc, q_own, q_oth, g_own, g_oth, enc, own, oth, inv, gain, dh_enc, gp_enc)


def small_call(kernel, out_shape, args, name):
    return pl.pallas_call(
        kernel,
        in_specs=[VMEM] * len(args),
        out_specs=jax.tree.map(lambda _: VMEM, out_shape),
        out_shape=out_shape,
        compiler_params=pltpu.CompilerParams(vmem_limit_bytes=12 * 1024 * 1024),
        cost_estimate=pl.CostEstimate(flops=1_000_000, bytes_accessed=3_000_000, transcendentals=0),
        name=name,
    )(*args)


SENT = jax.ShapeDtypeStruct((QUARTER + 16, D), bf16)
KEPT = jax.ShapeDtypeStruct((QUARTER + 8, D), f32)


def split_kernel(own_ref, gp_ref, got_ref, kept_ref, *sent):
    own_rows = two_rows(gp_ref[...])
    gain = one_row(own_rows) + one_row(got_ref[LEN:, :])
    rows = two_rows(gain)
    for step in range(4):
        at = slice(step * QUARTER, (step + 1) * QUARTER)
        part = own_ref[at, :].astype(f32) + got_ref[at, :].astype(f32)
        if step == 0:
            kept_ref[:QUARTER, :] = part
            kept_ref[QUARTER:, :] = jnp.broadcast_to(one_row(rows), (8, D))
        else:
            sent[step - 1][:QUARTER, :] = part.astype(bf16)
            sent[step - 1][QUARTER:, :] = rows


def sum_kernel(kept_ref, a_ref, b_ref, c_ref, sum_ref, sent_ref):
    total = kept_ref[:QUARTER, :] + (
        a_ref[:QUARTER, :].astype(f32) + b_ref[:QUARTER, :].astype(f32) + c_ref[:QUARTER, :].astype(f32)
    )
    gain = (kept_ref[QUARTER:QUARTER + 1, :] + one_row(b_ref[QUARTER:, :])) + (
        one_row(a_ref[QUARTER:, :]) + one_row(c_ref[QUARTER:, :])
    )
    rows = two_rows(gain)
    sum_ref[:QUARTER, :] = total
    sum_ref[QUARTER:, :] = jnp.broadcast_to(one_row(rows), (8, D))
    sent_ref[:QUARTER, :] = total.astype(bf16)
    sent_ref[QUARTER:, :] = rows


def last_kernel(sum_ref, got_ref, dh_ref, gain_ref):
    dh_ref[...] = (sum_ref[:QUARTER, :] + got_ref[:QUARTER, :].astype(f32)).astype(bf16)
    gain_ref[...] = sum_ref[QUARTER:QUARTER + 1, :] + one_row(got_ref[QUARTER:, :])


def out_kernel(offset, flag_ref, own_ref, oth_ref, *refs):
    *parts, out_ref, sems = refs
    core = lax.axis_index("dp") % 2
    y = lax.axis_index("section") % 4
    rows = LEN // len(parts)

    @pl.when(flag_ref[0] == 0)
    def _():
        copies = [
            pltpu.make_async_copy(
                ref.at[:, pl.ds(offset, F)],
                out_ref.at[:, pl.ds(pl.multiple_of(place * F, F), F)],
                sems.at[index],
            )
            for index, (ref, place) in enumerate(((own_ref, core), (oth_ref, 1 - core)))
        ]
        for copy in copies:
            copy.start()
        for copy in copies:
            copy.wait()

    @pl.when(flag_ref[0] != 0)
    def _():
        copies = []
        for index, part in enumerate(parts):
            start = 0 if len(parts) == 1 else pl.multiple_of(((y + index) % 4) * rows, rows)
            copies.append(pltpu.make_async_copy(part, out_ref.at[pl.ds(start, rows), :], sems.at[index]))
        for copy in copies:
            copy.start()
        for copy in copies:
            copy.wait()


def put_out(offset, flag, own, oth, parts, name):
    return pl.pallas_call(
        functools.partial(out_kernel, offset),
        in_specs=[SMEM] + [ANY] * (2 + len(parts)),
        out_specs=ANY,
        out_shape=jax.ShapeDtypeStruct((LEN, D), bf16),
        scratch_shapes=[pltpu.SemaphoreType.DMA((4,))],
        compiler_params=pltpu.CompilerParams(vmem_limit_bytes=1024 * 1024),
        cost_estimate=pl.CostEstimate(flops=0, bytes_accessed=2_000_000, transcendentals=0),
        name=name,
    )(flag, own, oth, *parts)


def butterfly(x, swaps):
    parts = [x] + [swap(x) for swap in swaps]
    while len(parts) > 1:
        parts = [parts[i] + parts[i + 1] for i in range(0, len(parts), 2)]
    return parts[0]


def sum_over_chips(x):
    x = butterfly(x, [lambda v, i=i: dp_swap(v, lambda c, z, k: (c, z ^ i, k)) for i in (1, 2, 3)])
    x = butterfly(x, [
        other_column,
        lambda v: dp_swap(v, lambda c, z, k: (c, z ^ 4, k)),
        lambda v: dp_swap(v, lambda c, z, k: (c + 1, z ^ 4, k)),
    ])
    return x


def on_device(section_rows, kv_weight, cotangent, gain, section_map):
    section = lax.axis_index("section")
    core = lax.axis_index("dp") % 2
    high, y = section // 4, section % 4
    order = jnp.arange(8, dtype=jnp.int32)
    root = jnp.sum(jnp.where(section_map == 0, order, 0))
    root_high, root_y = root // 4, root % 4
    flag = (root == section).astype(jnp.int32)[None]
    rows, cot, weight = section_rows[0], cotangent[0], kv_weight[0]
    gain = gain[None]

    def heads(x, which):
        return lax.dynamic_slice_in_dim(x, which * F, F, 1)

    def columns(which):
        return jnp.concatenate([heads(weight, which), heads(weight, 2 + which)], axis=1)

    def quarter(step):
        return lax.dynamic_slice_in_dim(rows, ((y + step) % 4) * QUARTER, QUARTER, 0)

    recv = other_core(columns(1 - core))
    quarters = [to_y(quarter(step), step) for step in (1, 3, 2)]
    recv, *quarters = join(recv, *quarters)
    mine = quarter(0)
    for step, got in zip((1, 3, 2), quarters):
        mine = jnp.where((y + 4 - step) % 4 == root_y, got, mine)

    keep = columns(core)
    a, b = {0: jnp.concatenate([jnp.where(core == 0, keep, recv), jnp.where(core == 0, recv, keep)], axis=0)}, {}
    crossed = other_high(mine)
    a[1], a[-1], b[0], crossed = join(from_above(a[0]), from_below(a[0]), other_column(a[0]), crossed)
    mine = jnp.where(high == root_high, mine, crossed)
    others = [to_y(mine, step) for step in (3, 2, 1)]
    a[2], a[-2], b[1], *others = join(from_above(a[1]), from_below(a[-1]), other_column(a[1]), *others)
    own = jnp.concatenate([mine] + others, axis=0)
    oth = other_core(own)
    q_oth, g_oth = other_core(heads(rows, 1 - core)), other_core(heads(cot, 1 - core))
    a[3], a[-3], b[2], oth, q_oth, g_oth = join(
        from_above(a[2]), from_below(a[-2]), other_column(a[2]), oth, q_oth, g_oth
    )
    b[3], a[4], b[-2] = join(from_above(b[2]), from_below(a[-3]), other_column(a[-2]))
    b[4], b[-3], b[-1] = from_above(b[3]), from_below(b[-2]), other_column(a[-1])
    units = [(a, b)[column][offset] for column, offset in SLOTS]

    acc, enc, inv, dh_enc, gp_enc, enc_out = project(units[:EARLY], flag, own, oth, gain, cot)
    own_out, oth_out, dh_own, dh_oth, gp = attend(
        units, flag, acc, heads(rows, core), q_oth, heads(cot, core), g_oth, enc, own, oth, inv, gain,
        dh_enc, gp_enc,
    )

    kept, *parts = small_call(split_kernel, [KEPT, SENT, SENT, SENT], (dh_own, gp, other_core(dh_oth)), "split")
    got_out = other_core(oth_out)
    *parts, got_out = join(*[to_y(part, step) for step, part in zip((1, 2, 3), parts)], got_out)
    kept, sent = small_call(sum_kernel, [KEPT, SENT], (kept, *parts), "sum")
    dh, gain_part = small_call(
        last_kernel,
        [jax.ShapeDtypeStruct((QUARTER, D), bf16), jax.ShapeDtypeStruct((1, D), f32)],
        (kept, other_high(sent)),
        "last",
    )
    gain_grad = sum_over_chips(gain_part).reshape(D)
    dhs = [dh] + [to_y(dh, step) for step in (3, 2, 1)]
    section_out = put_out(0, flag, own_out, got_out, [enc_out], "rows")
    section_grad = put_out(F, flag, own_out, got_out, dhs, "grads")
    return (section_out[None], section_grad[None], gain_grad)


def solution(mesh):
    return jax.shard_map(
        on_device,
        mesh=mesh,
        in_specs=(
            P("section", "dp", None),
            P("section", "dp", None),
            P("section", "dp", None),
            P(),
            P(),
        ),
        out_specs=(P("section", "dp", None), P("section", "dp", None), P()),
        check_vma=False,
    )
```

```python
import functools
import math

import jax
import jax.numpy as jnp
from jax import lax
from jax.experimental import pallas as pl
from jax.experimental.pallas import tpu as pltpu
from jax.sharding import PartitionSpec as P

HEAD = 256
LEN = 256
D = 2048
HALF = 4
F = HALF * HEAD
QUARTER = LEN // 4

eps = 1e-06
bf16 = jnp.bfloat16
f32 = jnp.float32

SLOTS = (
    (0, 0), (0, 1), (0, -1), (1, 0), (0, 2), (0, -2), (1, 1), (0, 3),
    (0, -3), (1, 2), (1, 3), (0, 4), (1, -2), (1, 4), (1, -3), (1, -1),
)
N_SLOT = len(SLOTS)
SLOT = D // N_SLOT
EARLY = 10

ANY = pl.BlockSpec(memory_space=pl.ANY)
VMEM = pl.BlockSpec(memory_space=pltpu.VMEM)
SMEM = pl.BlockSpec(memory_space=pltpu.SMEM)
MIB = 1024 * 1024


def dp_swap(x, move):
    pairs = []
    for index in range(32):
        column, place, core = index // 16, (index // 2) % 8, index % 2
        column, place, core = move(column, place, core)
        pairs.append((index, (column % 2) * 16 + (place % 8) * 2 + core % 2))
    return lax.ppermute(x, "dp", pairs)


def section_swap(x, move):
    pairs = []
    for index in range(8):
        high, y = move(index // 4, index % 4)
        pairs.append((index, (high % 2) * 4 + y % 4))
    return lax.ppermute(x, "section", pairs)


def other_core(x):
    return dp_swap(x, lambda c, z, k: (c, z, k + 1))


def other_column(x):
    return dp_swap(x, lambda c, z, k: (c + 1, z, k))


def from_above(x):
    return dp_swap(x, lambda c, z, k: (c, z - 1, k))


def from_below(x):
    return dp_swap(x, lambda c, z, k: (c, z + 1, k))


def other_high(x):
    return section_swap(x, lambda h, y: (h + 1, y))


def to_y(x, step):
    return section_swap(x, lambda h, y: (h, y + step))


def join_kernel(*refs):
    del refs


class Order:
    def __init__(self):
        self.token = jnp.zeros((8, 128), f32)

    def take(self, *arrays):
        arrays = arrays + (self.token,)
        count = len(arrays)
        *arrays, self.token = pl.pallas_call(
            join_kernel,
            in_specs=[ANY] * count,
            out_specs=[ANY] * count,
            out_shape=[jax.ShapeDtypeStruct(x.shape, x.dtype) for x in arrays],
            input_output_aliases={i: i for i in range(count)},
            compiler_params=pltpu.CompilerParams(vmem_limit_bytes=MIB),
            cost_estimate=pl.CostEstimate(flops=0, bytes_accessed=1024, transcendentals=0),
            name="join",
        )(*arrays)
        return arrays[0] if count == 2 else arrays


def slot_column(column, offset):
    dp = lax.axis_index("dp")
    column = (dp // 16 + column) % 2
    place = ((dp // 2) % 8 + offset + 8) % 8
    return pl.multiple_of((column * 8 + place) * SLOT, SLOT)


def project_kernel(*refs):
    units = refs[:EARLY]
    (flag_ref, own_ref, oth_ref, gain_ref, cot_ref,
     acc_ref, enc_out, inv_ref, dh_ref, gp_ref, full_ref, enc, cot, cot_sem) = refs[EARLY:]
    for seq, ref in enumerate((own_ref, oth_ref)):

        @pl.loop(0, LEN // QUARTER)
        def _(block):
            at = pl.ds(pl.multiple_of(block * QUARTER, QUARTER), QUARTER)
            rows = pl.ds(pl.multiple_of(seq * LEN + block * QUARTER, QUARTER), QUARTER)
            hidden = ref[at, :].astype(f32)
            inv = lax.rsqrt(jnp.mean(hidden * hidden, axis=1, keepdims=True) + eps)
            inv_ref[rows, :] = jnp.broadcast_to(inv, (QUARTER, 128))
            for slot in range(N_SLOT):
                cols = pl.ds(slot_column(*SLOTS[slot]), SLOT)
                part = ref[at, cols].astype(f32)
                enc[rows, slot * SLOT:(slot + 1) * SLOT] = (part * inv * gain_ref[:, cols]).astype(bf16)

    enc_out[...] = enc[:, EARLY * SLOT:]

    @pl.loop(0, 2 * F // HEAD)
    def _(block):
        cols = pl.ds(pl.multiple_of(block * HEAD, HEAD), HEAD)
        w = jnp.concatenate([unit[:, cols] for unit in units], axis=0)
        acc_ref[:, cols] = jnp.dot(enc[:, : EARLY * SLOT], w, preferred_element_type=f32)

    @pl.when(flag_ref[0] != 0)
    def _():
        fetch = pltpu.make_async_copy(cot_ref, cot, cot_sem)
        fetch.start()
        fetch.wait()
        y = lax.axis_index("section") % 4
        gain = gain_ref[...]
        total = jnp.zeros((1, D), f32)
        for quarter in range(4):
            rows = pl.ds(quarter * QUARTER, QUARTER)
            place = pl.ds(pl.multiple_of(((y + quarter) % 4) * QUARTER, QUARTER), QUARTER)
            g = cot[place, :].astype(f32)
            hidden = own_ref[rows, :].astype(f32)
            inv = inv_ref[rows, :1]
            full_ref[place, :] = (hidden * inv * gain).astype(bf16)
            mean = jnp.mean(hidden * gain * g, axis=1, keepdims=True)
            dh_ref[rows, :] = (inv * gain * g - hidden * (inv * inv * inv * mean)).astype(bf16)
            total = total + jnp.sum(g * hidden * inv, axis=0, keepdims=True)
        gp_ref[...] = total


def project(units, flag, own, oth, gain, cot):
    return pl.pallas_call(
        project_kernel,
        in_specs=[VMEM] * EARLY + [SMEM, VMEM, VMEM, VMEM, ANY],
        out_specs=[VMEM] * 6,
        out_shape=[
            jax.ShapeDtypeStruct((2 * LEN, 2 * F), f32),
            jax.ShapeDtypeStruct((2 * LEN, (N_SLOT - EARLY) * SLOT), bf16),
            jax.ShapeDtypeStruct((2 * LEN, 128), f32),
            jax.ShapeDtypeStruct((LEN, D), bf16),
            jax.ShapeDtypeStruct((1, D), f32),
            jax.ShapeDtypeStruct((LEN, D), bf16),
        ],
        scratch_shapes=[
            pltpu.VMEM((2 * LEN, D), bf16),
            pltpu.VMEM((LEN, D), bf16),
            pltpu.SemaphoreType.DMA,
        ],
        compiler_params=pltpu.CompilerParams(vmem_limit_bytes=16 * MIB),
        cost_estimate=pl.CostEstimate(flops=3_000_000_000, bytes_accessed=14_000_000, transcendentals=0),
        name="project",
    )(*units, flag, own, oth, gain, cot)


NT = (((1,), (1,)), ((), ()))
TN = (((0,), (0,)), ((), ()))
SCALE = 1.0 / math.sqrt(HEAD)


def main_kernel(*refs):
    units = refs[:N_SLOT]
    (flag_ref, acc, rows_ref, cot_ref, qg_oth, enc, own_ref, oth_ref, inv_ref, gain_ref, dh_enc, gp_enc,
     own_out, oth_out, dh_own, dh_oth, gp_ref, kv, dkv, mean_ref) = refs[N_SLOT:]
    for head in range(HALF):
        cols = slice(head * HEAD, (head + 1) * HEAD)
        vcols = slice(F + head * HEAD, F + (head + 1) * HEAD)
        for at in (cols, vcols):
            w = jnp.concatenate([unit[:, at] for unit in units[EARLY:]], axis=0)
            kv[:, at] = (acc[:, at] + jnp.dot(enc[...], w, preferred_element_type=f32)).astype(bf16)
        mine = pl.ds(pl.multiple_of(lax.axis_index("dp") % 2 * F + head * HEAD, HEAD), HEAD)
        for seq, (q, qcols, g, gcols, out) in enumerate((
            (rows_ref, mine, cot_ref, mine, own_out), (qg_oth, cols, qg_oth, vcols, oth_out)
        )):
            rows = slice(seq * LEN, (seq + 1) * LEN)
            qb, gb = q[:, qcols], g[:, gcols]
            kb, vb = kv[rows, cols], kv[rows, vcols]
            scores = lax.dot_general(kb, qb, NT, preferred_element_type=f32) * SCALE
            dprobs = lax.dot_general(vb, gb, NT, preferred_element_type=f32)
            peak = jnp.max(scores, axis=0, keepdims=True)
            e = jnp.exp(scores - peak)
            probs = e * (1.0 / jnp.sum(e, axis=0, keepdims=True))
            rounded = probs.astype(bf16)
            delta = jnp.sum(rounded.astype(f32) * dprobs, axis=0, keepdims=True)
            dscores = (probs * (dprobs - delta)).astype(bf16)
            context = lax.dot_general(rounded, vb, TN, preferred_element_type=f32)
            dq = lax.dot_general(dscores, kb, TN, preferred_element_type=f32) * SCALE
            out[:, cols] = context.astype(bf16)
            out[:, vcols] = dq.astype(bf16)
            dk = (jnp.dot(dscores, qb, preferred_element_type=f32) * SCALE).astype(bf16)
            dv = jnp.dot(rounded, gb, preferred_element_type=f32).astype(bf16)
            dkv[rows, cols] = dk
            dkv[rows, vcols] = dv
            term = dk.astype(f32) * kb.astype(f32) + dv.astype(f32) * vb.astype(f32)
            term = term[:, :128] + term[:, 128:]
            if head:
                term = term + mean_ref[rows, :]
            mean_ref[rows, :] = term

    top, low = slice(0, LEN), slice(LEN, 2 * LEN)
    inv = inv_ref[:, :1]
    factor = inv * inv * (jnp.sum(mean_ref[...], axis=1, keepdims=True) * (1.0 / D))

    @pl.when(flag_ref[0] == 0)
    def _():
        for block in range(N_SLOT // 2):
            w = jnp.concatenate([units[2 * block][...], units[2 * block + 1][...]], axis=0)
            denc = lax.dot_general(dkv[...], w, NT, preferred_element_type=f32)
            for side in range(2):
                cols = pl.ds(slot_column(*SLOTS[2 * block + side]), SLOT)
                total = jnp.zeros((1, SLOT), f32)
                for rows, hid, out in ((top, own_ref, dh_own), (low, oth_ref, dh_oth)):
                    hidden = hid[:, cols].astype(f32)
                    scaled = inv[rows] * denc[rows, side * SLOT:(side + 1) * SLOT]
                    out[:LEN, cols] = (gain_ref[:, cols] * scaled - hidden * factor[rows]).astype(bf16)
                    total = total + jnp.sum(scaled * hidden, axis=0, keepdims=True)
                gp_ref[:, cols] = total

    @pl.when(flag_ref[0] != 0)
    def _():
        dh_oth[...] = jnp.zeros_like(dh_oth)
        dh_own[...] = dh_enc[...]
        gp_ref[...] = gp_enc[...]

    dh_oth[LEN:, :] = two_rows(gp_ref[...])


def two_rows(x):
    high = x.astype(bf16).astype(f32)
    index = lax.broadcasted_iota(jnp.int32, (16, x.shape[1]), 0)
    rows = jnp.where(index == 0, high, jnp.where(index == 1, x - high, 0.0))
    return rows.astype(bf16)


def one_row(rows):
    return rows[0:1, :].astype(f32) + rows[1:2, :].astype(f32)


def attend(units, flag, acc, rows, cot, qg_oth, enc, own, oth, inv, gain, dh_enc, gp_enc):
    whole = jax.ShapeDtypeStruct((LEN, D), bf16)
    return pl.pallas_call(
        main_kernel,
        in_specs=[VMEM] * N_SLOT + [SMEM] + [VMEM] * 11,
        out_specs=[VMEM] * 5,
        out_shape=[
            whole, whole, whole, jax.ShapeDtypeStruct((LEN + 16, D), bf16), jax.ShapeDtypeStruct((1, D), f32)
        ],
        scratch_shapes=[
            pltpu.VMEM((2 * LEN, 2 * F), bf16),
            pltpu.VMEM((2 * LEN, 2 * F), bf16),
            pltpu.VMEM((2 * LEN, 128), f32),
        ],
        compiler_params=pltpu.CompilerParams(vmem_limit_bytes=16 * MIB),
        cost_estimate=pl.CostEstimate(flops=7_000_000_000, bytes_accessed=20_000_000, transcendentals=600_000),
        name="attend",
    )(*units, flag, acc, rows, cot, qg_oth, enc, own, oth, inv, gain, dh_enc, gp_enc)


def small_call(kernel, out_shape, args, name):
    return pl.pallas_call(
        kernel,
        in_specs=[VMEM] * len(args),
        out_specs=jax.tree.map(lambda _: VMEM, out_shape),
        out_shape=out_shape,
        compiler_params=pltpu.CompilerParams(vmem_limit_bytes=12 * MIB),
        cost_estimate=pl.CostEstimate(flops=1_000_000, bytes_accessed=3_000_000, transcendentals=0),
        name=name,
    )(*args)


ROWS = jax.ShapeDtypeStruct((QUARTER, D), bf16)
ROWS32 = jax.ShapeDtypeStruct((QUARTER, D), f32)
WITH_GAIN = jax.ShapeDtypeStruct((QUARTER + 16, D), bf16)
LINE = jax.ShapeDtypeStruct((1, D), f32)


def split_kernel(own_ref, gp_ref, got_ref, kept_ref, gain_ref, *sent):
    gain_ref[...] = one_row(two_rows(gp_ref[...])) + one_row(got_ref[LEN:, :])
    for step in range(4):
        at = slice(step * QUARTER, (step + 1) * QUARTER)
        part = own_ref[at, :].astype(f32) + got_ref[at, :].astype(f32)
        if step == 0:
            kept_ref[...] = part
        else:
            sent[step - 1][...] = part.astype(bf16)


def sum_kernel(kept_ref, a_ref, b_ref, c_ref, gain_ref, sum_ref, sent_ref, gain_out):
    gain_out[...] = gain_ref[...]
    total = kept_ref[...] + (a_ref[...].astype(f32) + b_ref[...].astype(f32) + c_ref[...].astype(f32))
    sum_ref[...] = total
    sent_ref[...] = total.astype(bf16)


def last_kernel(sum_ref, got_ref, gain_ref, dh_ref):
    dh_ref[:QUARTER, :] = (sum_ref[...] + got_ref[...].astype(f32)).astype(bf16)
    dh_ref[QUARTER:, :] = two_rows(gain_ref[...])


def gain_kernel(a_ref, b_ref, c_ref, d_ref, out_ref):
    a, b, c, d = (one_row(ref[QUARTER:, :]) for ref in (a_ref, b_ref, c_ref, d_ref))
    out_ref[...] = (a + c) + (b + d)


def out_kernel(offset, flag_ref, own_ref, oth_ref, *refs):
    *parts, out_ref, sems = refs
    core = lax.axis_index("dp") % 2
    y = lax.axis_index("section") % 4
    rows = LEN // len(parts)

    @pl.when(flag_ref[0] == 0)
    def _():
        copies = [
            pltpu.make_async_copy(
                ref.at[:, pl.ds(offset, F)],
                out_ref.at[:, pl.ds(pl.multiple_of(place * F, F), F)],
                sems.at[index],
            )
            for index, (ref, place) in enumerate(((own_ref, core), (oth_ref, 1 - core)))
        ]
        for copy in copies:
            copy.start()
        for copy in copies:
            copy.wait()

    @pl.when(flag_ref[0] != 0)
    def _():
        copies = []
        for index, part in enumerate(parts):
            start = 0 if len(parts) == 1 else pl.multiple_of(((y + index) % 4) * rows, rows)
            copies.append(
                pltpu.make_async_copy(part.at[pl.ds(0, rows), :], out_ref.at[pl.ds(start, rows), :], sems.at[index])
            )
        for copy in copies:
            copy.start()
        for copy in copies:
            copy.wait()


def put_out(offset, flag, own, oth, parts, name, cost):
    return pl.pallas_call(
        functools.partial(out_kernel, offset),
        in_specs=[SMEM] + [ANY] * (2 + len(parts)),
        out_specs=ANY,
        out_shape=jax.ShapeDtypeStruct((LEN, D), bf16),
        scratch_shapes=[pltpu.SemaphoreType.DMA((4,))],
        compiler_params=pltpu.CompilerParams(vmem_limit_bytes=MIB),
        cost_estimate=pl.CostEstimate(flops=cost, bytes_accessed=2_000_000, transcendentals=0),
        name=name,
    )(flag, own, oth, *parts)


def butterfly(x, swaps):
    parts = [x] + [swap(x) for swap in swaps]
    while len(parts) > 1:
        parts = [parts[i] + parts[i + 1] for i in range(0, len(parts), 2)]
    return parts[0]


def on_device(section_rows, kv_weight, cotangent, gain, section_map):
    section = lax.axis_index("section")
    core = lax.axis_index("dp") % 2
    high, y = section // 4, section % 4
    order = jnp.arange(8, dtype=jnp.int32)
    root = jnp.sum(jnp.where(section_map == 0, order, 0))
    root_high, root_y = root // 4, root % 4
    flag = (root == section).astype(jnp.int32)[None]
    rows, cot, weight = section_rows[0], cotangent[0], kv_weight[0]
    gain = gain[None]

    def heads(x, which):
        return lax.dynamic_slice_in_dim(x, which * F, F, 1)

    def columns(which):
        return jnp.concatenate([heads(weight, which), heads(weight, 2 + which)], axis=1)

    def quarter(step):
        return lax.dynamic_slice_in_dim(rows, ((y + step) % 4) * QUARTER, QUARTER, 0)

    order = Order()
    quarters = [to_y(quarter(step), step) for step in (2, 1, 3)]
    recv = other_core(columns(1 - core))
    keep = columns(core)
    a, b = {0: jnp.concatenate([jnp.where(core == 0, keep, recv), jnp.where(core == 0, recv, keep)], axis=0)}, {}
    qg_oth = other_core(jnp.concatenate([heads(rows, 1 - core), heads(cot, 1 - core)], axis=1))
    up, down, across = from_above(a[0]), from_below(a[0]), other_column(a[0])

    a[1] = order.take(up)
    up, across_1 = from_above(a[1]), other_column(a[1])
    a[-1] = order.take(down)
    down = from_below(a[-1])
    b[0] = order.take(across)
    quarters = order.take(*quarters)
    mine = quarter(0)
    for step, got in zip((2, 1, 3), quarters):
        mine = jnp.where((y + 4 - step) % 4 == root_y, got, mine)
    crossed = other_high(mine)

    a[2] = order.take(up)
    up, across_2 = from_above(a[2]), other_column(a[2])
    a[-2] = order.take(down)
    down, across_3 = from_below(a[-2]), other_column(a[-2])
    b[1] = order.take(across_1)
    crossed = order.take(crossed)
    mine = jnp.where(high == root_high, mine, crossed)
    others = [to_y(mine, step) for step in (2, 3, 1)]

    a[3] = order.take(up)
    a[-3] = order.take(down)
    down = from_below(a[-3])
    b[2] = order.take(across_2)
    up, across_4 = from_above(b[2]), other_column(a[-1])
    others = order.take(*others)
    own = jnp.concatenate([mine, others[1], others[0], others[2]], axis=0)
    oth = other_core(own)

    a[4] = order.take(down)
    b[-2] = order.take(across_3)
    down = from_below(b[-2])
    b[3] = order.take(up)
    up = from_above(b[3])
    oth, qg_oth = order.take(oth, qg_oth)
    b[4], b[-3], b[-1] = up, down, across_4
    units = [(a, b)[column][offset] for column, offset in SLOTS]

    acc, enc, inv, dh_enc, gp_enc, enc_out = project(units[:EARLY], flag, own, oth, gain, cot)
    own_out, oth_out, dh_own, dh_oth, gp = attend(
        units, flag, acc, rows, cot, qg_oth, enc, own, oth, inv, gain, dh_enc, gp_enc
    )

    kept, gain_part, *parts = small_call(
        split_kernel, [ROWS32, LINE, ROWS, ROWS, ROWS], (dh_own, gp, other_core(dh_oth)), "split"
    )
    parts = [to_y(part, step) for step, part in zip((2, 1, 3), (parts[1], parts[0], parts[2]))]
    gain_part, got_out = order.take(gain_part, other_core(oth_out))
    gain_part = butterfly(
        gain_part, [lambda v, i=i: dp_swap(v, lambda c, z, k: (c, z ^ i, k)) for i in (1, 2, 3)]
    )
    *parts, gain_part = order.take(*parts, gain_part)
    kept, sent, gain_part = small_call(sum_kernel, [ROWS32, ROWS, LINE], (kept, *parts, gain_part), "sum")
    crossed = other_high(sent)
    gain_part = butterfly(gain_part, [
        other_column,
        lambda v: dp_swap(v, lambda c, z, k: (c, z ^ 4, k)),
        lambda v: dp_swap(v, lambda c, z, k: (c + 1, z ^ 4, k)),
    ])
    gain_part = gain_part + other_high(gain_part)
    dh = small_call(last_kernel, WITH_GAIN, (kept, crossed, gain_part), "last")
    dhs = [dh] + [to_y(dh, step) for step in (3, 2, 1)]
    gain_grad = small_call(gain_kernel, LINE, dhs, "gain").reshape(D)
    section_out = put_out(0, flag, own_out, got_out, [enc_out], "rows", 0)
    section_grad = put_out(F, flag, own_out, got_out, dhs, "grads", 0)
    return (section_out[None], section_grad[None], gain_grad)


def solution(mesh):
    return jax.shard_map(
        on_device,
        mesh=mesh,
        in_specs=(
            P("section", "dp", None),
            P("section", "dp", None),
            P("section", "dp", None),
            P(),
            P(),
        ),
        out_specs=(P("section", "dp", None), P("section", "dp", None), P()),
        check_vma=False,
    )
```

```python
import functools
import math

import jax
import jax.numpy as jnp
from jax import lax
from jax.experimental import pallas as pl
from jax.experimental.pallas import tpu as pltpu
from jax.sharding import PartitionSpec as P

HEAD = 256
LEN = 256
D = 2048
HALF = 4
F = HALF * HEAD
QUARTER = LEN // 4

eps = 1e-06
bf16 = jnp.bfloat16
f32 = jnp.float32

SLOTS = (
    (0, 0), (0, 1), (0, -1), (1, 0), (0, 2), (0, -2), (1, 1), (0, 3),
    (0, -3), (1, 2), (1, 3), (0, 4), (1, -2), (1, 4), (1, -3), (1, -1),
)
N_SLOT = len(SLOTS)
SLOT = D // N_SLOT
EARLY = 13

ANY = pl.BlockSpec(memory_space=pl.ANY)
VMEM = pl.BlockSpec(memory_space=pltpu.VMEM)
SMEM = pl.BlockSpec(memory_space=pltpu.SMEM)
MIB = 1024 * 1024


def dp_swap(x, move):
    pairs = []
    for index in range(32):
        column, place, core = index // 16, (index // 2) % 8, index % 2
        column, place, core = move(column, place, core)
        pairs.append((index, (column % 2) * 16 + (place % 8) * 2 + core % 2))
    return lax.ppermute(x, "dp", pairs)


def section_swap(x, move):
    pairs = []
    for index in range(8):
        high, y = move(index // 4, index % 4)
        pairs.append((index, (high % 2) * 4 + y % 4))
    return lax.ppermute(x, "section", pairs)


def other_core(x):
    return dp_swap(x, lambda c, z, k: (c, z, k + 1))


def other_column(x):
    return dp_swap(x, lambda c, z, k: (c + 1, z, k))


def from_above(x):
    return dp_swap(x, lambda c, z, k: (c, z - 1, k))


def from_below(x):
    return dp_swap(x, lambda c, z, k: (c, z + 1, k))


def other_high(x):
    return section_swap(x, lambda h, y: (h + 1, y))


def other_y(x, bits):
    return section_swap(x, lambda h, y: (h, y ^ bits))


def join_kernel(*refs):
    del refs


class Order:
    def __init__(self, token):
        self.token = token

    def take(self, *arrays):
        arrays = arrays + (self.token,)
        count = len(arrays)
        *arrays, self.token = pl.pallas_call(
            join_kernel,
            in_specs=[ANY] * count,
            out_specs=[ANY] * count,
            out_shape=[jax.ShapeDtypeStruct(x.shape, x.dtype) for x in arrays],
            input_output_aliases={i: i for i in range(count)},
            compiler_params=pltpu.CompilerParams(vmem_limit_bytes=MIB),
            cost_estimate=pl.CostEstimate(flops=0, bytes_accessed=1024, transcendentals=0),
            name="join",
        )(*arrays)
        return arrays[0] if count == 2 else arrays


def core_index():
    return lax.axis_index("dp") % 2


def y_index():
    return lax.axis_index("section") % 4


def root_of(map_ref):
    root = jnp.int32(0)
    for index in range(8):
        root = jnp.where(map_ref[index] == 0, index, root)
    return root


def is_encoder(map_ref):
    return root_of(map_ref) == lax.axis_index("section")


def row_block(index, size):
    return pl.ds(pl.multiple_of(index * size, size), size)


def copy_all(pairs, sems):
    copies = [pltpu.make_async_copy(source, target, sems.at[i]) for i, (source, target) in enumerate(pairs)]
    for copy in copies:
        copy.start()
    for copy in copies:
        copy.wait()


def columns_kernel(w_ref, keep_ref, give_ref, token_ref, sems):
    core = core_index()
    token_ref[...] = jnp.zeros_like(token_ref)
    copy_all([
        (w_ref.at[:, row_block(side * 2 + which, F)], ref.at[:, pl.ds(side * F, F)])
        for ref, which in ((give_ref, 1 - core), (keep_ref, core))
        for side in range(2)
    ], sems)


def unit_kernel(keep_ref, got_ref, unit_ref, sems):
    core = core_index()
    copy_all([
        (keep_ref, unit_ref.at[row_block(core, SLOT // 2), :]),
        (got_ref, unit_ref.at[row_block(1 - core, SLOT // 2), :]),
    ], sems)


def half_kernel(rows_ref, half_ref, sems):
    copy_all([(rows_ref.at[row_block((y_index() // 2) ^ 1, 2 * QUARTER), :], half_ref)], sems)


def give_kernel(rows_ref, cot_ref, token_ref, give_ref, sems):
    del token_ref
    cols = row_block(1 - core_index(), F)
    copy_all([
        (rows_ref.at[:, cols], give_ref.at[:, pl.ds(0, F)]),
        (cot_ref.at[:, cols], give_ref.at[:, pl.ds(F, F)]),
    ], sems)


def select_kernel(step, map_ref, own_ref, got_ref, *outs):
    y, root = y_index(), root_of(map_ref)
    if step == 0:
        mine = y // 2 == root % 4 // 2
        keep_ref, send_ref = outs
        for ref, quarter in ((keep_ref, y), (send_ref, y ^ 1)):
            ref[...] = jnp.where(mine, own_ref[row_block(quarter, QUARTER), :], got_ref[row_block(quarter % 2, QUARTER), :])
    elif step == 1:
        outs[0][...] = jnp.where(y % 2 == root % 2, own_ref[...], got_ref[...])
    else:
        outs[0][...] = jnp.where(lax.axis_index("section") // 4 == root // 4, own_ref[...], got_ref[...])


def stack_kernel(a_ref, b_ref, out_ref):
    rows = a_ref.shape[0]
    out_ref[:rows, :] = a_ref[...]
    out_ref[rows:, :] = b_ref[...]


def add_kernel(a_ref, b_ref, out_ref):
    out_ref[...] = a_ref[...] + b_ref[...]


def slot_column(column, offset):
    dp = lax.axis_index("dp")
    column = (dp // 16 + column) % 2
    place = ((dp // 2) % 8 + offset + 8) % 8
    return pl.multiple_of((column * 8 + place) * SLOT, SLOT)


def project_kernel(*refs):
    units = refs[:EARLY]
    (map_ref, own_ref, oth_ref, gain_ref, cot_ref,
     acc_ref, enc_out, inv_ref, dh_ref, gp_ref, full_ref, enc, cot, cot_sem) = refs[EARLY:]
    for seq, ref in enumerate((own_ref, oth_ref)):

        @pl.loop(0, LEN // QUARTER)
        def _(block):
            at = pl.ds(pl.multiple_of(block * QUARTER, QUARTER), QUARTER)
            rows = pl.ds(pl.multiple_of(seq * LEN + block * QUARTER, QUARTER), QUARTER)
            hidden = ref[at, :].astype(f32)
            inv = lax.rsqrt(jnp.mean(hidden * hidden, axis=1, keepdims=True) + eps)
            inv_ref[rows, :] = jnp.broadcast_to(inv, (QUARTER, 128))
            for slot in range(N_SLOT):
                cols = pl.ds(slot_column(*SLOTS[slot]), SLOT)
                part = ref[at, cols].astype(f32)
                enc[rows, slot * SLOT:(slot + 1) * SLOT] = (part * inv * gain_ref[:, cols]).astype(bf16)

    enc_out[...] = enc[:, EARLY * SLOT:]

    @pl.loop(0, 2 * F // HEAD)
    def _(block):
        cols = pl.ds(pl.multiple_of(block * HEAD, HEAD), HEAD)
        w = jnp.concatenate([unit[:, cols] for unit in units], axis=0)
        acc_ref[:, cols] = jnp.dot(enc[:, : EARLY * SLOT], w, preferred_element_type=f32)

    @pl.when(is_encoder(map_ref))
    def _():
        fetch = pltpu.make_async_copy(cot_ref, cot, cot_sem)
        fetch.start()
        fetch.wait()
        y = y_index()
        gain = gain_ref[...]
        total = jnp.zeros((1, D), f32)
        for quarter in range(4):
            rows = pl.ds(quarter * QUARTER, QUARTER)
            place = row_block(y ^ quarter, QUARTER)
            g = cot[place, :].astype(f32)
            hidden = own_ref[rows, :].astype(f32)
            inv = inv_ref[rows, :1]
            full_ref[place, :] = (hidden * inv * gain).astype(bf16)
            mean = jnp.mean(hidden * gain * g, axis=1, keepdims=True)
            dh_ref[rows, :] = (inv * gain * g - hidden * (inv * inv * inv * mean)).astype(bf16)
            total = total + jnp.sum(g * hidden * inv, axis=0, keepdims=True)
        gp_ref[...] = total


def project(units, where, own, oth, gain, cot):
    return pl.pallas_call(
        project_kernel,
        in_specs=[VMEM] * EARLY + [SMEM, VMEM, VMEM, VMEM, ANY],
        out_specs=[VMEM] * 6,
        out_shape=[
            jax.ShapeDtypeStruct((2 * LEN, 2 * F), f32),
            jax.ShapeDtypeStruct((2 * LEN, (N_SLOT - EARLY) * SLOT), bf16),
            jax.ShapeDtypeStruct((2 * LEN, 128), f32),
            jax.ShapeDtypeStruct((LEN, D), bf16),
            jax.ShapeDtypeStruct((1, D), f32),
            jax.ShapeDtypeStruct((LEN, D), bf16),
        ],
        scratch_shapes=[
            pltpu.VMEM((2 * LEN, D), bf16),
            pltpu.VMEM((LEN, D), bf16),
            pltpu.SemaphoreType.DMA,
        ],
        compiler_params=pltpu.CompilerParams(vmem_limit_bytes=16 * MIB),
        cost_estimate=pl.CostEstimate(flops=0, bytes_accessed=1024, transcendentals=0),
        name="project",
    )(*units, where, own, oth, gain, cot)


NT = (((1,), (1,)), ((), ()))
TN = (((0,), (0,)), ((), ()))
SCALE = 1.0 / math.sqrt(HEAD)


def main_kernel(*refs):
    units = refs[:N_SLOT]
    (map_ref, acc, rows_ref, cot_ref, qg_oth, enc, own_ref, oth_ref, inv_ref, gain_ref, dh_enc, gp_enc,
     own_out, oth_out, dh_own, dh_oth, gp_ref, kv, dkv, mean_ref) = refs[N_SLOT:]
    for head in range(HALF):
        cols = slice(head * HEAD, (head + 1) * HEAD)
        vcols = slice(F + head * HEAD, F + (head + 1) * HEAD)
        for at in (cols, vcols):
            w = jnp.concatenate([unit[:, at] for unit in units[EARLY:]], axis=0)
            kv[:, at] = (acc[:, at] + jnp.dot(enc[...], w, preferred_element_type=f32)).astype(bf16)
        mine = row_block(core_index() * HALF + head, HEAD)
        for seq, (q, qcols, g, gcols, out) in enumerate((
            (rows_ref, mine, cot_ref, mine, own_out), (qg_oth, cols, qg_oth, vcols, oth_out)
        )):
            rows = slice(seq * LEN, (seq + 1) * LEN)
            qb, gb = q[:, qcols], g[:, gcols]
            kb, vb = kv[rows, cols], kv[rows, vcols]
            scores = lax.dot_general(kb, qb, NT, preferred_element_type=f32) * SCALE
            dprobs = lax.dot_general(vb, gb, NT, preferred_element_type=f32)
            peak = jnp.max(scores, axis=0, keepdims=True)
            e = jnp.exp(scores - peak)
            probs = e * (1.0 / jnp.sum(e, axis=0, keepdims=True))
            rounded = probs.astype(bf16)
            delta = jnp.sum(rounded.astype(f32) * dprobs, axis=0, keepdims=True)
            dscores = (probs * (dprobs - delta)).astype(bf16)
            context = lax.dot_general(rounded, vb, TN, preferred_element_type=f32)
            dq = lax.dot_general(dscores, kb, TN, preferred_element_type=f32) * SCALE
            out[:, cols] = context.astype(bf16)
            out[:, vcols] = dq.astype(bf16)
            dk = (jnp.dot(dscores, qb, preferred_element_type=f32) * SCALE).astype(bf16)
            dv = jnp.dot(rounded, gb, preferred_element_type=f32).astype(bf16)
            dkv[rows, cols] = dk
            dkv[rows, vcols] = dv
            term = dk.astype(f32) * kb.astype(f32) + dv.astype(f32) * vb.astype(f32)
            term = term[:, :128] + term[:, 128:]
            if head:
                term = term + mean_ref[rows, :]
            mean_ref[rows, :] = term

    top, low = slice(0, LEN), slice(LEN, 2 * LEN)
    inv = inv_ref[:, :1]
    factor = inv * inv * (jnp.sum(mean_ref[...], axis=1, keepdims=True) * (1.0 / D))

    @pl.when(jnp.logical_not(is_encoder(map_ref)))
    def _():
        for block in range(N_SLOT // 2):
            w = jnp.concatenate([units[2 * block][...], units[2 * block + 1][...]], axis=0)
            denc = lax.dot_general(dkv[...], w, NT, preferred_element_type=f32)
            for side in range(2):
                cols = pl.ds(slot_column(*SLOTS[2 * block + side]), SLOT)
                total = jnp.zeros((1, SLOT), f32)
                for rows, hid, out in ((top, own_ref, dh_own), (low, oth_ref, dh_oth)):
                    hidden = hid[:, cols].astype(f32)
                    scaled = inv[rows] * denc[rows, side * SLOT:(side + 1) * SLOT]
                    out[:LEN, cols] = (gain_ref[:, cols] * scaled - hidden * factor[rows]).astype(bf16)
                    total = total + jnp.sum(scaled * hidden, axis=0, keepdims=True)
                gp_ref[:, cols] = total

    @pl.when(is_encoder(map_ref))
    def _():
        dh_oth[...] = jnp.zeros_like(dh_oth)
        dh_own[...] = dh_enc[...]
        gp_ref[...] = gp_enc[...]

    dh_oth[LEN:, :] = two_rows(gp_ref[...])


def two_rows(x):
    high = x.astype(bf16).astype(f32)
    index = lax.broadcasted_iota(jnp.int32, (16, x.shape[1]), 0)
    rows = jnp.where(index == 0, high, jnp.where(index == 1, x - high, 0.0))
    return rows.astype(bf16)


def one_row(rows):
    return rows[0:1, :].astype(f32) + rows[1:2, :].astype(f32)


def attend(units, where, acc, rows, cot, qg_oth, enc, own, oth, inv, gain, dh_enc, gp_enc):
    whole = jax.ShapeDtypeStruct((LEN, D), bf16)
    return pl.pallas_call(
        main_kernel,
        in_specs=[VMEM] * N_SLOT + [SMEM] + [VMEM] * 11,
        out_specs=[VMEM] * 5,
        out_shape=[
            whole, whole, whole, jax.ShapeDtypeStruct((LEN + 16, D), bf16), jax.ShapeDtypeStruct((1, D), f32)
        ],
        scratch_shapes=[
            pltpu.VMEM((2 * LEN, 2 * F), bf16),
            pltpu.VMEM((2 * LEN, 2 * F), bf16),
            pltpu.VMEM((2 * LEN, 128), f32),
        ],
        compiler_params=pltpu.CompilerParams(vmem_limit_bytes=16 * MIB),
        cost_estimate=pl.CostEstimate(flops=7_000_000_000, bytes_accessed=20_000_000, transcendentals=600_000),
        name="attend",
    )(*units, where, acc, rows, cot, qg_oth, enc, own, oth, inv, gain, dh_enc, gp_enc)


def small_call(kernel, out_shape, args, name, limit=6, where=None):
    first = () if where is None else (where,)
    return pl.pallas_call(
        kernel,
        in_specs=[SMEM] * len(first) + [VMEM] * len(args),
        out_specs=jax.tree.map(lambda _: VMEM, out_shape),
        out_shape=out_shape,
        compiler_params=pltpu.CompilerParams(vmem_limit_bytes=limit * MIB),
        cost_estimate=pl.CostEstimate(flops=0, bytes_accessed=1024, transcendentals=0),
        name=name,
    )(*first, *args)


def copy_call(kernel, out_shape, args, name, count):
    return pl.pallas_call(
        kernel,
        in_specs=[ANY] * len(args),
        out_specs=jax.tree.map(lambda x: VMEM if x.dtype == f32 else ANY, out_shape),
        out_shape=out_shape,
        scratch_shapes=[pltpu.SemaphoreType.DMA((count,))],
        compiler_params=pltpu.CompilerParams(vmem_limit_bytes=MIB),
        cost_estimate=pl.CostEstimate(flops=0, bytes_accessed=1024, transcendentals=0),
        name=name,
    )(*args)


def bf16_rows(rows):
    return jax.ShapeDtypeStruct((rows, D), bf16)


ROWS32 = jax.ShapeDtypeStruct((QUARTER, D), f32)
LINE = jax.ShapeDtypeStruct((1, D), f32)


def split_kernel(own_ref, gp_ref, got_ref, kept_ref, gain_ref, *sent):
    rows = two_rows(one_row(two_rows(gp_ref[...])) + one_row(got_ref[LEN:, :]))
    gain_ref[...] = one_row(rows)
    for step in range(4):
        at = slice(step * QUARTER, (step + 1) * QUARTER)
        part = own_ref[at, :].astype(f32) + got_ref[at, :].astype(f32)
        if step == 0:
            kept_ref[...] = part
        else:
            sent[step - 1][:QUARTER, :] = part.astype(bf16)
            sent[step - 1][QUARTER:, :] = rows


def sum_kernel(kept_ref, gain_ref, a_ref, b_ref, c_ref, sum_ref, sent_ref, gain_out):
    a, b, c = (ref[:QUARTER, :].astype(f32) for ref in (a_ref, b_ref, c_ref))
    total = kept_ref[...] + (a + b + c)
    sum_ref[...] = total
    sent_ref[...] = total.astype(bf16)
    a, b, c = (one_row(ref[QUARTER:, :]) for ref in (a_ref, b_ref, c_ref))
    gain_out[...] = (gain_ref[...] + a) + (b + c)


def last_kernel(sum_ref, got_ref, gain_ref, dh_ref, gain_out):
    gain_out[...] = gain_ref[...]
    dh_ref[...] = (sum_ref[...] + got_ref[...].astype(f32)).astype(bf16)


def out_kernel(offset, map_ref, own_ref, oth_ref, *refs):
    *parts, out_ref, sems = refs
    core, y = core_index(), y_index()
    rows = LEN // len(parts)

    @pl.when(jnp.logical_not(is_encoder(map_ref)))
    def _():
        copies = [
            pltpu.make_async_copy(
                ref.at[:, pl.ds(offset, F)],
                out_ref.at[:, pl.ds(pl.multiple_of(place * F, F), F)],
                sems.at[index],
            )
            for index, (ref, place) in enumerate(((own_ref, core), (oth_ref, 1 - core)))
        ]
        for copy in copies:
            copy.start()
        for copy in copies:
            copy.wait()

    @pl.when(is_encoder(map_ref))
    def _():
        copies = []
        for index, part in enumerate(parts):
            start = 0 if len(parts) == 1 else pl.multiple_of((y ^ index) * rows, rows)
            copies.append(
                pltpu.make_async_copy(part, out_ref.at[pl.ds(start, rows), :], sems.at[index])
            )
        for copy in copies:
            copy.start()
        for copy in copies:
            copy.wait()


def put_out(offset, where, own, oth, parts, name):
    return pl.pallas_call(
        functools.partial(out_kernel, offset),
        in_specs=[SMEM] + [ANY] * (2 + len(parts)),
        out_specs=ANY,
        out_shape=jax.ShapeDtypeStruct((LEN, D), bf16),
        scratch_shapes=[pltpu.SemaphoreType.DMA((4,))],
        compiler_params=pltpu.CompilerParams(vmem_limit_bytes=MIB),
        cost_estimate=pl.CostEstimate(flops=0, bytes_accessed=2_000_000, transcendentals=0),
        name=name,
    )(where, own, oth, *parts)


def on_device(section_rows, kv_weight, cotangent, gain, section_map):
    rows, cot, weight, gain = section_rows[0], cotangent[0], kv_weight[0], gain[None]
    half, quarter = bf16_rows(2 * QUARTER), bf16_rows(QUARTER)

    def select(step, own, got):
        outs = [quarter, quarter] if step == 0 else quarter
        kernel = functools.partial(select_kernel, step)
        return small_call(kernel, outs, (own, got), "select", limit=3, where=section_map)

    keep, give, token = copy_call(
        columns_kernel,
        [bf16_rows(SLOT // 2), bf16_rows(SLOT // 2), jax.ShapeDtypeStruct((8, 128), f32)],
        (weight,), "columns", 4,
    )
    order = Order(token)
    got = other_core(give)
    hidden = other_y(copy_call(half_kernel, half, (rows,), "half", 1), 2)
    a, b = {0: copy_call(unit_kernel, bf16_rows(SLOT), (keep, got), "unit", 2)}, {}
    up, down, across = from_above(a[0]), from_below(a[0]), other_column(a[0])

    hidden = order.take(hidden)
    mine, send = select(0, rows, hidden)
    hidden = other_y(send, 1)

    a[1] = order.take(up)
    up, across_1 = from_above(a[1]), other_column(a[1])
    a[-1] = order.take(down)
    down = from_below(a[-1])
    b[0] = order.take(across)
    hidden = order.take(hidden)
    mine = select(1, mine, hidden)
    hidden = other_high(mine)

    a[2] = order.take(up)
    up, across_2 = from_above(a[2]), other_column(a[2])
    a[-2] = order.take(down)
    down, across_3 = from_below(a[-2]), other_column(a[-2])
    b[1] = order.take(across_1)
    hidden = order.take(hidden)
    mine = select(2, mine, hidden)
    hidden = other_y(mine, 1)

    a[3] = order.take(up)
    a[-3] = order.take(down)
    down = from_below(a[-3])
    b[2] = order.take(across_2)
    up, across_4 = from_above(b[2]), other_column(a[-1])
    hidden = order.take(hidden)
    mine = small_call(stack_kernel, half, (mine, hidden), "stack", limit=3)
    hidden = other_y(mine, 2)

    a[4] = order.take(down)
    b[-2] = order.take(across_3)
    down = from_below(b[-2])
    b[3] = order.take(up)
    up = from_above(b[3])
    hidden = order.take(hidden)
    own = small_call(stack_kernel, bf16_rows(LEN), (mine, hidden), "stack", limit=3)
    oth = other_core(own)
    qg_oth = other_core(copy_call(give_kernel, bf16_rows(LEN), (rows, cot, order.token), "give", 2))
    b[4], b[-3], b[-1] = up, down, across_4
    units = [(a, b)[column][offset] for column, offset in SLOTS]

    acc, enc, inv, dh_enc, gp_enc, enc_out = project(units[:EARLY], section_map, own, oth, gain, cot)
    own_out, oth_out, dh_own, dh_oth, gp = attend(
        units, section_map, acc, rows, cot, qg_oth, enc, own, oth, inv, gain, dh_enc, gp_enc
    )

    with_gain = bf16_rows(QUARTER + 16)
    kept, gain_part, *parts = small_call(
        split_kernel, [ROWS32, LINE, with_gain, with_gain, with_gain], (dh_own, gp, other_core(dh_oth)), "split"
    )
    *parts, got_out = order.take(*[other_y(part, bits) for bits, part in zip((1, 2, 3), parts)], other_core(oth_out))
    kept, sent, gain_part = small_call(sum_kernel, [ROWS32, quarter, LINE], (kept, gain_part, *parts), "sum")
    crossed = other_high(sent)

    def add_from(part, move):
        return small_call(add_kernel, LINE, (part, move(part)), "add", limit=1)

    for move in (other_high, other_column):
        gain_part = add_from(gain_part, move)
    dh, gain_part = small_call(last_kernel, [quarter, LINE], (kept, crossed, gain_part), "last")
    dhs = [dh] + [other_y(dh, bits) for bits in (1, 2, 3)]
    for bits in (1, 2, 4):
        gain_part = add_from(gain_part, lambda v, bits=bits: dp_swap(v, lambda c, z, k: (c, z ^ bits, k)))
    section_out = put_out(0, section_map, own_out, got_out, [enc_out], "rows")
    section_grad = put_out(F, section_map, own_out, got_out, dhs, "grads")
    return (section_out[None], section_grad[None], gain_part.reshape(D))


def solution(mesh):
    return jax.shard_map(
        on_device,
        mesh=mesh,
        in_specs=(
            P("section", "dp", None),
            P("section", "dp", None),
            P("section", "dp", None),
            P(),
            P(),
        ),
        out_specs=(P("section", "dp", None), P("section", "dp", None), P()),
        check_vma=False,
    )
```

```python
import functools
import math

import jax
import jax.numpy as jnp
from jax import lax
from jax.experimental import pallas as pl
from jax.experimental.pallas import tpu as pltpu
from jax.sharding import PartitionSpec as P

HEAD = 256
LEN = 256
D = 2048
HALF = 4
F = HALF * HEAD
QUARTER = LEN // 4
PIECE = LEN // 2

eps = 1e-06
bf16 = jnp.bfloat16
f32 = jnp.float32

SLOTS = (
    (0, 0), (0, 1), (0, -1), (1, 0), (0, 2), (0, -2), (1, 1), (0, 3),
    (0, -3), (1, -2), (0, 4), (1, 2), (1, -3), (1, 3), (1, -1), (1, 4),
)
N_SLOT = len(SLOTS)
SLOT = D // N_SLOT

ANY = pl.BlockSpec(memory_space=pl.ANY)
VMEM = pl.BlockSpec(memory_space=pltpu.VMEM)
SMEM = pl.BlockSpec(memory_space=pltpu.SMEM)
MIB = 1024 * 1024


def dp_swap(x, move):
    pairs = []
    for index in range(32):
        column, place, core = index // 16, (index // 2) % 8, index % 2
        column, place, core = move(column, place, core)
        pairs.append((index, (column % 2) * 16 + (place % 8) * 2 + core % 2))
    return lax.ppermute(x, "dp", pairs)


def section_swap(x, move):
    pairs = []
    for index in range(8):
        high, y = move(index // 4, index % 4)
        pairs.append((index, (high % 2) * 4 + y % 4))
    return lax.ppermute(x, "section", pairs)


def other_core(x):
    return dp_swap(x, lambda c, z, k: (c, z, k + 1))


def other_column(x):
    return dp_swap(x, lambda c, z, k: (c + 1, z, k))


def from_above(x):
    return dp_swap(x, lambda c, z, k: (c, z - 1, k))


def from_below(x):
    return dp_swap(x, lambda c, z, k: (c, z + 1, k))


def other_high(x):
    return section_swap(x, lambda h, y: (h + 1, y))


def other_y(x, bits):
    return section_swap(x, lambda h, y: (h, y ^ bits))


def join_kernel(*refs):
    del refs


class Order:
    def __init__(self, token):
        self.token = token

    def take(self, *arrays):
        arrays = arrays + (self.token,)
        count = len(arrays)
        *arrays, self.token = pl.pallas_call(
            join_kernel,
            in_specs=[ANY] * count,
            out_specs=[ANY] * count,
            out_shape=[jax.ShapeDtypeStruct(x.shape, x.dtype) for x in arrays],
            input_output_aliases={i: i for i in range(count)},
            compiler_params=pltpu.CompilerParams(vmem_limit_bytes=MIB),
            cost_estimate=pl.CostEstimate(flops=0, bytes_accessed=1024, transcendentals=0),
            name="join",
        )(*arrays)
        return arrays[0] if count == 2 else arrays


def core_index():
    return lax.axis_index("dp") % 2


def y_index():
    return lax.axis_index("section") % 4


def root_of(map_ref):
    root = jnp.int32(0)
    for index in range(8):
        root = jnp.where(map_ref[index] == 0, index, root)
    return root


def is_encoder(map_ref):
    return root_of(map_ref) == lax.axis_index("section")


def row_block(index, size):
    return pl.ds(pl.multiple_of(index * size, size), size)


def copy_all(pairs, sems):
    copies = [pltpu.make_async_copy(source, target, sems.at[i]) for i, (source, target) in enumerate(pairs)]
    for copy in copies:
        copy.start()
    for copy in copies:
        copy.wait()


def columns_kernel(w_ref, keep_ref, give_ref, token_ref, sems):
    core = core_index()
    token_ref[...] = jnp.zeros_like(token_ref)
    copy_all([
        (w_ref.at[:, row_block(side * 2 + which, F)], ref.at[:, pl.ds(side * F, F)])
        for ref, which in ((give_ref, 1 - core), (keep_ref, core))
        for side in range(2)
    ], sems)


def unit_kernel(keep_ref, got_ref, unit_ref, sems):
    core = core_index()
    copy_all([
        (keep_ref, unit_ref.at[row_block(core, SLOT // 2), :]),
        (got_ref, unit_ref.at[row_block(1 - core, SLOT // 2), :]),
    ], sems)


def half_kernel(rows_ref, half_ref, sems):
    copy_all([(rows_ref.at[row_block((y_index() // 2) ^ 1, 2 * QUARTER), :], half_ref)], sems)


def give_kernel(rows_ref, cot_ref, token_ref, give_ref, sems):
    del token_ref
    cols = row_block(1 - core_index(), F)
    copy_all([
        (rows_ref.at[:, cols], give_ref.at[:, pl.ds(0, F)]),
        (cot_ref.at[:, cols], give_ref.at[:, pl.ds(F, F)]),
    ], sems)


def select_kernel(step, map_ref, own_ref, got_ref, *outs):
    y, root = y_index(), root_of(map_ref)
    if step == 0:
        mine = y // 2 == root % 4 // 2
        keep_ref, send_ref = outs
        for ref, quarter in ((keep_ref, y), (send_ref, y ^ 1)):
            ref[...] = jnp.where(mine, own_ref[row_block(quarter, QUARTER), :], got_ref[row_block(quarter % 2, QUARTER), :])
    elif step == 1:
        outs[0][...] = jnp.where(y % 2 == root % 2, own_ref[...], got_ref[...])
    else:
        outs[0][...] = jnp.where(lax.axis_index("section") // 4 == root // 4, own_ref[...], got_ref[...])


def stack_kernel(*refs):
    *parts, out_ref = refs
    rows = out_ref.shape[0] // len(parts)
    for index, part in enumerate(parts):
        out_ref[index * rows:(index + 1) * rows, :] = part[...]


def add_kernel(a_ref, b_ref, out_ref):
    out_ref[...] = a_ref[...] + b_ref[...]


def slot_column(column, offset):
    dp = lax.axis_index("dp")
    column = (dp // 16 + column) % 2
    place = ((dp // 2) % 8 + offset + 8) % 8
    return pl.multiple_of((column * 8 + place) * SLOT, SLOT)


def norm_block(ref, gain_ref, enc_ref, inv_ref):
    @pl.loop(0, PIECE // QUARTER)
    def _(block):
        rows = row_block(block, QUARTER)
        hidden = ref[rows, :].astype(f32)
        inv = lax.rsqrt(jnp.mean(hidden * hidden, axis=1, keepdims=True) + eps)
        inv_ref[rows, :] = jnp.broadcast_to(inv, (QUARTER, 128))
        for slot in range(N_SLOT):
            cols = pl.ds(slot_column(*SLOTS[slot]), SLOT)
            part = ref[rows, cols].astype(f32)
            enc_ref[rows, slot * SLOT:(slot + 1) * SLOT] = (part * inv * gain_ref[:, cols]).astype(bf16)


def norm_kernel(gain_ref, *refs):
    count = len(refs) // 3
    for index in range(count):
        norm_block(refs[index], gain_ref, refs[count + 2 * index], refs[count + 2 * index + 1])


def encoder_kernel(map_ref, gain_ref, cot_ref, a_ref, b_ref, dh_ref, gp_ref, full_ref):
    @pl.when(is_encoder(map_ref))
    def _():
        y = y_index()
        gain = gain_ref[...]
        gp_ref[...] = jnp.zeros_like(gp_ref)
        for index, ref in enumerate((a_ref, b_ref)):

            @pl.loop(0, PIECE // QUARTER)
            def _(block):
                quarter = index * (PIECE // QUARTER) + block
                rows = row_block(quarter, QUARTER)
                place = row_block(y ^ quarter, QUARTER)
                g = cot_ref[place, :].astype(f32)
                hidden = ref[row_block(block, QUARTER), :].astype(f32)
                inv = lax.rsqrt(jnp.mean(hidden * hidden, axis=1, keepdims=True) + eps)
                full_ref[place, :] = (hidden * inv * gain).astype(bf16)
                mean = jnp.mean(hidden * gain * g, axis=1, keepdims=True)
                dh_ref[rows, :] = (inv * gain * g - hidden * (inv * inv * inv * mean)).astype(bf16)
                gp_ref[...] += jnp.sum(g * hidden * inv, axis=0, keepdims=True)


NT = (((1,), (1,)), ((), ()))
TN = (((0,), (0,)), ((), ()))
SCALE = 1.0 / math.sqrt(HEAD)


def main_kernel(*refs):
    units = refs[:N_SLOT]
    encs, hids, invs = refs[N_SLOT:N_SLOT + 4], refs[N_SLOT + 4:N_SLOT + 8], refs[N_SLOT + 8:N_SLOT + 12]
    (map_ref, rows_ref, cot_ref, qg_oth, gain_ref, dh_enc, gp_enc,
     own_out, oth_out, dh_own, dh_oth, gp_ref, kv, dkv, mean_ref) = refs[N_SLOT + 12:]
    for head in range(HALF):
        cols = slice(head * HEAD, (head + 1) * HEAD)
        vcols = slice(F + head * HEAD, F + (head + 1) * HEAD)
        for at in (cols, vcols):
            w = jnp.concatenate([unit[:, at] for unit in units], axis=0)
            enc = jnp.concatenate([ref[...] for ref in encs], axis=0)
            kv[:, at] = jnp.dot(enc, w, preferred_element_type=f32).astype(bf16)
        mine = row_block(core_index() * HALF + head, HEAD)
        for seq, (q, qcols, g, gcols, out) in enumerate((
            (rows_ref, mine, cot_ref, mine, own_out), (qg_oth, cols, qg_oth, vcols, oth_out)
        )):
            rows = slice(seq * LEN, (seq + 1) * LEN)
            qb, gb = q[:, qcols], g[:, gcols]
            kb, vb = kv[rows, cols], kv[rows, vcols]
            scores = lax.dot_general(kb, qb, NT, preferred_element_type=f32) * SCALE
            dprobs = lax.dot_general(vb, gb, NT, preferred_element_type=f32)
            peak = jnp.max(scores, axis=0, keepdims=True)
            e = jnp.exp(scores - peak)
            probs = e * (1.0 / jnp.sum(e, axis=0, keepdims=True))
            rounded = probs.astype(bf16)
            delta = jnp.sum(rounded.astype(f32) * dprobs, axis=0, keepdims=True)
            dscores = (probs * (dprobs - delta)).astype(bf16)
            context = lax.dot_general(rounded, vb, TN, preferred_element_type=f32)
            dq = lax.dot_general(dscores, kb, TN, preferred_element_type=f32) * SCALE
            out[:, cols] = context.astype(bf16)
            out[:, vcols] = dq.astype(bf16)
            dk = (jnp.dot(dscores, qb, preferred_element_type=f32) * SCALE).astype(bf16)
            dv = jnp.dot(rounded, gb, preferred_element_type=f32).astype(bf16)
            dkv[rows, cols] = dk
            dkv[rows, vcols] = dv
            term = dk.astype(f32) * kb.astype(f32) + dv.astype(f32) * vb.astype(f32)
            term = term[:, :128] + term[:, 128:]
            if head:
                term = term + mean_ref[rows, :]
            mean_ref[rows, :] = term

    inv = jnp.concatenate([ref[:, :1] for ref in invs], axis=0)
    factor = inv * inv * (jnp.sum(mean_ref[...], axis=1, keepdims=True) * (1.0 / D))

    @pl.when(jnp.logical_not(is_encoder(map_ref)))
    def _():
        for block in range(N_SLOT // 2):
            w = jnp.concatenate([units[2 * block][...], units[2 * block + 1][...]], axis=0)
            denc = lax.dot_general(dkv[...], w, NT, preferred_element_type=f32)
            for side in range(2):
                cols = pl.ds(slot_column(*SLOTS[2 * block + side]), SLOT)
                total = jnp.zeros((1, SLOT), f32)
                for index, hid in enumerate(hids):
                    rows = slice(index * PIECE, (index + 1) * PIECE)
                    at = slice(index % 2 * PIECE, (index % 2 + 1) * PIECE)
                    out = (dh_own, dh_oth)[index // 2]
                    hidden = hid[:, cols].astype(f32)
                    scaled = inv[rows] * denc[rows, side * SLOT:(side + 1) * SLOT]
                    out[at, cols] = (gain_ref[:, cols] * scaled - hidden * factor[rows]).astype(bf16)
                    total = total + jnp.sum(scaled * hidden, axis=0, keepdims=True)
                gp_ref[:, cols] = total

    @pl.when(is_encoder(map_ref))
    def _():
        dh_oth[...] = jnp.zeros_like(dh_oth)
        dh_own[...] = dh_enc[...]
        gp_ref[...] = gp_enc[...]

    dh_oth[LEN:, :] = two_rows(gp_ref[...])


def two_rows(x):
    high = x.astype(bf16).astype(f32)
    index = lax.broadcasted_iota(jnp.int32, (16, x.shape[1]), 0)
    rows = jnp.where(index == 0, high, jnp.where(index == 1, x - high, 0.0))
    return rows.astype(bf16)


def one_row(rows):
    return rows[0:1, :].astype(f32) + rows[1:2, :].astype(f32)


def attend(units, pieces, where, *args):
    whole = jax.ShapeDtypeStruct((LEN, D), bf16)
    return pl.pallas_call(
        main_kernel,
        in_specs=[VMEM] * (N_SLOT + 12) + [SMEM] + [VMEM] * 6,
        out_specs=[VMEM] * 5,
        out_shape=[
            whole, whole, whole, jax.ShapeDtypeStruct((LEN + 16, D), bf16), jax.ShapeDtypeStruct((1, D), f32)
        ],
        scratch_shapes=[
            pltpu.VMEM((2 * LEN, 2 * F), bf16),
            pltpu.VMEM((2 * LEN, 2 * F), bf16),
            pltpu.VMEM((2 * LEN, 128), f32),
        ],
        compiler_params=pltpu.CompilerParams(vmem_limit_bytes=16 * MIB),
        cost_estimate=pl.CostEstimate(flops=10_000_000_000, bytes_accessed=20_000_000, transcendentals=600_000),
        name="attend",
    )(*units, *pieces, where, *args)


def small_call(kernel, out_shape, args, name, limit=6, where=None):
    first = () if where is None else (where,)
    return pl.pallas_call(
        kernel,
        in_specs=[SMEM] * len(first) + [VMEM] * len(args),
        out_specs=jax.tree.map(lambda _: VMEM, out_shape),
        out_shape=out_shape,
        compiler_params=pltpu.CompilerParams(vmem_limit_bytes=limit * MIB),
        cost_estimate=pl.CostEstimate(flops=0, bytes_accessed=1024, transcendentals=0),
        name=name,
    )(*first, *args)


def copy_call(kernel, out_shape, args, name, count):
    return pl.pallas_call(
        kernel,
        in_specs=[ANY] * len(args),
        out_specs=jax.tree.map(lambda x: VMEM if x.dtype == f32 else ANY, out_shape),
        out_shape=out_shape,
        scratch_shapes=[pltpu.SemaphoreType.DMA((count,))],
        compiler_params=pltpu.CompilerParams(vmem_limit_bytes=MIB),
        cost_estimate=pl.CostEstimate(flops=0, bytes_accessed=1024, transcendentals=0),
        name=name,
    )(*args)


def bf16_rows(rows):
    return jax.ShapeDtypeStruct((rows, D), bf16)


ROWS32 = jax.ShapeDtypeStruct((QUARTER, D), f32)
LINE = jax.ShapeDtypeStruct((1, D), f32)


def split_kernel(own_ref, gp_ref, got_ref, kept_ref, gain_ref, *sent):
    gain_ref[...] = one_row(two_rows(gp_ref[...])) + one_row(got_ref[LEN:, :])
    for step in range(4):
        at = slice(step * QUARTER, (step + 1) * QUARTER)
        part = own_ref[at, :].astype(f32) + got_ref[at, :].astype(f32)
        if step == 0:
            kept_ref[...] = part
        else:
            sent[step - 1][...] = part.astype(bf16)


def sum_kernel(kept_ref, gain_ref, a_ref, b_ref, c_ref, sum_ref, sent_ref, gain_out):
    total = kept_ref[...] + (a_ref[...].astype(f32) + b_ref[...].astype(f32) + c_ref[...].astype(f32))
    sum_ref[...] = total
    sent_ref[...] = total.astype(bf16)
    gain_out[...] = gain_ref[...]


def last_kernel(sum_ref, got_ref, gain_ref, dh_ref, gain_out):
    gain_out[...] = gain_ref[...]
    dh_ref[...] = (sum_ref[...] + got_ref[...].astype(f32)).astype(bf16)


def out_kernel(offset, map_ref, own_ref, oth_ref, *refs):
    *parts, out_ref, sems = refs
    core, y = core_index(), y_index()
    rows = LEN // len(parts)

    @pl.when(jnp.logical_not(is_encoder(map_ref)))
    def _():
        copies = [
            pltpu.make_async_copy(
                ref.at[:, pl.ds(offset, F)],
                out_ref.at[:, pl.ds(pl.multiple_of(place * F, F), F)],
                sems.at[index],
            )
            for index, (ref, place) in enumerate(((own_ref, core), (oth_ref, 1 - core)))
        ]
        for copy in copies:
            copy.start()
        for copy in copies:
            copy.wait()

    @pl.when(is_encoder(map_ref))
    def _():
        copies = []
        for index, part in enumerate(parts):
            start = 0 if len(parts) == 1 else pl.multiple_of((y ^ index) * rows, rows)
            copies.append(
                pltpu.make_async_copy(part, out_ref.at[pl.ds(start, rows), :], sems.at[index])
            )
        for copy in copies:
            copy.start()
        for copy in copies:
            copy.wait()


def put_out(offset, where, own, oth, parts, name):
    return pl.pallas_call(
        functools.partial(out_kernel, offset),
        in_specs=[SMEM] + [ANY] * (2 + len(parts)),
        out_specs=ANY,
        out_shape=jax.ShapeDtypeStruct((LEN, D), bf16),
        scratch_shapes=[pltpu.SemaphoreType.DMA((4,))],
        compiler_params=pltpu.CompilerParams(vmem_limit_bytes=MIB),
        cost_estimate=pl.CostEstimate(flops=0, bytes_accessed=2_000_000, transcendentals=0),
        name=name,
    )(where, own, oth, *parts)


def on_device(section_rows, kv_weight, cotangent, gain, section_map):
    rows, cot, weight, gain = section_rows[0], cotangent[0], kv_weight[0], gain[None]
    quarter = bf16_rows(QUARTER)

    def select(step, own, got):
        outs = [quarter, quarter] if step == 0 else quarter
        kernel = functools.partial(select_kernel, step)
        return small_call(kernel, outs, (own, got), "select", limit=3, where=section_map)

    keep, give, token = copy_call(
        columns_kernel,
        [bf16_rows(SLOT // 2), bf16_rows(SLOT // 2), jax.ShapeDtypeStruct((8, 128), f32)],
        (weight,), "columns", 4,
    )
    order = Order(token)
    got = other_core(give)
    hidden = other_y(copy_call(half_kernel, bf16_rows(2 * QUARTER), (rows,), "half", 1), 2)
    a, b = {0: copy_call(unit_kernel, bf16_rows(SLOT), (keep, got), "unit", 2)}, {}
    up, down, across = from_above(a[0]), from_below(a[0]), other_column(a[0])
    qg_oth = other_core(copy_call(give_kernel, bf16_rows(LEN), (rows, cot, a[0]), "give", 2))

    hidden = order.take(hidden)
    mine, send = select(0, rows, hidden)
    hidden = other_y(send, 1)

    a[1] = order.take(up)
    up, across_1 = from_above(a[1]), other_column(a[1])
    a[-1] = order.take(down)
    down = from_below(a[-1])
    b[0], qg_oth = order.take(across, qg_oth)
    hidden = order.take(hidden)
    mine = select(1, mine, hidden)
    hidden = other_high(mine)

    a[2] = order.take(up)
    up = from_above(a[2])
    a[-2] = order.take(down)
    down, across_2 = from_below(a[-2]), other_column(a[-2])
    b[1] = order.take(across_1)
    hidden = order.take(hidden)
    mine = select(2, mine, hidden)
    hidden = other_y(mine, 1)

    a[3] = order.take(up)
    up = from_above(b[1])
    a[-3] = order.take(down)
    down, across_3 = from_below(a[-3]), other_column(a[-3])
    b[-2] = order.take(across_2)
    hidden = order.take(hidden)
    own_a = small_call(stack_kernel, bf16_rows(PIECE), (mine, hidden), "stack", limit=3)
    hidden, oth_a = other_y(own_a, 2), other_core(own_a)

    a[4] = order.take(down)
    down, across_4 = from_below(b[0]), other_column(a[4])
    b[2] = order.take(up)
    up = from_above(b[2])
    b[-3], oth_a = order.take(across_3, oth_a)
    own_b = order.take(hidden)
    oth_b = other_core(own_b)
    b[3] = order.take(up)
    b[-1] = order.take(down)
    b[4] = order.take(across_4)
    oth_b = order.take(oth_b)
    units = [(a, b)[column][offset] for column, offset in SLOTS]

    def normalise(*pieces):
        outs = [bf16_rows(PIECE), jax.ShapeDtypeStruct((PIECE, 128), f32)] * len(pieces)
        return small_call(norm_kernel, outs, (gain, *pieces), "norm")

    enc_0, inv_0, enc_2, inv_2 = normalise(own_a, oth_a)
    enc_1, inv_1 = normalise(own_b)
    enc_3, inv_3 = normalise(oth_b)
    dh_enc, gp_enc, enc_out = small_call(
        encoder_kernel, [bf16_rows(LEN), LINE, bf16_rows(LEN)], (gain, cot, own_a, own_b), "encoder",
        where=section_map,
    )
    pieces = (enc_0, enc_1, enc_2, enc_3, own_a, own_b, oth_a, oth_b, inv_0, inv_1, inv_2, inv_3)
    own_out, oth_out, dh_own, dh_oth, gp = attend(
        units, pieces, section_map, rows, cot, qg_oth, gain, dh_enc, gp_enc
    )

    def add_from(part, *moves):
        for move in moves:
            part = small_call(add_kernel, LINE, (part, move(part)), "add", limit=1)
        return part

    def z_move(bits):
        return lambda v: dp_swap(v, lambda c, z, k: (c, z ^ bits, k))

    kept, gain_part, *parts = small_call(
        split_kernel, [ROWS32, LINE, quarter, quarter, quarter], (dh_own, gp, other_core(dh_oth)), "split"
    )
    far, near, other = other_y(parts[1], 2), other_y(parts[0], 1), other_y(parts[2], 3)
    gain_part = add_from(gain_part, z_move(1), z_move(2), z_move(4))
    near, far, other, gain_part, got_out = order.take(near, far, other, gain_part, other_core(oth_out))
    kept, sent, gain_part = small_call(
        sum_kernel, [ROWS32, quarter, LINE], (kept, gain_part, near, far, other), "sum"
    )
    crossed = other_high(sent)
    gain_part = add_from(gain_part, other_high, other_column)
    dh, gain_part = small_call(last_kernel, [quarter, LINE], (kept, crossed, gain_part), "last")
    far, near, other = other_y(dh, 2), other_y(dh, 1), other_y(dh, 3)
    gain_part = add_from(gain_part, lambda v: other_y(v, 1), lambda v: other_y(v, 2))
    dhs = [dh, near, far, other]
    section_out = put_out(0, section_map, own_out, got_out, [enc_out], "rows")
    section_grad = put_out(F, section_map, own_out, got_out, dhs, "grads")
    return (section_out[None], section_grad[None], gain_part.reshape(D))


def solution(mesh):
    return jax.shard_map(
        on_device,
        mesh=mesh,
        in_specs=(
            P("section", "dp", None),
            P("section", "dp", None),
            P("section", "dp", None),
            P(),
            P(),
        ),
        out_specs=(P("section", "dp", None), P("section", "dp", None), P()),
        check_vma=False,
    )
```

```python
import functools
import math

import jax
import jax.numpy as jnp
from jax import lax
from jax.experimental import pallas as pl
from jax.experimental.pallas import tpu as pltpu
from jax.sharding import PartitionSpec as P

HEAD = 256
LEN = 256
D = 2048
HALF = 4
F = HALF * HEAD
QUARTER = LEN // 4
PIECE = LEN // 2

eps = 1e-06
bf16 = jnp.bfloat16
f32 = jnp.float32

SLOTS = (
    (0, 0), (0, 1), (0, -1), (1, 0), (0, 2), (0, -2), (1, 1), (0, 3),
    (0, -3), (1, -2), (0, 4), (1, 2), (1, -3), (1, 3), (1, -1), (1, 4),
)
N_SLOT = len(SLOTS)
SLOT = D // N_SLOT

ANY = pl.BlockSpec(memory_space=pl.ANY)
VMEM = pl.BlockSpec(memory_space=pltpu.VMEM)
SMEM = pl.BlockSpec(memory_space=pltpu.SMEM)
MIB = 1024 * 1024


def dp_swap(x, move):
    pairs = []
    for index in range(32):
        column, place, core = index // 16, (index // 2) % 8, index % 2
        column, place, core = move(column, place, core)
        pairs.append((index, (column % 2) * 16 + (place % 8) * 2 + core % 2))
    return lax.ppermute(x, "dp", pairs)


def section_swap(x, move):
    pairs = []
    for index in range(8):
        high, y = move(index // 4, index % 4)
        pairs.append((index, (high % 2) * 4 + y % 4))
    return lax.ppermute(x, "section", pairs)


def other_core(x):
    return dp_swap(x, lambda c, z, k: (c, z, k + 1))


def other_column(x):
    return dp_swap(x, lambda c, z, k: (c + 1, z, k))


def from_above(x):
    return dp_swap(x, lambda c, z, k: (c, z - 1, k))


def from_below(x):
    return dp_swap(x, lambda c, z, k: (c, z + 1, k))


def other_high(x):
    return section_swap(x, lambda h, y: (h + 1, y))


def other_y(x, bits):
    return section_swap(x, lambda h, y: (h, y ^ bits))


def join_kernel(*refs):
    del refs


class Order:
    def __init__(self, token):
        self.token = token

    def take(self, *arrays):
        arrays = arrays + (self.token,)
        count = len(arrays)
        *arrays, self.token = pl.pallas_call(
            join_kernel,
            in_specs=[ANY] * count,
            out_specs=[ANY] * count,
            out_shape=[jax.ShapeDtypeStruct(x.shape, x.dtype) for x in arrays],
            input_output_aliases={i: i for i in range(count)},
            compiler_params=pltpu.CompilerParams(vmem_limit_bytes=MIB),
            cost_estimate=pl.CostEstimate(flops=0, bytes_accessed=1024, transcendentals=0),
            name="join",
        )(*arrays)
        return arrays[0] if count == 2 else arrays


def core_index():
    return lax.axis_index("dp") % 2


def y_index():
    return lax.axis_index("section") % 4


def root_of(map_ref):
    root = jnp.int32(0)
    for index in range(8):
        root = jnp.where(map_ref[index] == 0, index, root)
    return root


def is_encoder(map_ref):
    return root_of(map_ref) == lax.axis_index("section")


def row_block(index, size):
    return pl.ds(pl.multiple_of(index * size, size), size)


def copy_all(pairs, sems):
    copies = [pltpu.make_async_copy(source, target, sems.at[i]) for i, (source, target) in enumerate(pairs)]
    for copy in copies:
        copy.start()
    for copy in copies:
        copy.wait()


def columns_kernel(w_ref, keep_ref, give_ref, token_ref, sems):
    core = core_index()
    token_ref[...] = jnp.zeros_like(token_ref)
    copy_all([
        (w_ref.at[:, row_block(side * 2 + which, F)], ref.at[:, pl.ds(side * F, F)])
        for ref, which in ((give_ref, 1 - core), (keep_ref, core))
        for side in range(2)
    ], sems)


def unit_kernel(keep_ref, got_ref, unit_ref, sems):
    core = core_index()
    copy_all([
        (keep_ref, unit_ref.at[row_block(core, SLOT // 2), :]),
        (got_ref, unit_ref.at[row_block(1 - core, SLOT // 2), :]),
    ], sems)


def half_kernel(rows_ref, half_ref, sems):
    copy_all([(rows_ref.at[row_block((y_index() // 2) ^ 1, 2 * QUARTER), :], half_ref)], sems)


def give_kernel(rows_ref, cot_ref, token_ref, give_ref, sems):
    del token_ref
    cols = row_block(1 - core_index(), F)
    copy_all([
        (rows_ref.at[:, cols], give_ref.at[:, pl.ds(0, F)]),
        (cot_ref.at[:, cols], give_ref.at[:, pl.ds(F, F)]),
    ], sems)


def select_kernel(step, map_ref, own_ref, got_ref, *outs):
    y, root = y_index(), root_of(map_ref)
    if step == 0:
        mine = y // 2 == root % 4 // 2
        keep_ref, send_ref = outs
        for ref, quarter in ((keep_ref, y), (send_ref, y ^ 1)):
            ref[...] = jnp.where(mine, own_ref[row_block(quarter, QUARTER), :], got_ref[row_block(quarter % 2, QUARTER), :])
    elif step == 1:
        outs[0][...] = jnp.where(y % 2 == root % 2, own_ref[...], got_ref[...])
    else:
        outs[0][...] = jnp.where(lax.axis_index("section") // 4 == root // 4, own_ref[...], got_ref[...])


def stack_kernel(*refs):
    *parts, out_ref = refs
    rows = out_ref.shape[0] // len(parts)
    for index, part in enumerate(parts):
        out_ref[index * rows:(index + 1) * rows, :] = part[...]


def add_kernel(a_ref, b_ref, out_ref):
    out_ref[...] = a_ref[...] + b_ref[...]


def slot_column(column, offset):
    dp = lax.axis_index("dp")
    column = (dp // 16 + column) % 2
    place = ((dp // 2) % 8 + offset + 8) % 8
    return pl.multiple_of((column * 8 + place) * SLOT, SLOT)


def norm_block(ref, gain_ref, enc_ref, inv_ref):
    @pl.loop(0, PIECE // QUARTER)
    def _(block):
        rows = row_block(block, QUARTER)
        hidden = ref[rows, :].astype(f32)
        inv = lax.rsqrt(jnp.mean(hidden * hidden, axis=1, keepdims=True) + eps)
        inv_ref[rows, :] = jnp.broadcast_to(inv, (QUARTER, 128))
        for slot in range(N_SLOT):
            cols = pl.ds(slot_column(*SLOTS[slot]), SLOT)
            part = ref[rows, cols].astype(f32)
            enc_ref[rows, slot * SLOT:(slot + 1) * SLOT] = (part * inv * gain_ref[:, cols]).astype(bf16)


def norm_kernel(gain_ref, *refs):
    count = len(refs) // 3
    for index in range(count):
        norm_block(refs[index], gain_ref, refs[count + 2 * index], refs[count + 2 * index + 1])


def encoder_kernel(map_ref, gain_ref, cot_ref, a_ref, b_ref, dh_ref, gp_ref, full_ref):
    @pl.when(is_encoder(map_ref))
    def _():
        y = y_index()
        gain = gain_ref[...]
        gp_ref[...] = jnp.zeros_like(gp_ref)
        for index, ref in enumerate((a_ref, b_ref)):

            @pl.loop(0, PIECE // QUARTER)
            def _(block):
                quarter = index * (PIECE // QUARTER) + block
                rows = row_block(quarter, QUARTER)
                place = row_block(y ^ quarter, QUARTER)
                g = cot_ref[place, :].astype(f32)
                hidden = ref[row_block(block, QUARTER), :].astype(f32)
                inv = lax.rsqrt(jnp.mean(hidden * hidden, axis=1, keepdims=True) + eps)
                full_ref[place, :] = (hidden * inv * gain).astype(bf16)
                mean = jnp.mean(hidden * gain * g, axis=1, keepdims=True)
                dh_ref[rows, :] = (inv * gain * g - hidden * (inv * inv * inv * mean)).astype(bf16)
                gp_ref[...] += jnp.sum(g * hidden * inv, axis=0, keepdims=True)


NT = (((1,), (1,)), ((), ()))
TN = (((0,), (0,)), ((), ()))
SCALE = 1.0 / math.sqrt(HEAD)


def main_kernel(*refs):
    units = refs[:N_SLOT]
    encs, hids, invs = refs[N_SLOT:N_SLOT + 4], refs[N_SLOT + 4:N_SLOT + 8], refs[N_SLOT + 8:N_SLOT + 12]
    (map_ref, rows_ref, cot_ref, qg_oth, gain_ref, dh_enc, gp_enc,
     own_out, oth_out, dh_own, dh_oth, gp_ref, dkv, mean_ref) = refs[N_SLOT + 12:]
    mean_ref[...] = jnp.zeros_like(mean_ref)

    @pl.loop(0, HALF)
    def _(head):
        cols, vcols = row_block(head, HEAD), row_block(HALF + head, HEAD)
        mine = row_block(core_index() * HALF + head, HEAD)
        both = []
        for at in (cols, vcols):
            w = jnp.concatenate([unit[:, at] for unit in units], axis=0)
            enc = jnp.concatenate([ref[...] for ref in encs], axis=0)
            both.append(jnp.dot(enc, w, preferred_element_type=f32).astype(bf16))
        rows = (slice(0, LEN), slice(LEN, 2 * LEN))
        k = [both[0][at] for at in rows]
        v = [both[1][at] for at in rows]
        q = (rows_ref[:, mine], qg_oth[:, cols])
        g = (cot_ref[:, mine], qg_oth[:, vcols])
        two = range(2)
        scores = [lax.dot_general(k[i], q[i], NT, preferred_element_type=f32) * SCALE for i in two]
        dprobs = [lax.dot_general(v[i], g[i], NT, preferred_element_type=f32) for i in two]
        e = [jnp.exp(x - jnp.max(x, axis=0, keepdims=True)) for x in scores]
        probs = [x * (1.0 / jnp.sum(x, axis=0, keepdims=True)) for x in e]
        rounded = [x.astype(bf16) for x in probs]
        delta = [jnp.sum(rounded[i].astype(f32) * dprobs[i], axis=0, keepdims=True) for i in two]
        dscores = [(probs[i] * (dprobs[i] - delta[i])).astype(bf16) for i in two]
        context = [lax.dot_general(rounded[i], v[i], TN, preferred_element_type=f32) for i in two]
        dv = [jnp.dot(rounded[i], g[i], preferred_element_type=f32).astype(bf16) for i in two]
        dk = [(jnp.dot(dscores[i], q[i], preferred_element_type=f32) * SCALE).astype(bf16) for i in two]
        dq = [lax.dot_general(dscores[i], k[i], TN, preferred_element_type=f32) * SCALE for i in two]
        for i, out in enumerate((own_out, oth_out)):
            out[:, cols] = context[i].astype(bf16)
            out[:, vcols] = dq[i].astype(bf16)
            dkv[rows[i], cols] = dk[i]
            dkv[rows[i], vcols] = dv[i]
            term = dk[i].astype(f32) * k[i].astype(f32) + dv[i].astype(f32) * v[i].astype(f32)
            mean_ref[rows[i], :] += term[:, :128] + term[:, 128:]

    inv = jnp.concatenate([ref[:, :1] for ref in invs], axis=0)
    factor = inv * inv * (jnp.sum(mean_ref[...], axis=1, keepdims=True) * (1.0 / D))

    @pl.when(jnp.logical_not(is_encoder(map_ref)))
    def _():
        for block in range(N_SLOT // 2):
            w = jnp.concatenate([units[2 * block][...], units[2 * block + 1][...]], axis=0)
            denc = lax.dot_general(dkv[...], w, NT, preferred_element_type=f32)
            for side in range(2):
                cols = pl.ds(slot_column(*SLOTS[2 * block + side]), SLOT)
                total = jnp.zeros((1, SLOT), f32)
                for index, hid in enumerate(hids):
                    rows = slice(index * PIECE, (index + 1) * PIECE)
                    at = slice(index % 2 * PIECE, (index % 2 + 1) * PIECE)
                    out = (dh_own, dh_oth)[index // 2]
                    hidden = hid[:, cols].astype(f32)
                    scaled = inv[rows] * denc[rows, side * SLOT:(side + 1) * SLOT]
                    out[at, cols] = (gain_ref[:, cols] * scaled - hidden * factor[rows]).astype(bf16)
                    total = total + jnp.sum(scaled * hidden, axis=0, keepdims=True)
                gp_ref[:, cols] = total

    @pl.when(is_encoder(map_ref))
    def _():
        dh_oth[...] = jnp.zeros_like(dh_oth)
        dh_own[...] = dh_enc[...]
        gp_ref[...] = gp_enc[...]

    dh_oth[LEN:, :] = two_rows(gp_ref[...])


def two_rows(x):
    high = x.astype(bf16).astype(f32)
    index = lax.broadcasted_iota(jnp.int32, (16, x.shape[1]), 0)
    rows = jnp.where(index == 0, high, jnp.where(index == 1, x - high, 0.0))
    return rows.astype(bf16)


def one_row(rows):
    return rows[0:1, :].astype(f32) + rows[1:2, :].astype(f32)


def attend(units, pieces, where, *args):
    whole = jax.ShapeDtypeStruct((LEN, D), bf16)
    return pl.pallas_call(
        main_kernel,
        in_specs=[VMEM] * (N_SLOT + 12) + [SMEM] + [VMEM] * 6,
        out_specs=[VMEM] * 5,
        out_shape=[
            whole, whole, whole, jax.ShapeDtypeStruct((LEN + 16, D), bf16), jax.ShapeDtypeStruct((1, D), f32)
        ],
        scratch_shapes=[
            pltpu.VMEM((2 * LEN, 2 * F), bf16),
            pltpu.VMEM((2 * LEN, 128), f32),
        ],
        compiler_params=pltpu.CompilerParams(vmem_limit_bytes=16 * MIB),
        cost_estimate=pl.CostEstimate(flops=10_000_000_000, bytes_accessed=20_000_000, transcendentals=600_000),
        name="attend",
    )(*units, *pieces, where, *args)


def small_call(kernel, out_shape, args, name, limit=6, where=None):
    first = () if where is None else (where,)
    return pl.pallas_call(
        kernel,
        in_specs=[SMEM] * len(first) + [VMEM] * len(args),
        out_specs=jax.tree.map(lambda _: VMEM, out_shape),
        out_shape=out_shape,
        compiler_params=pltpu.CompilerParams(vmem_limit_bytes=limit * MIB),
        cost_estimate=pl.CostEstimate(flops=0, bytes_accessed=1024, transcendentals=0),
        name=name,
    )(*first, *args)


def copy_call(kernel, out_shape, args, name, count):
    return pl.pallas_call(
        kernel,
        in_specs=[ANY] * len(args),
        out_specs=jax.tree.map(lambda x: VMEM if x.dtype == f32 else ANY, out_shape),
        out_shape=out_shape,
        scratch_shapes=[pltpu.SemaphoreType.DMA((count,))],
        compiler_params=pltpu.CompilerParams(vmem_limit_bytes=MIB),
        cost_estimate=pl.CostEstimate(flops=0, bytes_accessed=1024, transcendentals=0),
        name=name,
    )(*args)


def bf16_rows(rows):
    return jax.ShapeDtypeStruct((rows, D), bf16)


ROWS32 = jax.ShapeDtypeStruct((QUARTER, D), f32)
LINE = jax.ShapeDtypeStruct((1, D), f32)


def split_kernel(own_ref, gp_ref, got_ref, kept_ref, gain_ref, *sent):
    gain_ref[...] = one_row(two_rows(gp_ref[...])) + one_row(got_ref[LEN:, :])
    for step in range(4):
        at = slice(step * QUARTER, (step + 1) * QUARTER)
        part = own_ref[at, :].astype(f32) + got_ref[at, :].astype(f32)
        if step == 0:
            kept_ref[...] = part
        else:
            sent[step - 1][...] = part.astype(bf16)


def sum_kernel(kept_ref, gain_ref, a_ref, b_ref, c_ref, sum_ref, sent_ref, gain_out):
    total = kept_ref[...] + (a_ref[...].astype(f32) + b_ref[...].astype(f32) + c_ref[...].astype(f32))
    sum_ref[...] = total
    sent_ref[...] = total.astype(bf16)
    gain_out[...] = gain_ref[...]


def last_kernel(sum_ref, got_ref, gain_ref, dh_ref, gain_out):
    gain_out[...] = gain_ref[...]
    dh_ref[...] = (sum_ref[...] + got_ref[...].astype(f32)).astype(bf16)


def out_kernel(offset, map_ref, own_ref, oth_ref, *refs):
    *parts, out_ref, sems = refs
    core, y = core_index(), y_index()
    rows = LEN // len(parts)

    @pl.when(jnp.logical_not(is_encoder(map_ref)))
    def _():
        copies = [
            pltpu.make_async_copy(
                ref.at[:, pl.ds(offset, F)],
                out_ref.at[:, pl.ds(pl.multiple_of(place * F, F), F)],
                sems.at[index],
            )
            for index, (ref, place) in enumerate(((own_ref, core), (oth_ref, 1 - core)))
        ]
        for copy in copies:
            copy.start()
        for copy in copies:
            copy.wait()

    @pl.when(is_encoder(map_ref))
    def _():
        copies = []
        for index, part in enumerate(parts):
            start = 0 if len(parts) == 1 else pl.multiple_of((y ^ index) * rows, rows)
            copies.append(
                pltpu.make_async_copy(part, out_ref.at[pl.ds(start, rows), :], sems.at[index])
            )
        for copy in copies:
            copy.start()
        for copy in copies:
            copy.wait()


def put_out(offset, where, own, oth, parts, name):
    return pl.pallas_call(
        functools.partial(out_kernel, offset),
        in_specs=[SMEM] + [ANY] * (2 + len(parts)),
        out_specs=ANY,
        out_shape=jax.ShapeDtypeStruct((LEN, D), bf16),
        scratch_shapes=[pltpu.SemaphoreType.DMA((4,))],
        compiler_params=pltpu.CompilerParams(vmem_limit_bytes=MIB),
        cost_estimate=pl.CostEstimate(flops=0, bytes_accessed=2_000_000, transcendentals=0),
        name=name,
    )(where, own, oth, *parts)


def on_device(section_rows, kv_weight, cotangent, gain, section_map):
    rows, cot, weight, gain = section_rows[0], cotangent[0], kv_weight[0], gain[None]
    quarter = bf16_rows(QUARTER)

    def select(step, own, got):
        outs = [quarter, quarter] if step == 0 else quarter
        kernel = functools.partial(select_kernel, step)
        return small_call(kernel, outs, (own, got), "select", limit=3, where=section_map)

    keep, give, token = copy_call(
        columns_kernel,
        [bf16_rows(SLOT // 2), bf16_rows(SLOT // 2), jax.ShapeDtypeStruct((8, 128), f32)],
        (weight,), "columns", 4,
    )
    order = Order(token)
    got = other_core(give)
    hidden = other_y(copy_call(half_kernel, bf16_rows(2 * QUARTER), (rows,), "half", 1), 2)
    a, b = {0: copy_call(unit_kernel, bf16_rows(SLOT), (keep, got), "unit", 2)}, {}
    up, down, across = from_above(a[0]), from_below(a[0]), other_column(a[0])
    qg_oth = other_core(copy_call(give_kernel, bf16_rows(LEN), (rows, cot, a[0]), "give", 2))

    hidden = order.take(hidden)
    mine, send = select(0, rows, hidden)
    hidden = other_y(send, 1)

    a[1] = order.take(up)
    up, across_1 = from_above(a[1]), other_column(a[1])
    a[-1] = order.take(down)
    down = from_below(a[-1])
    b[0], qg_oth = order.take(across, qg_oth)
    hidden = order.take(hidden)
    mine = select(1, mine, hidden)
    hidden = other_high(mine)

    a[2] = order.take(up)
    up = from_above(a[2])
    a[-2] = order.take(down)
    down, across_2 = from_below(a[-2]), other_column(a[-2])
    b[1] = order.take(across_1)
    hidden = order.take(hidden)
    mine = select(2, mine, hidden)
    hidden = other_y(mine, 1)

    a[3] = order.take(up)
    up = from_above(b[1])
    a[-3] = order.take(down)
    down, across_3 = from_below(a[-3]), other_column(a[-3])
    hidden = order.take(hidden)
    own_a = small_call(stack_kernel, bf16_rows(PIECE), (mine, hidden), "stack", limit=3)
    hidden, oth_a = other_y(own_a, 2), other_core(own_a)
    b[-2] = order.take(across_2)

    a[4] = order.take(down)
    down, across_4 = from_below(b[0]), other_column(a[4])
    b[2] = order.take(up)
    up = from_above(b[2])
    b[-3], oth_a = order.take(across_3, oth_a)
    own_b = order.take(hidden)
    oth_b = other_core(own_b)
    b[3] = order.take(up)
    b[-1] = order.take(down)
    b[4] = order.take(across_4)
    oth_b = order.take(oth_b)
    units = [(a, b)[column][offset] for column, offset in SLOTS]

    def normalise(*pieces):
        outs = [bf16_rows(PIECE), jax.ShapeDtypeStruct((PIECE, 128), f32)] * len(pieces)
        return small_call(norm_kernel, outs, (gain, *pieces), "norm")

    enc_0, inv_0, enc_2, inv_2 = normalise(own_a, oth_a)
    enc_1, inv_1 = normalise(own_b)
    enc_3, inv_3 = normalise(oth_b)
    dh_enc, gp_enc, enc_out = small_call(
        encoder_kernel, [bf16_rows(LEN), LINE, bf16_rows(LEN)], (gain, cot, own_a, own_b), "encoder",
        where=section_map,
    )
    pieces = (enc_0, enc_1, enc_2, enc_3, own_a, own_b, oth_a, oth_b, inv_0, inv_1, inv_2, inv_3)
    own_out, oth_out, dh_own, dh_oth, gp = attend(
        units, pieces, section_map, rows, cot, qg_oth, gain, dh_enc, gp_enc
    )

    def add_from(part, *moves):
        for move in moves:
            part = small_call(add_kernel, LINE, (part, move(part)), "add", limit=1)
        return part

    def z_move(bits):
        return lambda v: dp_swap(v, lambda c, z, k: (c, z ^ bits, k))

    kept, gain_part, *parts = small_call(
        split_kernel, [ROWS32, LINE, quarter, quarter, quarter], (dh_own, gp, other_core(dh_oth)), "split"
    )
    far, near, other = other_y(parts[1], 2), other_y(parts[0], 1), other_y(parts[2], 3)
    gain_part = add_from(gain_part, z_move(1), z_move(2))
    near, far, other, gain_part, got_out = order.take(near, far, other, gain_part, other_core(oth_out))
    kept, sent, gain_part = small_call(
        sum_kernel, [ROWS32, quarter, LINE], (kept, gain_part, near, far, other), "sum"
    )
    crossed = other_high(sent)
    gain_part = add_from(gain_part, lambda v: other_y(v, 1), lambda v: other_y(v, 2))
    dh, gain_part = small_call(last_kernel, [quarter, LINE], (kept, crossed, gain_part), "last")
    far, near, other = other_y(dh, 2), other_y(dh, 1), other_y(dh, 3)
    gain_part = add_from(gain_part, z_move(4), other_column, other_high)
    dhs = [dh, near, far, other]
    section_out = put_out(0, section_map, own_out, got_out, [enc_out], "rows")
    section_grad = put_out(F, section_map, own_out, got_out, dhs, "grads")
    return (section_out[None], section_grad[None], gain_part.reshape(D))


def solution(mesh):
    return jax.shard_map(
        on_device,
        mesh=mesh,
        in_specs=(
            P("section", "dp", None),
            P("section", "dp", None),
            P("section", "dp", None),
            P(),
            P(),
        ),
        out_specs=(P("section", "dp", None), P("section", "dp", None), P()),
        check_vma=False,
    )
```

```python
import functools
import math

import jax
import jax.numpy as jnp
from jax import lax
from jax.experimental import pallas as pl
from jax.experimental.pallas import tpu as pltpu
from jax.sharding import PartitionSpec as P

HEAD = 256
LEN = 256
D = 2048
HALF = 4
F = HALF * HEAD
QUARTER = LEN // 4
PIECE = LEN // 2

eps = 1e-06
bf16 = jnp.bfloat16
f32 = jnp.float32

SLOTS = (
    (0, 0), (0, 1), (0, -1), (1, 0), (0, 2), (0, -2), (1, 1), (0, 3),
    (0, -3), (1, -2), (0, 4), (1, 2), (1, -3), (1, 3), (1, -1), (1, 4),
)
N_SLOT = len(SLOTS)
SLOT = D // N_SLOT

ANY = pl.BlockSpec(memory_space=pl.ANY)
VMEM = pl.BlockSpec(memory_space=pltpu.VMEM)
SMEM = pl.BlockSpec(memory_space=pltpu.SMEM)
MIB = 1024 * 1024


def dp_swap(x, move):
    pairs = []
    for index in range(32):
        column, place, core = index // 16, (index // 2) % 8, index % 2
        column, place, core = move(column, place, core)
        pairs.append((index, (column % 2) * 16 + (place % 8) * 2 + core % 2))
    return lax.ppermute(x, "dp", pairs)


def section_swap(x, move):
    pairs = []
    for index in range(8):
        high, y = move(index // 4, index % 4)
        pairs.append((index, (high % 2) * 4 + y % 4))
    return lax.ppermute(x, "section", pairs)


def other_core(x):
    return dp_swap(x, lambda c, z, k: (c, z, k + 1))


def other_column(x):
    return dp_swap(x, lambda c, z, k: (c + 1, z, k))


def from_above(x):
    return dp_swap(x, lambda c, z, k: (c, z - 1, k))


def from_below(x):
    return dp_swap(x, lambda c, z, k: (c, z + 1, k))


def other_high(x):
    return section_swap(x, lambda h, y: (h + 1, y))


def other_y(x, bits):
    return section_swap(x, lambda h, y: (h, y ^ bits))


def join_kernel(*refs):
    del refs


class Order:
    def __init__(self, token):
        self.token = token

    def take(self, *arrays):
        arrays = arrays + (self.token,)
        count = len(arrays)
        *arrays, self.token = pl.pallas_call(
            join_kernel,
            in_specs=[ANY] * count,
            out_specs=[ANY] * count,
            out_shape=[jax.ShapeDtypeStruct(x.shape, x.dtype) for x in arrays],
            input_output_aliases={i: i for i in range(count)},
            compiler_params=pltpu.CompilerParams(vmem_limit_bytes=MIB),
            cost_estimate=pl.CostEstimate(flops=0, bytes_accessed=1024, transcendentals=0),
            name="join",
        )(*arrays)
        return arrays[0] if count == 2 else arrays


def core_index():
    return lax.axis_index("dp") % 2


def y_index():
    return lax.axis_index("section") % 4


def root_of(map_ref):
    root = jnp.int32(0)
    for index in range(8):
        root = jnp.where(map_ref[index] == 0, index, root)
    return root


def is_encoder(map_ref):
    return root_of(map_ref) == lax.axis_index("section")


def row_block(index, size):
    return pl.ds(pl.multiple_of(index * size, size), size)


def copy_all(pairs, sems):
    copies = [pltpu.make_async_copy(source, target, sems.at[i]) for i, (source, target) in enumerate(pairs)]
    for copy in copies:
        copy.start()
    for copy in copies:
        copy.wait()


def columns_kernel(w_ref, keep_ref, give_ref, token_ref, sems):
    core = core_index()
    token_ref[...] = jnp.zeros_like(token_ref)
    copy_all([
        (w_ref.at[:, row_block(side * 2 + which, F)], ref.at[:, pl.ds(side * F, F)])
        for ref, which in ((give_ref, 1 - core), (keep_ref, core))
        for side in range(2)
    ], sems)


def unit_kernel(keep_ref, got_ref, unit_ref, sems):
    core = core_index()
    copy_all([
        (keep_ref, unit_ref.at[row_block(core, SLOT // 2), :]),
        (got_ref, unit_ref.at[row_block(1 - core, SLOT // 2), :]),
    ], sems)


def half_kernel(rows_ref, half_ref, sems):
    copy_all([(rows_ref.at[row_block((y_index() // 2) ^ 1, 2 * QUARTER), :], half_ref)], sems)


def give_kernel(rows_ref, cot_ref, token_ref, give_ref, sems):
    del token_ref
    cols = row_block(1 - core_index(), F)
    copy_all([
        (rows_ref.at[:, cols], give_ref.at[:, pl.ds(0, F)]),
        (cot_ref.at[:, cols], give_ref.at[:, pl.ds(F, F)]),
    ], sems)


def butterfly_kernel(a_ref, b_ref, c_ref, d_ref, out_ref):
    out_ref[...] = (a_ref[...] + b_ref[...]) + (c_ref[...] + d_ref[...])


def select_kernel(step, map_ref, own_ref, got_ref, *outs):
    y, root = y_index(), root_of(map_ref)
    if step == 0:
        mine = y // 2 == root % 4 // 2
        keep_ref, send_ref = outs
        for ref, quarter in ((keep_ref, y), (send_ref, y ^ 1)):
            ref[...] = jnp.where(mine, own_ref[row_block(quarter, QUARTER), :], got_ref[row_block(quarter % 2, QUARTER), :])
    elif step == 1:
        outs[0][...] = jnp.where(y % 2 == root % 2, own_ref[...], got_ref[...])
    else:
        outs[0][...] = jnp.where(lax.axis_index("section") // 4 == root // 4, own_ref[...], got_ref[...])


def stack_kernel(*refs):
    *parts, out_ref = refs
    rows = out_ref.shape[0] // len(parts)
    for index, part in enumerate(parts):
        out_ref[index * rows:(index + 1) * rows, :] = part[...]


def add_kernel(a_ref, b_ref, out_ref):
    out_ref[...] = a_ref[...] + b_ref[...]


def slot_column(column, offset):
    dp = lax.axis_index("dp")
    column = (dp // 16 + column) % 2
    place = ((dp // 2) % 8 + offset + 8) % 8
    return pl.multiple_of((column * 8 + place) * SLOT, SLOT)


def norm_block(ref, gain_ref, enc_ref, inv_ref):
    @pl.loop(0, PIECE // QUARTER)
    def _(block):
        rows = row_block(block, QUARTER)
        hidden = ref[rows, :].astype(f32)
        inv = lax.rsqrt(jnp.mean(hidden * hidden, axis=1, keepdims=True) + eps)
        inv_ref[rows, :] = jnp.broadcast_to(inv, (QUARTER, 128))
        for slot in range(N_SLOT):
            cols = pl.ds(slot_column(*SLOTS[slot]), SLOT)
            part = ref[rows, cols].astype(f32)
            enc_ref[rows, slot * SLOT:(slot + 1) * SLOT] = (part * inv * gain_ref[:, cols]).astype(bf16)


def norm_kernel(gain_ref, *refs):
    count = len(refs) // 3
    for index in range(count):
        norm_block(refs[index], gain_ref, refs[count + 2 * index], refs[count + 2 * index + 1])


def encoder_kernel(map_ref, gain_ref, cot_ref, a_ref, b_ref, dh_ref, gp_ref, full_ref):
    @pl.when(is_encoder(map_ref))
    def _():
        y = y_index()
        gain = gain_ref[...]
        gp_ref[...] = jnp.zeros_like(gp_ref)
        for index, ref in enumerate((a_ref, b_ref)):

            @pl.loop(0, PIECE // QUARTER)
            def _(block):
                quarter = index * (PIECE // QUARTER) + block
                rows = row_block(quarter, QUARTER)
                place = row_block(y ^ quarter, QUARTER)
                g = cot_ref[place, :].astype(f32)
                hidden = ref[row_block(block, QUARTER), :].astype(f32)
                inv = lax.rsqrt(jnp.mean(hidden * hidden, axis=1, keepdims=True) + eps)
                full_ref[place, :] = (hidden * inv * gain).astype(bf16)
                mean = jnp.mean(hidden * gain * g, axis=1, keepdims=True)
                dh_ref[rows, :] = (inv * gain * g - hidden * (inv * inv * inv * mean)).astype(bf16)
                gp_ref[...] += jnp.sum(g * hidden * inv, axis=0, keepdims=True)


NT = (((1,), (1,)), ((), ()))
TN = (((0,), (0,)), ((), ()))
SCALE = 1.0 / math.sqrt(HEAD)


def main_kernel(*refs):
    units = refs[:N_SLOT]
    encs, hids, invs = refs[N_SLOT:N_SLOT + 4], refs[N_SLOT + 4:N_SLOT + 8], refs[N_SLOT + 8:N_SLOT + 12]
    (map_ref, rows_ref, cot_ref, qg_oth, gain_ref, dh_enc, gp_enc,
     own_out, oth_out, dh_own, dh_oth, gp_ref, dkv, mean_ref) = refs[N_SLOT + 12:]
    mean_ref[...] = jnp.zeros_like(mean_ref)

    @pl.loop(0, HALF)
    def _(head):
        cols, vcols = row_block(head, HEAD), row_block(HALF + head, HEAD)
        mine = row_block(core_index() * HALF + head, HEAD)
        both = []
        for at in (cols, vcols):
            w = jnp.concatenate([unit[:, at] for unit in units], axis=0)
            enc = jnp.concatenate([ref[...] for ref in encs], axis=0)
            both.append(jnp.dot(enc, w, preferred_element_type=f32).astype(bf16))
        rows = (slice(0, LEN), slice(LEN, 2 * LEN))
        k = [both[0][at] for at in rows]
        v = [both[1][at] for at in rows]
        q = (rows_ref[:, mine], qg_oth[:, cols])
        g = (cot_ref[:, mine], qg_oth[:, vcols])
        two = range(2)
        scores = [lax.dot_general(k[i], q[i], NT, preferred_element_type=f32) * SCALE for i in two]
        dprobs = [lax.dot_general(v[i], g[i], NT, preferred_element_type=f32) for i in two]
        e = [jnp.exp(x - jnp.max(x, axis=0, keepdims=True)) for x in scores]
        probs = [x * (1.0 / jnp.sum(x, axis=0, keepdims=True)) for x in e]
        rounded = [x.astype(bf16) for x in probs]
        delta = [jnp.sum(rounded[i].astype(f32) * dprobs[i], axis=0, keepdims=True) for i in two]
        dscores = [(probs[i] * (dprobs[i] - delta[i])).astype(bf16) for i in two]
        context = [lax.dot_general(rounded[i], v[i], TN, preferred_element_type=f32) for i in two]
        dv = [jnp.dot(rounded[i], g[i], preferred_element_type=f32).astype(bf16) for i in two]
        dk = [(jnp.dot(dscores[i], q[i], preferred_element_type=f32) * SCALE).astype(bf16) for i in two]
        dq = [lax.dot_general(dscores[i], k[i], TN, preferred_element_type=f32) * SCALE for i in two]
        for i, out in enumerate((own_out, oth_out)):
            out[:, cols] = context[i].astype(bf16)
            out[:, vcols] = dq[i].astype(bf16)
            dkv[rows[i], cols] = dk[i]
            dkv[rows[i], vcols] = dv[i]
            term = dk[i].astype(f32) * k[i].astype(f32) + dv[i].astype(f32) * v[i].astype(f32)
            mean_ref[rows[i], :] += term[:, :128] + term[:, 128:]

    inv = jnp.concatenate([ref[:, :1] for ref in invs], axis=0)
    factor = inv * inv * (jnp.sum(mean_ref[...], axis=1, keepdims=True) * (1.0 / D))

    @pl.when(jnp.logical_not(is_encoder(map_ref)))
    def _():
        for block in range(N_SLOT // 2):
            w = jnp.concatenate([units[2 * block][...], units[2 * block + 1][...]], axis=0)
            denc = lax.dot_general(dkv[...], w, NT, preferred_element_type=f32)
            for side in range(2):
                cols = pl.ds(slot_column(*SLOTS[2 * block + side]), SLOT)
                total = jnp.zeros((1, SLOT), f32)
                for index, hid in enumerate(hids):
                    rows = slice(index * PIECE, (index + 1) * PIECE)
                    at = slice(index % 2 * PIECE, (index % 2 + 1) * PIECE)
                    out = (dh_own, dh_oth)[index // 2]
                    hidden = hid[:, cols].astype(f32)
                    scaled = inv[rows] * denc[rows, side * SLOT:(side + 1) * SLOT]
                    out[at, cols] = (gain_ref[:, cols] * scaled - hidden * factor[rows]).astype(bf16)
                    total = total + jnp.sum(scaled * hidden, axis=0, keepdims=True)
                gp_ref[:, cols] = total

    @pl.when(is_encoder(map_ref))
    def _():
        dh_oth[...] = jnp.zeros_like(dh_oth)
        dh_own[...] = dh_enc[...]
        gp_ref[...] = gp_enc[...]

    dh_oth[LEN:, :] = two_rows(gp_ref[...])


def two_rows(x):
    high = x.astype(bf16).astype(f32)
    index = lax.broadcasted_iota(jnp.int32, (16, x.shape[1]), 0)
    rows = jnp.where(index == 0, high, jnp.where(index == 1, x - high, 0.0))
    return rows.astype(bf16)


def one_row(rows):
    return rows[0:1, :].astype(f32) + rows[1:2, :].astype(f32)


def attend(units, pieces, where, *args):
    whole = jax.ShapeDtypeStruct((LEN, D), bf16)
    return pl.pallas_call(
        main_kernel,
        in_specs=[VMEM] * (N_SLOT + 12) + [SMEM] + [VMEM] * 6,
        out_specs=[VMEM] * 5,
        out_shape=[
            whole, whole, whole, jax.ShapeDtypeStruct((LEN + 16, D), bf16), jax.ShapeDtypeStruct((1, D), f32)
        ],
        scratch_shapes=[
            pltpu.VMEM((2 * LEN, 2 * F), bf16),
            pltpu.VMEM((2 * LEN, 128), f32),
        ],
        compiler_params=pltpu.CompilerParams(vmem_limit_bytes=16 * MIB),
        cost_estimate=pl.CostEstimate(flops=10_000_000_000, bytes_accessed=20_000_000, transcendentals=600_000),
        name="attend",
    )(*units, *pieces, where, *args)


def small_call(kernel, out_shape, args, name, limit=6, where=None):
    first = () if where is None else (where,)
    return pl.pallas_call(
        kernel,
        in_specs=[SMEM] * len(first) + [VMEM] * len(args),
        out_specs=jax.tree.map(lambda _: VMEM, out_shape),
        out_shape=out_shape,
        compiler_params=pltpu.CompilerParams(vmem_limit_bytes=limit * MIB),
        cost_estimate=pl.CostEstimate(flops=0, bytes_accessed=1024, transcendentals=0),
        name=name,
    )(*first, *args)


def copy_call(kernel, out_shape, args, name, count):
    return pl.pallas_call(
        kernel,
        in_specs=[ANY] * len(args),
        out_specs=jax.tree.map(lambda x: VMEM if x.dtype == f32 else ANY, out_shape),
        out_shape=out_shape,
        scratch_shapes=[pltpu.SemaphoreType.DMA((count,))],
        compiler_params=pltpu.CompilerParams(vmem_limit_bytes=MIB),
        cost_estimate=pl.CostEstimate(flops=0, bytes_accessed=1024, transcendentals=0),
        name=name,
    )(*args)


def bf16_rows(rows):
    return jax.ShapeDtypeStruct((rows, D), bf16)


ROWS32 = jax.ShapeDtypeStruct((QUARTER, D), f32)
LINE = jax.ShapeDtypeStruct((1, D), f32)


def split_kernel(own_ref, gp_ref, got_ref, kept_ref, gain_ref, *sent):
    gain_ref[...] = one_row(two_rows(gp_ref[...])) + one_row(got_ref[LEN:, :])
    for step in range(4):
        at = slice(step * QUARTER, (step + 1) * QUARTER)
        part = own_ref[at, :].astype(f32) + got_ref[at, :].astype(f32)
        if step == 0:
            kept_ref[...] = part
        else:
            sent[step - 1][...] = part.astype(bf16)


def sum_kernel(kept_ref, gain_ref, a_ref, b_ref, c_ref, sum_ref, sent_ref, gain_out):
    total = kept_ref[...] + (a_ref[...].astype(f32) + b_ref[...].astype(f32) + c_ref[...].astype(f32))
    sum_ref[...] = total
    sent_ref[...] = total.astype(bf16)
    gain_out[...] = gain_ref[...]


def last_kernel(sum_ref, got_ref, gain_ref, dh_ref, gain_out):
    gain_out[...] = gain_ref[...]
    dh_ref[...] = (sum_ref[...] + got_ref[...].astype(f32)).astype(bf16)


def out_kernel(offset, map_ref, own_ref, oth_ref, *refs):
    *parts, out_ref, sems = refs
    core, y = core_index(), y_index()
    rows = LEN // len(parts)

    @pl.when(jnp.logical_not(is_encoder(map_ref)))
    def _():
        copies = [
            pltpu.make_async_copy(
                ref.at[:, pl.ds(offset, F)],
                out_ref.at[:, pl.ds(pl.multiple_of(place * F, F), F)],
                sems.at[index],
            )
            for index, (ref, place) in enumerate(((own_ref, core), (oth_ref, 1 - core)))
        ]
        for copy in copies:
            copy.start()
        for copy in copies:
            copy.wait()

    @pl.when(is_encoder(map_ref))
    def _():
        copies = []
        for index, part in enumerate(parts):
            start = 0 if len(parts) == 1 else pl.multiple_of((y ^ index) * rows, rows)
            copies.append(
                pltpu.make_async_copy(part, out_ref.at[pl.ds(start, rows), :], sems.at[index])
            )
        for copy in copies:
            copy.start()
        for copy in copies:
            copy.wait()


def put_out(offset, where, own, oth, parts, name):
    return pl.pallas_call(
        functools.partial(out_kernel, offset),
        in_specs=[SMEM] + [ANY] * (2 + len(parts)),
        out_specs=ANY,
        out_shape=jax.ShapeDtypeStruct((LEN, D), bf16),
        scratch_shapes=[pltpu.SemaphoreType.DMA((4,))],
        compiler_params=pltpu.CompilerParams(vmem_limit_bytes=MIB),
        cost_estimate=pl.CostEstimate(flops=0, bytes_accessed=2_000_000, transcendentals=0),
        name=name,
    )(where, own, oth, *parts)


def on_device(section_rows, kv_weight, cotangent, gain, section_map):
    rows, cot, weight, gain = section_rows[0], cotangent[0], kv_weight[0], gain[None]
    quarter = bf16_rows(QUARTER)

    def select(step, own, got):
        outs = [quarter, quarter] if step == 0 else quarter
        kernel = functools.partial(select_kernel, step)
        return small_call(kernel, outs, (own, got), "select", limit=3, where=section_map)

    keep, give, token = copy_call(
        columns_kernel,
        [bf16_rows(SLOT // 2), bf16_rows(SLOT // 2), jax.ShapeDtypeStruct((8, 128), f32)],
        (weight,), "columns", 4,
    )
    order = Order(token)
    got = other_core(give)
    hidden = other_y(copy_call(half_kernel, bf16_rows(2 * QUARTER), (rows,), "half", 1), 2)
    a, b = {0: copy_call(unit_kernel, bf16_rows(SLOT), (keep, got), "unit", 2)}, {}
    up, down, across = from_above(a[0]), from_below(a[0]), other_column(a[0])
    qg_oth = other_core(copy_call(give_kernel, bf16_rows(LEN), (rows, cot, a[0]), "give", 2))

    hidden = order.take(hidden)
    mine, send = select(0, rows, hidden)
    hidden = other_y(send, 1)

    a[1] = order.take(up)
    up, across_1 = from_above(a[1]), other_column(a[1])
    a[-1] = order.take(down)
    down = from_below(a[-1])
    b[0], qg_oth = order.take(across, qg_oth)
    hidden = order.take(hidden)
    mine = select(1, mine, hidden)
    hidden = other_high(mine)

    a[2] = order.take(up)
    up = from_above(a[2])
    a[-2] = order.take(down)
    down, across_2 = from_below(a[-2]), other_column(a[-2])
    b[1] = order.take(across_1)
    hidden = order.take(hidden)
    mine = select(2, mine, hidden)
    hidden = other_y(mine, 1)

    a[3] = order.take(up)
    up = from_above(b[1])
    a[-3] = order.take(down)
    down, across_3 = from_below(a[-3]), other_column(a[-3])
    b[-2] = order.take(across_2)
    hidden = order.take(hidden)
    own_a = small_call(stack_kernel, bf16_rows(PIECE), (mine, hidden), "stack", limit=3)
    hidden = other_y(own_a, 2)

    a[4] = order.take(down)
    down, across_4 = from_below(b[0]), other_column(a[4])
    b[2] = order.take(up)
    up = from_above(b[2])
    b[-3] = order.take(across_3)
    own_b = order.take(hidden)
    oth_a, oth_b = other_core(own_a), other_core(own_b)
    b[3] = order.take(up)
    b[-1] = order.take(down)
    b[4] = order.take(across_4)
    oth_a, oth_b = order.take(oth_a, oth_b)
    units = [(a, b)[column][offset] for column, offset in SLOTS]

    def normalise(*pieces):
        outs = [bf16_rows(PIECE), jax.ShapeDtypeStruct((PIECE, 128), f32)] * len(pieces)
        return small_call(norm_kernel, outs, (gain, *pieces), "norm")

    enc_0, inv_0, enc_1, inv_1 = normalise(own_a, own_b)
    enc_2, inv_2, enc_3, inv_3 = normalise(oth_a, oth_b)
    dh_enc, gp_enc, enc_out = small_call(
        encoder_kernel, [bf16_rows(LEN), LINE, bf16_rows(LEN)], (gain, cot, own_a, own_b), "encoder",
        where=section_map,
    )
    pieces = (enc_0, enc_1, enc_2, enc_3, own_a, own_b, oth_a, oth_b, inv_0, inv_1, inv_2, inv_3)
    own_out, oth_out, dh_own, dh_oth, gp = attend(
        units, pieces, section_map, rows, cot, qg_oth, gain, dh_enc, gp_enc
    )

    def add_from(part, *moves):
        for move in moves:
            part = small_call(add_kernel, LINE, (part, move(part)), "add", limit=1)
        return part

    def z_move(bits):
        return lambda v: dp_swap(v, lambda c, z, k: (c, z ^ bits, k))

    kept, gain_part, *parts = small_call(
        split_kernel, [ROWS32, LINE, quarter, quarter, quarter], (dh_own, gp, other_core(dh_oth)), "split"
    )
    far, near, other = other_y(parts[1], 2), other_y(parts[0], 1), other_y(parts[2], 3)
    gain_part = add_from(gain_part, z_move(1), z_move(2))
    near, far, other, gain_part, got_out = order.take(near, far, other, gain_part, other_core(oth_out))
    kept, sent, gain_part = small_call(
        sum_kernel, [ROWS32, quarter, LINE], (kept, gain_part, near, far, other), "sum"
    )
    crossed = other_high(sent)
    gain_part = small_call(
        butterfly_kernel, LINE, (gain_part, *[other_y(gain_part, bits) for bits in (1, 2, 3)]), "add", limit=1
    )
    dh, gain_part = small_call(last_kernel, [quarter, LINE], (kept, crossed, gain_part), "last")
    far, near, other = other_y(dh, 2), other_y(dh, 1), other_y(dh, 3)
    gain_part = add_from(gain_part, z_move(4), other_column, other_high)
    dhs = [dh, near, far, other]
    section_out = put_out(0, section_map, own_out, got_out, [enc_out], "rows")
    section_grad = put_out(F, section_map, own_out, got_out, dhs, "grads")
    return (section_out[None], section_grad[None], gain_part.reshape(D))


def solution(mesh):
    return jax.shard_map(
        on_device,
        mesh=mesh,
        in_specs=(
            P("section", "dp", None),
            P("section", "dp", None),
            P("section", "dp", None),
            P(),
            P(),
        ),
        out_specs=(P("section", "dp", None), P("section", "dp", None), P()),
        check_vma=False,
    )
```

```python
import functools
import math

import jax
import jax.numpy as jnp
from jax import lax
from jax.experimental import pallas as pl
from jax.experimental.pallas import tpu as pltpu
from jax.sharding import PartitionSpec as P

HEAD = 256
LEN = 256
D = 2048
HALF = 4
F = HALF * HEAD
QUARTER = LEN // 4
PIECE = LEN // 2

eps = 1e-06
bf16 = jnp.bfloat16
f32 = jnp.float32

SLOTS = (
    (0, 0), (0, 1), (0, -1), (1, 0), (0, 2), (0, -2), (1, 1), (0, 3),
    (0, -3), (1, -2), (0, 4), (1, 2), (1, -3), (1, 3), (1, -1), (1, 4),
)
N_SLOT = len(SLOTS)
SLOT = D // N_SLOT

ANY = pl.BlockSpec(memory_space=pl.ANY)
VMEM = pl.BlockSpec(memory_space=pltpu.VMEM)
SMEM = pl.BlockSpec(memory_space=pltpu.SMEM)
MIB = 1024 * 1024


def dp_swap(x, move):
    pairs = []
    for index in range(32):
        column, place, core = index // 16, (index // 2) % 8, index % 2
        column, place, core = move(column, place, core)
        pairs.append((index, (column % 2) * 16 + (place % 8) * 2 + core % 2))
    return lax.ppermute(x, "dp", pairs)


def section_swap(x, move):
    pairs = []
    for index in range(8):
        high, y = move(index // 4, index % 4)
        pairs.append((index, (high % 2) * 4 + y % 4))
    return lax.ppermute(x, "section", pairs)


def other_core(x):
    return dp_swap(x, lambda c, z, k: (c, z, k + 1))


def other_column(x):
    return dp_swap(x, lambda c, z, k: (c + 1, z, k))


def from_above(x):
    return dp_swap(x, lambda c, z, k: (c, z - 1, k))


def from_below(x):
    return dp_swap(x, lambda c, z, k: (c, z + 1, k))


def other_high(x):
    return section_swap(x, lambda h, y: (h + 1, y))


def other_y(x, bits):
    return section_swap(x, lambda h, y: (h, y ^ bits))


def join_kernel(*refs):
    del refs


class Order:
    def __init__(self, token):
        self.token = token

    def take(self, *arrays):
        arrays = arrays + (self.token,)
        count = len(arrays)
        *arrays, self.token = pl.pallas_call(
            join_kernel,
            in_specs=[ANY] * count,
            out_specs=[ANY] * count,
            out_shape=[jax.ShapeDtypeStruct(x.shape, x.dtype) for x in arrays],
            input_output_aliases={i: i for i in range(count)},
            compiler_params=pltpu.CompilerParams(vmem_limit_bytes=MIB),
            cost_estimate=pl.CostEstimate(flops=0, bytes_accessed=1024, transcendentals=0),
            name="join",
        )(*arrays)
        return arrays[0] if count == 2 else arrays


def core_index():
    return lax.axis_index("dp") % 2


def y_index():
    return lax.axis_index("section") % 4


def root_of(map_ref):
    root = jnp.int32(0)
    for index in range(8):
        root = jnp.where(map_ref[index] == 0, index, root)
    return root


def is_encoder(map_ref):
    return root_of(map_ref) == lax.axis_index("section")


def row_block(index, size):
    return pl.ds(pl.multiple_of(index * size, size), size)


def copy_all(pairs, sems):
    copies = [pltpu.make_async_copy(source, target, sems.at[i]) for i, (source, target) in enumerate(pairs)]
    for copy in copies:
        copy.start()
    for copy in copies:
        copy.wait()


def columns_kernel(w_ref, keep_ref, give_ref, token_ref, sems):
    core = core_index()
    token_ref[...] = jnp.zeros_like(token_ref)
    copy_all([
        (w_ref.at[:, row_block(side * 2 + which, F)], ref.at[:, pl.ds(side * F, F)])
        for ref, which in ((give_ref, 1 - core), (keep_ref, core))
        for side in range(2)
    ], sems)


def unit_kernel(keep_ref, got_ref, unit_ref, sems):
    core = core_index()
    copy_all([
        (keep_ref, unit_ref.at[row_block(core, SLOT // 2), :]),
        (got_ref, unit_ref.at[row_block(1 - core, SLOT // 2), :]),
    ], sems)


def half_kernel(rows_ref, half_ref, sems):
    copy_all([(rows_ref.at[row_block((y_index() // 2) ^ 1, 2 * QUARTER), :], half_ref)], sems)


def give_kernel(rows_ref, cot_ref, token_ref, give_ref, sems):
    del token_ref
    cols = row_block(1 - core_index(), F)
    copy_all([
        (rows_ref.at[:, cols], give_ref.at[:, pl.ds(0, F)]),
        (cot_ref.at[:, cols], give_ref.at[:, pl.ds(F, F)]),
    ], sems)


def butterfly_kernel(a_ref, b_ref, c_ref, d_ref, out_ref):
    out_ref[...] = (a_ref[...] + b_ref[...]) + (c_ref[...] + d_ref[...])


def select_kernel(step, map_ref, own_ref, got_ref, *outs):
    y, root = y_index(), root_of(map_ref)
    if step == 0:
        mine = y // 2 == root % 4 // 2
        keep_ref, send_ref = outs
        for ref, quarter in ((keep_ref, y), (send_ref, y ^ 1)):
            ref[...] = jnp.where(mine, own_ref[row_block(quarter, QUARTER), :], got_ref[row_block(quarter % 2, QUARTER), :])
    elif step == 1:
        outs[0][...] = jnp.where(y % 2 == root % 2, own_ref[...], got_ref[...])
    else:
        outs[0][...] = jnp.where(lax.axis_index("section") // 4 == root // 4, own_ref[...], got_ref[...])


def stack_kernel(*refs):
    *parts, out_ref = refs
    rows = out_ref.shape[0] // len(parts)
    for index, part in enumerate(parts):
        out_ref[index * rows:(index + 1) * rows, :] = part[...]


def late_kernel(a_ref, token_ref, out_ref):
    del token_ref
    out_ref[...] = a_ref[...]


def add_kernel(a_ref, b_ref, out_ref):
    out_ref[...] = a_ref[...] + b_ref[...]


def slot_column(column, offset):
    dp = lax.axis_index("dp")
    column = (dp // 16 + column) % 2
    place = ((dp // 2) % 8 + offset + 8) % 8
    return pl.multiple_of((column * 8 + place) * SLOT, SLOT)


def norm_block(ref, gain_ref, enc_ref, inv_ref):
    @pl.loop(0, PIECE // QUARTER)
    def _(block):
        rows = row_block(block, QUARTER)
        hidden = ref[rows, :].astype(f32)
        inv = lax.rsqrt(jnp.mean(hidden * hidden, axis=1, keepdims=True) + eps)
        inv_ref[rows, :] = jnp.broadcast_to(inv, (QUARTER, 128))
        for slot in range(N_SLOT):
            cols = pl.ds(slot_column(*SLOTS[slot]), SLOT)
            part = ref[rows, cols].astype(f32)
            enc_ref[rows, slot * SLOT:(slot + 1) * SLOT] = (part * inv * gain_ref[:, cols]).astype(bf16)


def norm_kernel(gain_ref, *refs):
    count = len(refs) // 3
    for index in range(count):
        norm_block(refs[index], gain_ref, refs[count + 2 * index], refs[count + 2 * index + 1])


def encoder_kernel(map_ref, gain_ref, cot_ref, a_ref, b_ref, dh_ref, gp_ref, full_ref):
    @pl.when(is_encoder(map_ref))
    def _():
        y = y_index()
        gain = gain_ref[...]
        gp_ref[...] = jnp.zeros_like(gp_ref)
        for index, ref in enumerate((a_ref, b_ref)):

            @pl.loop(0, PIECE // QUARTER)
            def _(block):
                quarter = index * (PIECE // QUARTER) + block
                rows = row_block(quarter, QUARTER)
                place = row_block(y ^ quarter, QUARTER)
                g = cot_ref[place, :].astype(f32)
                hidden = ref[row_block(block, QUARTER), :].astype(f32)
                inv = lax.rsqrt(jnp.mean(hidden * hidden, axis=1, keepdims=True) + eps)
                full_ref[place, :] = (hidden * inv * gain).astype(bf16)
                mean = jnp.mean(hidden * gain * g, axis=1, keepdims=True)
                dh_ref[rows, :] = (inv * gain * g - hidden * (inv * inv * inv * mean)).astype(bf16)
                gp_ref[...] += jnp.sum(g * hidden * inv, axis=0, keepdims=True)


NT = (((1,), (1,)), ((), ()))
TN = (((0,), (0,)), ((), ()))
SCALE = 1.0 / math.sqrt(HEAD)


def main_kernel(*refs):
    units = refs[:N_SLOT]
    encs, hids, invs = refs[N_SLOT:N_SLOT + 4], refs[N_SLOT + 4:N_SLOT + 8], refs[N_SLOT + 8:N_SLOT + 12]
    (map_ref, rows_ref, cot_ref, qg_oth, gain_ref, dh_enc, gp_enc,
     own_out, oth_out, dh_own, dh_oth, gp_ref, dkv, mean_ref) = refs[N_SLOT + 12:]
    mean_ref[...] = jnp.zeros_like(mean_ref)

    @pl.loop(0, HALF)
    def _(head):
        cols, vcols = row_block(head, HEAD), row_block(HALF + head, HEAD)
        mine = row_block(core_index() * HALF + head, HEAD)
        both = []
        for at in (cols, vcols):
            w = jnp.concatenate([unit[:, at] for unit in units], axis=0)
            enc = jnp.concatenate([ref[...] for ref in encs], axis=0)
            both.append(jnp.dot(enc, w, preferred_element_type=f32).astype(bf16))
        rows = (slice(0, LEN), slice(LEN, 2 * LEN))
        k = [both[0][at] for at in rows]
        v = [both[1][at] for at in rows]
        q = (rows_ref[:, mine], qg_oth[:, cols])
        g = (cot_ref[:, mine], qg_oth[:, vcols])
        two = range(2)
        scores = [lax.dot_general(k[i], q[i], NT, preferred_element_type=f32) * SCALE for i in two]
        dprobs = [lax.dot_general(v[i], g[i], NT, preferred_element_type=f32) for i in two]
        e = [jnp.exp(x - jnp.max(x, axis=0, keepdims=True)) for x in scores]
        probs = [x * (1.0 / jnp.sum(x, axis=0, keepdims=True)) for x in e]
        rounded = [x.astype(bf16) for x in probs]
        delta = [jnp.sum(rounded[i].astype(f32) * dprobs[i], axis=0, keepdims=True) for i in two]
        dscores = [(probs[i] * (dprobs[i] - delta[i])).astype(bf16) for i in two]
        context = [lax.dot_general(rounded[i], v[i], TN, preferred_element_type=f32) for i in two]
        dv = [jnp.dot(rounded[i], g[i], preferred_element_type=f32).astype(bf16) for i in two]
        dk = [(jnp.dot(dscores[i], q[i], preferred_element_type=f32) * SCALE).astype(bf16) for i in two]
        dq = [lax.dot_general(dscores[i], k[i], TN, preferred_element_type=f32) * SCALE for i in two]
        for i, out in enumerate((own_out, oth_out)):
            out[:, cols] = context[i].astype(bf16)
            out[:, vcols] = dq[i].astype(bf16)
            dkv[rows[i], cols] = dk[i]
            dkv[rows[i], vcols] = dv[i]
            term = dk[i].astype(f32) * k[i].astype(f32) + dv[i].astype(f32) * v[i].astype(f32)
            mean_ref[rows[i], :] += term[:, :128] + term[:, 128:]

    inv = jnp.concatenate([ref[:, :1] for ref in invs], axis=0)
    factor = inv * inv * (jnp.sum(mean_ref[...], axis=1, keepdims=True) * (1.0 / D))

    @pl.when(jnp.logical_not(is_encoder(map_ref)))
    def _():
        for block in range(N_SLOT // 2):
            w = jnp.concatenate([units[2 * block][...], units[2 * block + 1][...]], axis=0)
            denc = lax.dot_general(dkv[...], w, NT, preferred_element_type=f32)
            for side in range(2):
                cols = pl.ds(slot_column(*SLOTS[2 * block + side]), SLOT)
                total = jnp.zeros((1, SLOT), f32)
                for index, hid in enumerate(hids):
                    rows = slice(index * PIECE, (index + 1) * PIECE)
                    at = slice(index % 2 * PIECE, (index % 2 + 1) * PIECE)
                    out = (dh_own, dh_oth)[index // 2]
                    hidden = hid[:, cols].astype(f32)
                    scaled = inv[rows] * denc[rows, side * SLOT:(side + 1) * SLOT]
                    out[at, cols] = (gain_ref[:, cols] * scaled - hidden * factor[rows]).astype(bf16)
                    total = total + jnp.sum(scaled * hidden, axis=0, keepdims=True)
                gp_ref[:, cols] = total

    @pl.when(is_encoder(map_ref))
    def _():
        dh_oth[...] = jnp.zeros_like(dh_oth)
        dh_own[...] = dh_enc[...]
        gp_ref[...] = gp_enc[...]

    dh_oth[LEN:, :] = two_rows(gp_ref[...])


def two_rows(x):
    high = x.astype(bf16).astype(f32)
    index = lax.broadcasted_iota(jnp.int32, (16, x.shape[1]), 0)
    rows = jnp.where(index == 0, high, jnp.where(index == 1, x - high, 0.0))
    return rows.astype(bf16)


def one_row(rows):
    return rows[0:1, :].astype(f32) + rows[1:2, :].astype(f32)


def attend(units, pieces, where, *args):
    whole = jax.ShapeDtypeStruct((LEN, D), bf16)
    return pl.pallas_call(
        main_kernel,
        in_specs=[VMEM] * (N_SLOT + 12) + [SMEM] + [VMEM] * 6,
        out_specs=[VMEM] * 5,
        out_shape=[
            whole, whole, whole, jax.ShapeDtypeStruct((LEN + 16, D), bf16), jax.ShapeDtypeStruct((1, D), f32)
        ],
        scratch_shapes=[
            pltpu.VMEM((2 * LEN, 2 * F), bf16),
            pltpu.VMEM((2 * LEN, 128), f32),
        ],
        compiler_params=pltpu.CompilerParams(vmem_limit_bytes=16 * MIB),
        cost_estimate=pl.CostEstimate(flops=10_000_000_000, bytes_accessed=20_000_000, transcendentals=600_000),
        name="attend",
    )(*units, *pieces, where, *args)


def small_call(kernel, out_shape, args, name, limit=6, where=None):
    first = () if where is None else (where,)
    return pl.pallas_call(
        kernel,
        in_specs=[SMEM] * len(first) + [VMEM] * len(args),
        out_specs=jax.tree.map(lambda _: VMEM, out_shape),
        out_shape=out_shape,
        compiler_params=pltpu.CompilerParams(vmem_limit_bytes=limit * MIB),
        cost_estimate=pl.CostEstimate(flops=0, bytes_accessed=1024, transcendentals=0),
        name=name,
    )(*first, *args)


def copy_call(kernel, out_shape, args, name, count):
    return pl.pallas_call(
        kernel,
        in_specs=[ANY] * len(args),
        out_specs=jax.tree.map(lambda x: VMEM if x.dtype == f32 else ANY, out_shape),
        out_shape=out_shape,
        scratch_shapes=[pltpu.SemaphoreType.DMA((count,))],
        compiler_params=pltpu.CompilerParams(vmem_limit_bytes=MIB),
        cost_estimate=pl.CostEstimate(flops=0, bytes_accessed=1024, transcendentals=0),
        name=name,
    )(*args)


def bf16_rows(rows):
    return jax.ShapeDtypeStruct((rows, D), bf16)


ROWS32 = jax.ShapeDtypeStruct((QUARTER, D), f32)
LINE = jax.ShapeDtypeStruct((1, D), f32)


def split_kernel(own_ref, gp_ref, got_ref, kept_ref, gain_ref, *sent):
    gain_ref[...] = one_row(two_rows(gp_ref[...])) + one_row(got_ref[LEN:, :])
    for step in range(4):
        at = slice(step * QUARTER, (step + 1) * QUARTER)
        part = own_ref[at, :].astype(f32) + got_ref[at, :].astype(f32)
        if step == 0:
            kept_ref[...] = part
        else:
            sent[step - 1][...] = part.astype(bf16)


def sum_kernel(kept_ref, gain_ref, a_ref, b_ref, c_ref, sum_ref, sent_ref, gain_out):
    total = kept_ref[...] + (a_ref[...].astype(f32) + b_ref[...].astype(f32) + c_ref[...].astype(f32))
    sum_ref[...] = total
    sent_ref[...] = total.astype(bf16)
    gain_out[...] = gain_ref[...]


def last_kernel(sum_ref, got_ref, gain_ref, dh_ref, gain_out):
    gain_out[...] = gain_ref[...]
    dh_ref[...] = (sum_ref[...] + got_ref[...].astype(f32)).astype(bf16)


def out_kernel(offset, map_ref, own_ref, oth_ref, *refs):
    *parts, out_ref, sems = refs
    core, y = core_index(), y_index()
    rows = LEN // len(parts)

    @pl.when(jnp.logical_not(is_encoder(map_ref)))
    def _():
        copies = [
            pltpu.make_async_copy(
                ref.at[:, pl.ds(offset, F)],
                out_ref.at[:, pl.ds(pl.multiple_of(place * F, F), F)],
                sems.at[index],
            )
            for index, (ref, place) in enumerate(((own_ref, core), (oth_ref, 1 - core)))
        ]
        for copy in copies:
            copy.start()
        for copy in copies:
            copy.wait()

    @pl.when(is_encoder(map_ref))
    def _():
        copies = []
        for index, part in enumerate(parts):
            start = 0 if len(parts) == 1 else pl.multiple_of((y ^ index) * rows, rows)
            copies.append(
                pltpu.make_async_copy(part, out_ref.at[pl.ds(start, rows), :], sems.at[index])
            )
        for copy in copies:
            copy.start()
        for copy in copies:
            copy.wait()


def put_out(offset, where, own, oth, parts, name):
    return pl.pallas_call(
        functools.partial(out_kernel, offset),
        in_specs=[SMEM] + [ANY] * (2 + len(parts)),
        out_specs=ANY,
        out_shape=jax.ShapeDtypeStruct((LEN, D), bf16),
        scratch_shapes=[pltpu.SemaphoreType.DMA((4,))],
        compiler_params=pltpu.CompilerParams(vmem_limit_bytes=MIB),
        cost_estimate=pl.CostEstimate(flops=0, bytes_accessed=2_000_000, transcendentals=0),
        name=name,
    )(where, own, oth, *parts)


def on_device(section_rows, kv_weight, cotangent, gain, section_map):
    rows, cot, weight, gain = section_rows[0], cotangent[0], kv_weight[0], gain[None]
    quarter = bf16_rows(QUARTER)

    def select(step, own, got):
        outs = [quarter, quarter] if step == 0 else quarter
        kernel = functools.partial(select_kernel, step)
        return small_call(kernel, outs, (own, got), "select", limit=3, where=section_map)

    keep, give, token = copy_call(
        columns_kernel,
        [bf16_rows(SLOT // 2), bf16_rows(SLOT // 2), jax.ShapeDtypeStruct((8, 128), f32)],
        (weight,), "columns", 4,
    )
    order = Order(token)
    got = other_core(give)
    hidden = other_y(copy_call(half_kernel, bf16_rows(2 * QUARTER), (rows,), "half", 1), 2)
    a, b = {0: copy_call(unit_kernel, bf16_rows(SLOT), (keep, got), "unit", 2)}, {}
    up, down, across = from_above(a[0]), from_below(a[0]), other_column(a[0])
    qg_oth = other_core(copy_call(give_kernel, bf16_rows(LEN), (rows, cot, a[0]), "give", 2))

    hidden = order.take(hidden)
    mine, send = select(0, rows, hidden)
    hidden = other_y(send, 1)

    a[1] = order.take(up)
    up, across_1 = from_above(a[1]), other_column(a[1])
    a[-1] = order.take(down)
    down = from_below(a[-1])
    b[0], qg_oth = order.take(across, qg_oth)
    hidden = order.take(hidden)
    mine = select(1, mine, hidden)
    hidden = other_high(mine)

    a[2] = order.take(up)
    up = from_above(a[2])
    a[-2] = order.take(down)
    down, across_2 = from_below(a[-2]), other_column(a[-2])
    b[1] = order.take(across_1)
    hidden = order.take(hidden)
    mine = select(2, mine, hidden)
    hidden = other_y(mine, 1)

    a[3] = order.take(up)
    up = from_above(b[1])
    a[-3] = order.take(down)
    down, across_3 = from_below(a[-3]), other_column(a[-3])
    b[-2] = order.take(across_2)
    hidden = order.take(hidden)
    own_a = small_call(stack_kernel, bf16_rows(PIECE), (mine, hidden), "stack", limit=3)
    hidden = other_y(own_a, 2)

    a[4] = order.take(down)
    down, across_4 = from_below(b[0]), other_column(a[4])
    b[2] = order.take(up)
    up = from_above(b[2])
    b[-3] = order.take(across_3)
    own_b = order.take(hidden)
    late_a = small_call(late_kernel, bf16_rows(PIECE), (own_a, order.token), "late", limit=3)
    oth_a, oth_b = other_core(late_a), other_core(own_b)
    b[3] = order.take(up)
    b[-1] = order.take(down)
    b[4] = order.take(across_4)
    oth_a, oth_b = order.take(oth_a, oth_b)
    units = [(a, b)[column][offset] for column, offset in SLOTS]

    def normalise(*pieces):
        outs = [bf16_rows(PIECE), jax.ShapeDtypeStruct((PIECE, 128), f32)] * len(pieces)
        return small_call(norm_kernel, outs, (gain, *pieces), "norm")

    enc_0, inv_0, enc_1, inv_1 = normalise(own_a, own_b)
    enc_2, inv_2, enc_3, inv_3 = normalise(oth_a, oth_b)
    dh_enc, gp_enc, enc_out = small_call(
        encoder_kernel, [bf16_rows(LEN), LINE, bf16_rows(LEN)], (gain, cot, own_a, own_b), "encoder",
        where=section_map,
    )
    pieces = (enc_0, enc_1, enc_2, enc_3, own_a, own_b, oth_a, oth_b, inv_0, inv_1, inv_2, inv_3)
    own_out, oth_out, dh_own, dh_oth, gp = attend(
        units, pieces, section_map, rows, cot, qg_oth, gain, dh_enc, gp_enc
    )

    def add_from(part, *moves):
        for move in moves:
            part = small_call(add_kernel, LINE, (part, move(part)), "add", limit=1)
        return part

    def butterfly(part, *moves):
        return small_call(butterfly_kernel, LINE, (part, *[move(part) for move in moves]), "add", limit=1)

    def z_move(bits):
        return lambda v: dp_swap(v, lambda c, z, k: (c, z ^ bits, k))

    kept, gain_part, *parts = small_call(
        split_kernel, [ROWS32, LINE, quarter, quarter, quarter], (dh_own, gp, other_core(dh_oth)), "split"
    )
    far, near, other = other_y(parts[1], 2), other_y(parts[0], 1), other_y(parts[2], 3)
    gain_part, got_out = order.take(gain_part, other_core(oth_out))
    gain_part = butterfly(gain_part, *[z_move(bits) for bits in (1, 2, 3)])
    gain_part = add_from(gain_part, z_move(4))
    near, far, other, gain_part = order.take(near, far, other, gain_part)
    kept, sent, gain_part = small_call(
        sum_kernel, [ROWS32, quarter, LINE], (kept, gain_part, near, far, other), "sum"
    )
    crossed = other_high(sent)
    gain_part = butterfly(gain_part, *[lambda v, bits=bits: other_y(v, bits) for bits in (1, 2, 3)])
    dh, gain_part = small_call(last_kernel, [quarter, LINE], (kept, crossed, gain_part), "last")
    far, near, other = other_y(dh, 2), other_y(dh, 1), other_y(dh, 3)
    gain_part = add_from(gain_part, other_column)
    gain_part = add_from(gain_part, other_high)
    dhs = [dh, near, far, other]
    section_out = put_out(0, section_map, own_out, got_out, [enc_out], "rows")
    section_grad = put_out(F, section_map, own_out, got_out, dhs, "grads")
    return (section_out[None], section_grad[None], gain_part.reshape(D))


def solution(mesh):
    return jax.shard_map(
        on_device,
        mesh=mesh,
        in_specs=(
            P("section", "dp", None),
            P("section", "dp", None),
            P("section", "dp", None),
            P(),
            P(),
        ),
        out_specs=(P("section", "dp", None), P("section", "dp", None), P()),
        check_vma=False,
    )
```

```python
import functools
import math

import jax
import jax.numpy as jnp
from jax import lax
from jax.experimental import pallas as pl
from jax.experimental.pallas import tpu as pltpu
from jax.sharding import PartitionSpec as P

HEAD = 256
LEN = 256
D = 2048
HALF = 4
F = HALF * HEAD
QUARTER = LEN // 4
PIECE = LEN // 2

eps = 1e-06
bf16 = jnp.bfloat16
f32 = jnp.float32

SLOTS = (
    (0, 0), (0, 1), (0, -1), (1, 0), (0, 2), (0, -2), (1, 1), (0, 3),
    (0, -3), (1, -2), (0, 4), (1, 2), (1, -3), (1, 3), (1, -1), (1, 4),
)
N_SLOT = len(SLOTS)
SLOT = D // N_SLOT

ANY = pl.BlockSpec(memory_space=pl.ANY)
VMEM = pl.BlockSpec(memory_space=pltpu.VMEM)
SMEM = pl.BlockSpec(memory_space=pltpu.SMEM)
MIB = 1024 * 1024


def dp_swap(x, move):
    pairs = []
    for index in range(32):
        column, place, core = index // 16, (index // 2) % 8, index % 2
        column, place, core = move(column, place, core)
        pairs.append((index, (column % 2) * 16 + (place % 8) * 2 + core % 2))
    return lax.ppermute(x, "dp", pairs)


def section_swap(x, move):
    pairs = []
    for index in range(8):
        high, y = move(index // 4, index % 4)
        pairs.append((index, (high % 2) * 4 + y % 4))
    return lax.ppermute(x, "section", pairs)


def other_core(x):
    return dp_swap(x, lambda c, z, k: (c, z, k + 1))


def other_column(x):
    return dp_swap(x, lambda c, z, k: (c + 1, z, k))


def from_above(x):
    return dp_swap(x, lambda c, z, k: (c, z - 1, k))


def from_below(x):
    return dp_swap(x, lambda c, z, k: (c, z + 1, k))


def other_high(x):
    return section_swap(x, lambda h, y: (h + 1, y))


def other_y(x, bits):
    return section_swap(x, lambda h, y: (h, y ^ bits))


def join_kernel(*refs):
    del refs


class Order:
    def __init__(self, token):
        self.token = token

    def take(self, *arrays):
        arrays = arrays + (self.token,)
        count = len(arrays)
        *arrays, self.token = pl.pallas_call(
            join_kernel,
            in_specs=[ANY] * count,
            out_specs=[ANY] * count,
            out_shape=[jax.ShapeDtypeStruct(x.shape, x.dtype) for x in arrays],
            input_output_aliases={i: i for i in range(count)},
            compiler_params=pltpu.CompilerParams(vmem_limit_bytes=MIB),
            cost_estimate=pl.CostEstimate(flops=0, bytes_accessed=1024, transcendentals=0),
            name="join",
        )(*arrays)
        return arrays[0] if count == 2 else arrays


def core_index():
    return lax.axis_index("dp") % 2


def y_index():
    return lax.axis_index("section") % 4


def root_of(map_ref):
    root = jnp.int32(0)
    for index in range(8):
        root = jnp.where(map_ref[index] == 0, index, root)
    return root


def is_encoder(map_ref):
    return root_of(map_ref) == lax.axis_index("section")


def row_block(index, size):
    return pl.ds(pl.multiple_of(index * size, size), size)


def copy_all(pairs, sems):
    copies = [pltpu.make_async_copy(source, target, sems.at[i]) for i, (source, target) in enumerate(pairs)]
    for copy in copies:
        copy.start()
    for copy in copies:
        copy.wait()


def columns_kernel(w_ref, keep_ref, give_ref, token_ref, sems):
    core = core_index()
    token_ref[...] = jnp.zeros_like(token_ref)
    copy_all([
        (w_ref.at[:, row_block(side * 2 + which, F)], ref.at[:, pl.ds(side * F, F)])
        for ref, which in ((give_ref, 1 - core), (keep_ref, core))
        for side in range(2)
    ], sems)


def unit_kernel(keep_ref, got_ref, unit_ref, sems):
    core = core_index()
    copy_all([
        (keep_ref, unit_ref.at[row_block(core, SLOT // 2), :]),
        (got_ref, unit_ref.at[row_block(1 - core, SLOT // 2), :]),
    ], sems)


def half_kernel(rows_ref, half_ref, sems):
    copy_all([(rows_ref.at[row_block((y_index() // 2) ^ 1, 2 * QUARTER), :], half_ref)], sems)


def give_kernel(rows_ref, cot_ref, token_ref, give_ref, sems):
    del token_ref
    cols = row_block(1 - core_index(), F)
    copy_all([
        (rows_ref.at[:, cols], give_ref.at[:, pl.ds(0, F)]),
        (cot_ref.at[:, cols], give_ref.at[:, pl.ds(F, F)]),
    ], sems)


def butterfly_kernel(a_ref, b_ref, c_ref, d_ref, out_ref):
    out_ref[...] = (a_ref[...] + b_ref[...]) + (c_ref[...] + d_ref[...])


def select_kernel(step, map_ref, own_ref, got_ref, *outs):
    y, root = y_index(), root_of(map_ref)
    if step == 0:
        mine = y // 2 == root % 4 // 2
        keep_ref, send_ref = outs
        for ref, quarter in ((keep_ref, y), (send_ref, y ^ 1)):
            ref[...] = jnp.where(mine, own_ref[row_block(quarter, QUARTER), :], got_ref[row_block(quarter % 2, QUARTER), :])
    elif step == 1:
        outs[0][...] = jnp.where(y % 2 == root % 2, own_ref[...], got_ref[...])
    else:
        outs[0][...] = jnp.where(lax.axis_index("section") // 4 == root // 4, own_ref[...], got_ref[...])


def stack_kernel(*refs):
    *parts, out_ref = refs
    rows = out_ref.shape[0] // len(parts)
    for index, part in enumerate(parts):
        out_ref[index * rows:(index + 1) * rows, :] = part[...]


def add_after_kernel(a_ref, b_ref, done_ref, out_ref):
    del done_ref
    out_ref[...] = a_ref[...] + b_ref[...]


def late_kernel(a_ref, token_ref, out_ref):
    del token_ref
    out_ref[...] = a_ref[...]


def add_kernel(a_ref, b_ref, out_ref):
    out_ref[...] = a_ref[...] + b_ref[...]


def slot_column(column, offset):
    dp = lax.axis_index("dp")
    column = (dp // 16 + column) % 2
    place = ((dp // 2) % 8 + offset + 8) % 8
    return pl.multiple_of((column * 8 + place) * SLOT, SLOT)


def norm_block(ref, gain_ref, enc_ref, inv_ref):
    @pl.loop(0, PIECE // QUARTER)
    def _(block):
        rows = row_block(block, QUARTER)
        hidden = ref[rows, :].astype(f32)
        inv = lax.rsqrt(jnp.mean(hidden * hidden, axis=1, keepdims=True) + eps)
        inv_ref[rows, :] = jnp.broadcast_to(inv, (QUARTER, 128))
        for slot in range(N_SLOT):
            cols = pl.ds(slot_column(*SLOTS[slot]), SLOT)
            part = ref[rows, cols].astype(f32)
            enc_ref[rows, slot * SLOT:(slot + 1) * SLOT] = (part * inv * gain_ref[:, cols]).astype(bf16)


def norm_kernel(gain_ref, *refs):
    count = len(refs) // 3
    for index in range(count):
        norm_block(refs[index], gain_ref, refs[count + 2 * index], refs[count + 2 * index + 1])


def encoder_kernel(map_ref, gain_ref, cot_ref, a_ref, b_ref, dh_ref, gp_ref, full_ref):
    @pl.when(is_encoder(map_ref))
    def _():
        y = y_index()
        gain = gain_ref[...]
        gp_ref[...] = jnp.zeros_like(gp_ref)
        for index, ref in enumerate((a_ref, b_ref)):

            @pl.loop(0, PIECE // QUARTER)
            def _(block):
                quarter = index * (PIECE // QUARTER) + block
                rows = row_block(quarter, QUARTER)
                place = row_block(y ^ quarter, QUARTER)
                g = cot_ref[place, :].astype(f32)
                hidden = ref[row_block(block, QUARTER), :].astype(f32)
                inv = lax.rsqrt(jnp.mean(hidden * hidden, axis=1, keepdims=True) + eps)
                full_ref[place, :] = (hidden * inv * gain).astype(bf16)
                mean = jnp.mean(hidden * gain * g, axis=1, keepdims=True)
                dh_ref[rows, :] = (inv * gain * g - hidden * (inv * inv * inv * mean)).astype(bf16)
                gp_ref[...] += jnp.sum(g * hidden * inv, axis=0, keepdims=True)


NT = (((1,), (1,)), ((), ()))
TN = (((0,), (0,)), ((), ()))
SCALE = 1.0 / math.sqrt(HEAD)


def main_kernel(*refs):
    units = refs[:N_SLOT]
    encs, hids, invs = refs[N_SLOT:N_SLOT + 4], refs[N_SLOT + 4:N_SLOT + 8], refs[N_SLOT + 8:N_SLOT + 12]
    (map_ref, rows_ref, cot_ref, qg_oth, gain_ref, dh_enc, gp_enc,
     own_out, oth_out, dh_own, dh_oth, gp_ref, dkv, mean_ref) = refs[N_SLOT + 12:]
    mean_ref[...] = jnp.zeros_like(mean_ref)

    @pl.loop(0, HALF)
    def _(head):
        cols, vcols = row_block(head, HEAD), row_block(HALF + head, HEAD)
        mine = row_block(core_index() * HALF + head, HEAD)
        both = []
        for at in (cols, vcols):
            w = jnp.concatenate([unit[:, at] for unit in units], axis=0)
            enc = jnp.concatenate([ref[...] for ref in encs], axis=0)
            both.append(jnp.dot(enc, w, preferred_element_type=f32).astype(bf16))
        rows = (slice(0, LEN), slice(LEN, 2 * LEN))
        k = [both[0][at] for at in rows]
        v = [both[1][at] for at in rows]
        q = (rows_ref[:, mine], qg_oth[:, cols])
        g = (cot_ref[:, mine], qg_oth[:, vcols])
        two = range(2)
        scores = [lax.dot_general(k[i], q[i], NT, preferred_element_type=f32) * SCALE for i in two]
        dprobs = [lax.dot_general(v[i], g[i], NT, preferred_element_type=f32) for i in two]
        e = [jnp.exp(x - jnp.max(x, axis=0, keepdims=True)) for x in scores]
        probs = [x * (1.0 / jnp.sum(x, axis=0, keepdims=True)) for x in e]
        rounded = [x.astype(bf16) for x in probs]
        delta = [jnp.sum(rounded[i].astype(f32) * dprobs[i], axis=0, keepdims=True) for i in two]
        dscores = [(probs[i] * (dprobs[i] - delta[i])).astype(bf16) for i in two]
        context = [lax.dot_general(rounded[i], v[i], TN, preferred_element_type=f32) for i in two]
        dv = [jnp.dot(rounded[i], g[i], preferred_element_type=f32).astype(bf16) for i in two]
        dk = [(jnp.dot(dscores[i], q[i], preferred_element_type=f32) * SCALE).astype(bf16) for i in two]
        dq = [lax.dot_general(dscores[i], k[i], TN, preferred_element_type=f32) * SCALE for i in two]
        for i, out in enumerate((own_out, oth_out)):
            out[:, cols] = context[i].astype(bf16)
            out[:, vcols] = dq[i].astype(bf16)
            dkv[rows[i], cols] = dk[i]
            dkv[rows[i], vcols] = dv[i]
            term = dk[i].astype(f32) * k[i].astype(f32) + dv[i].astype(f32) * v[i].astype(f32)
            mean_ref[rows[i], :] += term[:, :128] + term[:, 128:]

    inv = jnp.concatenate([ref[:, :1] for ref in invs], axis=0)
    factor = inv * inv * (jnp.sum(mean_ref[...], axis=1, keepdims=True) * (1.0 / D))

    @pl.when(jnp.logical_not(is_encoder(map_ref)))
    def _():
        for block in range(N_SLOT // 2):
            w = jnp.concatenate([units[2 * block][...], units[2 * block + 1][...]], axis=0)
            denc = lax.dot_general(dkv[...], w, NT, preferred_element_type=f32)
            for side in range(2):
                cols = pl.ds(slot_column(*SLOTS[2 * block + side]), SLOT)
                total = jnp.zeros((1, SLOT), f32)
                for index, hid in enumerate(hids):
                    rows = slice(index * PIECE, (index + 1) * PIECE)
                    at = slice(index % 2 * PIECE, (index % 2 + 1) * PIECE)
                    out = (dh_own, dh_oth)[index // 2]
                    hidden = hid[:, cols].astype(f32)
                    scaled = inv[rows] * denc[rows, side * SLOT:(side + 1) * SLOT]
                    out[at, cols] = (gain_ref[:, cols] * scaled - hidden * factor[rows]).astype(bf16)
                    total = total + jnp.sum(scaled * hidden, axis=0, keepdims=True)
                gp_ref[:, cols] = total

    @pl.when(is_encoder(map_ref))
    def _():
        dh_oth[...] = jnp.zeros_like(dh_oth)
        dh_own[...] = dh_enc[...]
        gp_ref[...] = gp_enc[...]

    dh_oth[LEN:, :] = two_rows(gp_ref[...])


def two_rows(x):
    high = x.astype(bf16).astype(f32)
    index = lax.broadcasted_iota(jnp.int32, (16, x.shape[1]), 0)
    rows = jnp.where(index == 0, high, jnp.where(index == 1, x - high, 0.0))
    return rows.astype(bf16)


def one_row(rows):
    return rows[0:1, :].astype(f32) + rows[1:2, :].astype(f32)


def attend(units, pieces, where, *args):
    whole = jax.ShapeDtypeStruct((LEN, D), bf16)
    return pl.pallas_call(
        main_kernel,
        in_specs=[VMEM] * (N_SLOT + 12) + [SMEM] + [VMEM] * 6,
        out_specs=[VMEM] * 5,
        out_shape=[
            whole, whole, whole, jax.ShapeDtypeStruct((LEN + 16, D), bf16), jax.ShapeDtypeStruct((1, D), f32)
        ],
        scratch_shapes=[
            pltpu.VMEM((2 * LEN, 2 * F), bf16),
            pltpu.VMEM((2 * LEN, 128), f32),
        ],
        compiler_params=pltpu.CompilerParams(vmem_limit_bytes=16 * MIB),
        cost_estimate=pl.CostEstimate(flops=10_000_000_000, bytes_accessed=20_000_000, transcendentals=600_000),
        name="attend",
    )(*units, *pieces, where, *args)


def small_call(kernel, out_shape, args, name, limit=6, where=None):
    first = () if where is None else (where,)
    return pl.pallas_call(
        kernel,
        in_specs=[SMEM] * len(first) + [VMEM] * len(args),
        out_specs=jax.tree.map(lambda _: VMEM, out_shape),
        out_shape=out_shape,
        compiler_params=pltpu.CompilerParams(vmem_limit_bytes=limit * MIB),
        cost_estimate=pl.CostEstimate(flops=0, bytes_accessed=1024, transcendentals=0),
        name=name,
    )(*first, *args)


def copy_call(kernel, out_shape, args, name, count):
    return pl.pallas_call(
        kernel,
        in_specs=[ANY] * len(args),
        out_specs=jax.tree.map(lambda x: VMEM if x.dtype == f32 else ANY, out_shape),
        out_shape=out_shape,
        scratch_shapes=[pltpu.SemaphoreType.DMA((count,))],
        compiler_params=pltpu.CompilerParams(vmem_limit_bytes=MIB),
        cost_estimate=pl.CostEstimate(flops=0, bytes_accessed=1024, transcendentals=0),
        name=name,
    )(*args)


def add_after(a, b, done):
    return pl.pallas_call(
        add_after_kernel,
        in_specs=[VMEM, VMEM, ANY],
        out_specs=VMEM,
        out_shape=jax.ShapeDtypeStruct(a.shape, a.dtype),
        compiler_params=pltpu.CompilerParams(vmem_limit_bytes=MIB),
        cost_estimate=pl.CostEstimate(flops=0, bytes_accessed=1024, transcendentals=0),
        name="add",
    )(a, b, done)


def bf16_rows(rows):
    return jax.ShapeDtypeStruct((rows, D), bf16)


ROWS32 = jax.ShapeDtypeStruct((QUARTER, D), f32)
LINE = jax.ShapeDtypeStruct((1, D), f32)


def split_kernel(own_ref, gp_ref, got_ref, kept_ref, gain_ref, *sent):
    gain_ref[...] = one_row(two_rows(gp_ref[...])) + one_row(got_ref[LEN:, :])
    for step in range(4):
        at = slice(step * QUARTER, (step + 1) * QUARTER)
        part = own_ref[at, :].astype(f32) + got_ref[at, :].astype(f32)
        if step == 0:
            kept_ref[...] = part
        else:
            sent[step - 1][...] = part.astype(bf16)


def sum_kernel(kept_ref, gain_ref, a_ref, b_ref, c_ref, sum_ref, sent_ref, gain_out):
    total = kept_ref[...] + (a_ref[...].astype(f32) + b_ref[...].astype(f32) + c_ref[...].astype(f32))
    sum_ref[...] = total
    sent_ref[...] = total.astype(bf16)
    gain_out[...] = gain_ref[...]


def last_kernel(sum_ref, got_ref, gain_ref, dh_ref, gain_out):
    gain_out[...] = gain_ref[...]
    dh_ref[...] = (sum_ref[...] + got_ref[...].astype(f32)).astype(bf16)


def out_kernel(offset, map_ref, own_ref, oth_ref, *refs):
    *parts, out_ref, sems = refs
    core, y = core_index(), y_index()
    rows = LEN // len(parts)

    @pl.when(jnp.logical_not(is_encoder(map_ref)))
    def _():
        copies = [
            pltpu.make_async_copy(
                ref.at[:, pl.ds(offset, F)],
                out_ref.at[:, pl.ds(pl.multiple_of(place * F, F), F)],
                sems.at[index],
            )
            for index, (ref, place) in enumerate(((own_ref, core), (oth_ref, 1 - core)))
        ]
        for copy in copies:
            copy.start()
        for copy in copies:
            copy.wait()

    @pl.when(is_encoder(map_ref))
    def _():
        copies = []
        for index, part in enumerate(parts):
            start = 0 if len(parts) == 1 else pl.multiple_of((y ^ index) * rows, rows)
            copies.append(
                pltpu.make_async_copy(part, out_ref.at[pl.ds(start, rows), :], sems.at[index])
            )
        for copy in copies:
            copy.start()
        for copy in copies:
            copy.wait()


def put_out(offset, where, own, oth, parts, name):
    return pl.pallas_call(
        functools.partial(out_kernel, offset),
        in_specs=[SMEM] + [ANY] * (2 + len(parts)),
        out_specs=ANY,
        out_shape=jax.ShapeDtypeStruct((LEN, D), bf16),
        scratch_shapes=[pltpu.SemaphoreType.DMA((4,))],
        compiler_params=pltpu.CompilerParams(vmem_limit_bytes=MIB),
        cost_estimate=pl.CostEstimate(flops=0, bytes_accessed=2_000_000, transcendentals=0),
        name=name,
    )(where, own, oth, *parts)


def on_device(section_rows, kv_weight, cotangent, gain, section_map):
    rows, cot, weight, gain = section_rows[0], cotangent[0], kv_weight[0], gain[None]
    quarter = bf16_rows(QUARTER)

    def select(step, own, got):
        outs = [quarter, quarter] if step == 0 else quarter
        kernel = functools.partial(select_kernel, step)
        return small_call(kernel, outs, (own, got), "select", limit=3, where=section_map)

    keep, give, token = copy_call(
        columns_kernel,
        [bf16_rows(SLOT // 2), bf16_rows(SLOT // 2), jax.ShapeDtypeStruct((8, 128), f32)],
        (weight,), "columns", 4,
    )
    order = Order(token)
    got = other_core(give)
    hidden = other_y(copy_call(half_kernel, bf16_rows(2 * QUARTER), (rows,), "half", 1), 2)
    a, b = {0: copy_call(unit_kernel, bf16_rows(SLOT), (keep, got), "unit", 2)}, {}
    up, down, across = from_above(a[0]), from_below(a[0]), other_column(a[0])
    qg_oth = other_core(copy_call(give_kernel, bf16_rows(LEN), (rows, cot, a[0]), "give", 2))

    a[1], qg_oth = order.take(up, qg_oth)
    up, across_1 = from_above(a[1]), other_column(a[1])
    a[-1] = order.take(down)
    down = from_below(a[-1])
    hidden = order.take(hidden)
    mine, send = select(0, rows, hidden)
    hidden = other_y(send, 1)
    b[0] = order.take(across)
    hidden = order.take(hidden)
    mine = select(1, mine, hidden)
    hidden = other_high(mine)

    a[2] = order.take(up)
    up = from_above(a[2])
    a[-2] = order.take(down)
    down, across_2 = from_below(a[-2]), other_column(a[-2])
    b[1] = order.take(across_1)
    hidden = order.take(hidden)
    mine = select(2, mine, hidden)
    hidden = other_y(mine, 1)

    a[3] = order.take(up)
    up = from_above(b[1])
    a[-3] = order.take(down)
    down, across_3 = from_below(a[-3]), other_column(a[-3])
    b[-2] = order.take(across_2)
    hidden = order.take(hidden)
    own_a = small_call(stack_kernel, bf16_rows(PIECE), (mine, hidden), "stack", limit=3)
    hidden = other_y(own_a, 2)

    a[4] = order.take(down)
    down, across_4 = from_below(b[0]), other_column(a[4])
    b[2] = order.take(up)
    up = from_above(b[2])
    b[-3] = order.take(across_3)
    own_b = order.take(hidden)
    late_a = small_call(late_kernel, bf16_rows(PIECE), (own_a, order.token), "late", limit=3)
    oth_a, oth_b = other_core(late_a), other_core(own_b)
    b[3] = order.take(up)
    b[-1] = order.take(down)
    b[4] = order.take(across_4)
    oth_a, oth_b = order.take(oth_a, oth_b)
    units = [(a, b)[column][offset] for column, offset in SLOTS]

    def normalise(*pieces):
        outs = [bf16_rows(PIECE), jax.ShapeDtypeStruct((PIECE, 128), f32)] * len(pieces)
        return small_call(norm_kernel, outs, (gain, *pieces), "norm")

    enc_0, inv_0, enc_1, inv_1 = normalise(own_a, own_b)
    enc_2, inv_2, enc_3, inv_3 = normalise(oth_a, oth_b)
    dh_enc, gp_enc, enc_out = small_call(
        encoder_kernel, [bf16_rows(LEN), LINE, bf16_rows(LEN)], (gain, cot, own_a, own_b), "encoder",
        where=section_map,
    )
    pieces = (enc_0, enc_1, enc_2, enc_3, own_a, own_b, oth_a, oth_b, inv_0, inv_1, inv_2, inv_3)
    own_out, oth_out, dh_own, dh_oth, gp = attend(
        units, pieces, section_map, rows, cot, qg_oth, gain, dh_enc, gp_enc
    )

    def add_from(part, *moves):
        for move in moves:
            part = small_call(add_kernel, LINE, (part, move(part)), "add", limit=1)
        return part

    def butterfly(part, *moves):
        return small_call(butterfly_kernel, LINE, (part, *[move(part) for move in moves]), "add", limit=1)

    def z_move(bits):
        return lambda v: dp_swap(v, lambda c, z, k: (c, z ^ bits, k))

    kept, gain_part, *parts = small_call(
        split_kernel, [ROWS32, LINE, quarter, quarter, quarter], (dh_own, gp, other_core(dh_oth)), "split"
    )
    far, near, other = other_y(parts[1], 2), other_y(parts[0], 1), other_y(parts[2], 3)
    gain_part, got_out = order.take(gain_part, other_core(oth_out))
    gain_part = butterfly(gain_part, *[z_move(bits) for bits in (1, 2, 3)])
    section_out = put_out(0, section_map, own_out, got_out, [enc_out], "rows")
    gain_part = add_after(gain_part, z_move(4)(gain_part), section_out)
    near, far, other, gain_part = order.take(near, far, other, gain_part)
    kept, sent, gain_part = small_call(
        sum_kernel, [ROWS32, quarter, LINE], (kept, gain_part, near, far, other), "sum"
    )
    crossed = other_high(sent)
    gain_part = butterfly(gain_part, *[lambda v, bits=bits: other_y(v, bits) for bits in (1, 2, 3)])
    dh, gain_part = small_call(last_kernel, [quarter, LINE], (kept, crossed, gain_part), "last")
    far, near, other = other_y(dh, 2), other_y(dh, 1), other_y(dh, 3)
    gain_part = add_from(gain_part, other_column)
    gain_part = add_from(gain_part, other_high)
    dhs = [dh, near, far, other]
    section_grad = put_out(F, section_map, own_out, got_out, dhs, "grads")
    return (section_out[None], section_grad[None], gain_part.reshape(D))


def solution(mesh):
    return jax.shard_map(
        on_device,
        mesh=mesh,
        in_specs=(
            P("section", "dp", None),
            P("section", "dp", None),
            P("section", "dp", None),
            P(),
            P(),
        ),
        out_specs=(P("section", "dp", None), P("section", "dp", None), P()),
        check_vma=False,
    )
```

```python
import functools
import math

import jax
import jax.numpy as jnp
from jax import lax
from jax.experimental import pallas as pl
from jax.experimental.pallas import tpu as pltpu
from jax.sharding import PartitionSpec as P

HEAD = 256
LEN = 256
D = 2048
HALF = 4
F = HALF * HEAD
QUARTER = LEN // 4
PIECE = LEN // 2
NORM = 32

eps = 1e-06
bf16 = jnp.bfloat16
f32 = jnp.float32

SLOTS = (
    (0, 0), (0, 1), (0, -1), (1, 0), (0, 2), (0, -2), (1, 1), (0, 3),
    (0, -3), (1, -2), (0, 4), (1, 2), (1, -3), (1, 3), (1, -1), (1, 4),
)
N_SLOT = len(SLOTS)
SLOT = D // N_SLOT

ANY = pl.BlockSpec(memory_space=pl.ANY)
VMEM = pl.BlockSpec(memory_space=pltpu.VMEM)
SMEM = pl.BlockSpec(memory_space=pltpu.SMEM)
MIB = 1024 * 1024


def dp_swap(x, move):
    pairs = []
    for index in range(32):
        column, place, core = index // 16, (index // 2) % 8, index % 2
        column, place, core = move(column, place, core)
        pairs.append((index, (column % 2) * 16 + (place % 8) * 2 + core % 2))
    return lax.ppermute(x, "dp", pairs)


def section_swap(x, move):
    pairs = []
    for index in range(8):
        high, y = move(index // 4, index % 4)
        pairs.append((index, (high % 2) * 4 + y % 4))
    return lax.ppermute(x, "section", pairs)


def other_core(x):
    return dp_swap(x, lambda c, z, k: (c, z, k + 1))


def other_column(x):
    return dp_swap(x, lambda c, z, k: (c + 1, z, k))


def from_above(x):
    return dp_swap(x, lambda c, z, k: (c, z - 1, k))


def from_below(x):
    return dp_swap(x, lambda c, z, k: (c, z + 1, k))


def other_high(x):
    return section_swap(x, lambda h, y: (h + 1, y))


def other_y(x, bits):
    return section_swap(x, lambda h, y: (h, y ^ bits))


def join_kernel(*refs):
    del refs


class Order:
    def __init__(self, token):
        self.token = token

    def take(self, *arrays):
        arrays = arrays + (self.token,)
        count = len(arrays)
        *arrays, self.token = pl.pallas_call(
            join_kernel,
            in_specs=[ANY] * count,
            out_specs=[ANY] * count,
            out_shape=[jax.ShapeDtypeStruct(x.shape, x.dtype) for x in arrays],
            input_output_aliases={i: i for i in range(count)},
            compiler_params=pltpu.CompilerParams(vmem_limit_bytes=MIB),
            cost_estimate=pl.CostEstimate(flops=0, bytes_accessed=1024, transcendentals=0),
            name="join",
        )(*arrays)
        return arrays[0] if count == 2 else arrays


def core_index():
    return lax.axis_index("dp") % 2


def y_index():
    return lax.axis_index("section") % 4


def root_of(map_ref):
    root = jnp.int32(0)
    for index in range(8):
        root = jnp.where(map_ref[index] == 0, index, root)
    return root


def is_encoder(map_ref):
    return root_of(map_ref) == lax.axis_index("section")


def row_block(index, size):
    return pl.ds(pl.multiple_of(index * size, size), size)


def copy_all(pairs, sems):
    copies = [pltpu.make_async_copy(source, target, sems.at[i]) for i, (source, target) in enumerate(pairs)]
    for copy in copies:
        copy.start()
    for copy in copies:
        copy.wait()


def columns_kernel(w_ref, keep_ref, give_ref, token_ref, sems):
    core = core_index()
    token_ref[...] = jnp.zeros_like(token_ref)
    copy_all([
        (w_ref.at[:, row_block(side * 2 + which, F)], ref.at[:, pl.ds(side * F, F)])
        for ref, which in ((give_ref, 1 - core), (keep_ref, core))
        for side in range(2)
    ], sems)


def unit_kernel(keep_ref, got_ref, unit_ref, sems):
    core = core_index()
    copy_all([
        (keep_ref, unit_ref.at[row_block(core, SLOT // 2), :]),
        (got_ref, unit_ref.at[row_block(1 - core, SLOT // 2), :]),
    ], sems)


def half_kernel(rows_ref, half_ref, sems):
    copy_all([(rows_ref.at[row_block((y_index() // 2) ^ 1, 2 * QUARTER), :], half_ref)], sems)


def give_kernel(rows_ref, cot_ref, token_ref, give_ref, sems):
    del token_ref
    cols = row_block(1 - core_index(), F)
    copy_all([
        (rows_ref.at[:, cols], give_ref.at[:, pl.ds(0, F)]),
        (cot_ref.at[:, cols], give_ref.at[:, pl.ds(F, F)]),
    ], sems)


def butterfly_kernel(*refs):
    *parts, out_ref = refs
    parts = [ref[...] for ref in parts]
    while len(parts) > 1:
        parts = [parts[i] + parts[i + 1] for i in range(0, len(parts), 2)]
    out_ref[...] = parts[0]


def select_kernel(step, map_ref, own_ref, got_ref, *outs):
    y, root = y_index(), root_of(map_ref)
    if step == 0:
        mine = y // 2 == root % 4 // 2
        keep_ref, send_ref = outs
        for ref, quarter in ((keep_ref, y), (send_ref, y ^ 1)):
            ref[...] = jnp.where(mine, own_ref[row_block(quarter, QUARTER), :], got_ref[row_block(quarter % 2, QUARTER), :])
    elif step == 1:
        outs[0][...] = jnp.where(y % 2 == root % 2, own_ref[...], got_ref[...])
    else:
        outs[0][...] = jnp.where(lax.axis_index("section") // 4 == root // 4, own_ref[...], got_ref[...])


def stack_kernel(*refs):
    *parts, out_ref = refs
    rows = out_ref.shape[0] // len(parts)
    for index, part in enumerate(parts):
        out_ref[index * rows:(index + 1) * rows, :] = part[...]


def late_kernel(a_ref, token_ref, out_ref):
    del token_ref
    out_ref[...] = a_ref[...]


def butterfly_kernel(*refs):
    *parts, out_ref = refs
    parts = [ref[...] for ref in parts]
    while len(parts) > 1:
        parts = [parts[i] + parts[i + 1] for i in range(0, len(parts), 2)]
    out_ref[...] = parts[0]


def select_kernel(step, map_ref, own_ref, got_ref, *outs):
    y, root = y_index(), root_of(map_ref)
    if step == 0:
        mine = y // 2 == root % 4 // 2
        keep_ref, send_ref = outs
        for ref, quarter in ((keep_ref, y), (send_ref, y ^ 1)):
            ref[...] = jnp.where(mine, own_ref[row_block(quarter, QUARTER), :], got_ref[row_block(quarter % 2, QUARTER), :])
    elif step == 1:
        outs[0][...] = jnp.where(y % 2 == root % 2, own_ref[...], got_ref[...])
    else:
        outs[0][...] = jnp.where(lax.axis_index("section") // 4 == root // 4, own_ref[...], got_ref[...])


def stack_kernel(*refs):
    *parts, out_ref = refs
    rows = out_ref.shape[0] // len(parts)
    for index, part in enumerate(parts):
        out_ref[index * rows:(index + 1) * rows, :] = part[...]


def late_kernel(a_ref, token_ref, out_ref):
    del token_ref
    out_ref[...] = a_ref[...]


def add_kernel(a_ref, b_ref, out_ref):
    out_ref[...] = a_ref[...] + b_ref[...]


def slot_column(column, offset):
    dp = lax.axis_index("dp")
    column = (dp // 16 + column) % 2
    place = ((dp // 2) % 8 + offset + 8) % 8
    return pl.multiple_of((column * 8 + place) * SLOT, SLOT)


def norm_block(ref, gain_ref, enc_ref, inv_ref):
    @pl.loop(0, PIECE // NORM)
    def _(block):
        rows = row_block(block, NORM)
        hidden = ref[rows, :].astype(f32)
        inv = lax.rsqrt(jnp.mean(hidden * hidden, axis=1, keepdims=True) + eps)
        inv_ref[rows, :] = jnp.broadcast_to(inv, (NORM, 128))
        for slot in range(N_SLOT):
            cols = pl.ds(slot_column(*SLOTS[slot]), SLOT)
            part = ref[rows, cols].astype(f32)
            enc_ref[rows, slot * SLOT:(slot + 1) * SLOT] = (part * inv * gain_ref[:, cols]).astype(bf16)


def norm_kernel(gain_ref, *refs):
    count = len(refs) // 3
    for index in range(count):
        norm_block(refs[index], gain_ref, refs[count + 2 * index], refs[count + 2 * index + 1])


def encoder_kernel(map_ref, gain_ref, cot_ref, a_ref, b_ref, dh_ref, gp_ref, full_ref, flag_ref):
    flag_ref[...] = jnp.where(is_encoder(map_ref), 1.0, 0.0) * jnp.ones_like(flag_ref)

    @pl.when(is_encoder(map_ref))
    def _():
        y = y_index()
        gain = gain_ref[...]
        gp_ref[...] = jnp.zeros_like(gp_ref)
        for index, ref in enumerate((a_ref, b_ref)):

            @pl.loop(0, PIECE // NORM)
            def _(block):
                part = QUARTER // NORM
                quarter = index * (PIECE // QUARTER) + block // part
                rows = row_block(index * (PIECE // NORM) + block, NORM)
                place = row_block((y ^ quarter) * part + block % part, NORM)
                g = cot_ref[place, :].astype(f32)
                hidden = ref[row_block(block, NORM), :].astype(f32)
                inv = lax.rsqrt(jnp.mean(hidden * hidden, axis=1, keepdims=True) + eps)
                full_ref[place, :] = (hidden * inv * gain).astype(bf16)
                mean = jnp.mean(hidden * gain * g, axis=1, keepdims=True)
                dh_ref[rows, :] = (inv * gain * g - hidden * (inv * inv * inv * mean)).astype(bf16)
                gp_ref[...] += jnp.sum(g * hidden * inv, axis=0, keepdims=True)


NT = (((1,), (1,)), ((), ()))
TN = (((0,), (0,)), ((), ()))
SCALE = 1.0 / math.sqrt(HEAD)


def main_kernel(*refs):
    units = refs[:N_SLOT]
    encs, hids, invs = refs[N_SLOT:N_SLOT + 4], refs[N_SLOT + 4:N_SLOT + 8], refs[N_SLOT + 8:N_SLOT + 12]
    (map_ref, rows_ref, cot_ref, qg_oth, gain_ref, dh_enc, gp_enc,
     own_out, oth_out, dh_own, dh_oth, gp_ref, dkv, mean_ref) = refs[N_SLOT + 12:]
    mean_ref[...] = jnp.zeros_like(mean_ref)

    @pl.loop(0, HALF)
    def _(head):
        cols, vcols = row_block(head, HEAD), row_block(HALF + head, HEAD)
        mine = row_block(core_index() * HALF + head, HEAD)
        both = []
        for at in (cols, vcols):
            w = jnp.concatenate([unit[:, at] for unit in units], axis=0)
            enc = jnp.concatenate([ref[...] for ref in encs], axis=0)
            both.append(jnp.dot(enc, w, preferred_element_type=f32).astype(bf16))
        rows = (slice(0, LEN), slice(LEN, 2 * LEN))
        k = [both[0][at] for at in rows]
        v = [both[1][at] for at in rows]
        q = (rows_ref[:, mine], qg_oth[:, cols])
        g = (cot_ref[:, mine], qg_oth[:, vcols])
        two = range(2)
        scores = [lax.dot_general(k[i], q[i], NT, preferred_element_type=f32) * SCALE for i in two]
        dprobs = [lax.dot_general(v[i], g[i], NT, preferred_element_type=f32) for i in two]
        e = [jnp.exp(x - jnp.max(x, axis=0, keepdims=True)) for x in scores]
        probs = [x * (1.0 / jnp.sum(x, axis=0, keepdims=True)) for x in e]
        rounded = [x.astype(bf16) for x in probs]
        delta = [jnp.sum(rounded[i].astype(f32) * dprobs[i], axis=0, keepdims=True) for i in two]
        dscores = [(probs[i] * (dprobs[i] - delta[i])).astype(bf16) for i in two]
        context = [lax.dot_general(rounded[i], v[i], TN, preferred_element_type=f32) for i in two]
        dv = [jnp.dot(rounded[i], g[i], preferred_element_type=f32).astype(bf16) for i in two]
        dk = [(jnp.dot(dscores[i], q[i], preferred_element_type=f32) * SCALE).astype(bf16) for i in two]
        dq = [lax.dot_general(dscores[i], k[i], TN, preferred_element_type=f32) * SCALE for i in two]
        for i, out in enumerate((own_out, oth_out)):
            out[:, cols] = context[i].astype(bf16)
            out[:, vcols] = dq[i].astype(bf16)
            dkv[rows[i], cols] = dk[i]
            dkv[rows[i], vcols] = dv[i]
            term = dk[i].astype(f32) * k[i].astype(f32) + dv[i].astype(f32) * v[i].astype(f32)
            mean_ref[rows[i], :] += term[:, :128] + term[:, 128:]

    inv = jnp.concatenate([ref[:, :1] for ref in invs], axis=0)
    factor = inv * inv * (jnp.sum(mean_ref[...], axis=1, keepdims=True) * (1.0 / D))

    @pl.when(jnp.logical_not(is_encoder(map_ref)))
    def _():
        for block in range(N_SLOT // 2):
            w = jnp.concatenate([units[2 * block][...], units[2 * block + 1][...]], axis=0)
            denc = lax.dot_general(dkv[...], w, NT, preferred_element_type=f32)
            for side in range(2):
                cols = pl.ds(slot_column(*SLOTS[2 * block + side]), SLOT)
                total = jnp.zeros((1, SLOT), f32)
                for index, hid in enumerate(hids):
                    rows = slice(index * PIECE, (index + 1) * PIECE)
                    at = slice(index % 2 * PIECE, (index % 2 + 1) * PIECE)
                    out = (dh_own, dh_oth)[index // 2]
                    hidden = hid[:, cols].astype(f32)
                    scaled = inv[rows] * denc[rows, side * SLOT:(side + 1) * SLOT]
                    out[at, cols] = (gain_ref[:, cols] * scaled - hidden * factor[rows]).astype(bf16)
                    total = total + jnp.sum(scaled * hidden, axis=0, keepdims=True)
                gp_ref[:, cols] = total

    @pl.when(is_encoder(map_ref))
    def _():
        dh_oth[...] = jnp.zeros_like(dh_oth)
        dh_own[...] = dh_enc[...]
        gp_ref[...] = gp_enc[...]

    dh_oth[LEN:, :] = two_rows(gp_ref[...])


def two_rows(x):
    high = x.astype(bf16).astype(f32)
    index = lax.broadcasted_iota(jnp.int32, (16, x.shape[1]), 0)
    rows = jnp.where(index == 0, high, jnp.where(index == 1, x - high, 0.0))
    return rows.astype(bf16)


def one_row(rows):
    return rows[0:1, :].astype(f32) + rows[1:2, :].astype(f32)


def attend(units, pieces, where, *args):
    whole = jax.ShapeDtypeStruct((LEN, D), bf16)
    return pl.pallas_call(
        main_kernel,
        in_specs=[VMEM] * (N_SLOT + 12) + [SMEM] + [VMEM] * 6,
        out_specs=[VMEM] * 5,
        out_shape=[
            whole, whole, whole, jax.ShapeDtypeStruct((LEN + 16, D), bf16), jax.ShapeDtypeStruct((1, D), f32)
        ],
        scratch_shapes=[
            pltpu.VMEM((2 * LEN, 2 * F), bf16),
            pltpu.VMEM((2 * LEN, 128), f32),
        ],
        compiler_params=pltpu.CompilerParams(vmem_limit_bytes=16 * MIB),
        cost_estimate=pl.CostEstimate(flops=10_000_000_000, bytes_accessed=20_000_000, transcendentals=600_000),
        name="attend",
    )(*units, *pieces, where, *args)


def small_call(kernel, out_shape, args, name, limit=6, where=None):
    first = () if where is None else (where,)
    return pl.pallas_call(
        kernel,
        in_specs=[SMEM] * len(first) + [VMEM] * len(args),
        out_specs=jax.tree.map(lambda _: VMEM, out_shape),
        out_shape=out_shape,
        compiler_params=pltpu.CompilerParams(vmem_limit_bytes=limit * MIB),
        cost_estimate=pl.CostEstimate(flops=0, bytes_accessed=1024, transcendentals=0),
        name=name,
    )(*first, *args)


def copy_call(kernel, out_shape, args, name, count):
    return pl.pallas_call(
        kernel,
        in_specs=[ANY] * len(args),
        out_specs=jax.tree.map(lambda x: VMEM if x.dtype == f32 else ANY, out_shape),
        out_shape=out_shape,
        scratch_shapes=[pltpu.SemaphoreType.DMA((count,))],
        compiler_params=pltpu.CompilerParams(vmem_limit_bytes=MIB),
        cost_estimate=pl.CostEstimate(flops=0, bytes_accessed=1024, transcendentals=0),
        name=name,
    )(*args)


def bf16_rows(rows):
    return jax.ShapeDtypeStruct((rows, D), bf16)


ROWS32 = jax.ShapeDtypeStruct((QUARTER, D), f32)
LINE = jax.ShapeDtypeStruct((1, D), f32)


def split_kernel(own_ref, gp_ref, got_ref, kept_ref, gain_ref, *sent):
    gain_ref[...] = one_row(two_rows(gp_ref[...])) + one_row(got_ref[LEN:, :])
    for step in range(4):
        at = slice(step * QUARTER, (step + 1) * QUARTER)
        part = own_ref[at, :].astype(f32) + got_ref[at, :].astype(f32)
        if step == 0:
            kept_ref[...] = part
        else:
            sent[step - 1][...] = part.astype(bf16)


def sum_kernel(kept_ref, gain_ref, a_ref, b_ref, c_ref, sum_ref, sent_ref, gain_out):
    total = kept_ref[...] + (a_ref[...].astype(f32) + b_ref[...].astype(f32) + c_ref[...].astype(f32))
    sum_ref[...] = total
    sent_ref[...] = total.astype(bf16)
    gain_out[...] = gain_ref[...]


def last_kernel(sum_ref, got_ref, gain_ref, dh_ref, gain_out):
    gain_out[...] = gain_ref[...]
    dh_ref[...] = (sum_ref[...] + got_ref[...].astype(f32)).astype(bf16)


def out_kernel(offset, flag_ref, own_ref, oth_ref, *refs):
    *parts, out_ref, sems = refs
    core, y = core_index(), y_index()
    rows = LEN // len(parts)

    encoder = jnp.max(flag_ref[...]) > 0.5

    @pl.when(jnp.logical_not(encoder))
    def _():
        copies = [
            pltpu.make_async_copy(
                ref.at[:, pl.ds(offset, F)],
                out_ref.at[:, pl.ds(pl.multiple_of(place * F, F), F)],
                sems.at[index],
            )
            for index, (ref, place) in enumerate(((own_ref, core), (oth_ref, 1 - core)))
        ]
        for copy in copies:
            copy.start()
        for copy in copies:
            copy.wait()

    @pl.when(encoder)
    def _():
        copies = []
        for index, part in enumerate(parts):
            start = 0 if len(parts) == 1 else pl.multiple_of((y ^ index) * rows, rows)
            copies.append(
                pltpu.make_async_copy(part, out_ref.at[pl.ds(start, rows), :], sems.at[index])
            )
        for copy in copies:
            copy.start()
        for copy in copies:
            copy.wait()


def put_out(offset, where, own, oth, parts, name):
    return pl.pallas_call(
        functools.partial(out_kernel, offset),
        in_specs=[VMEM] + [ANY] * (2 + len(parts)),
        out_specs=ANY,
        out_shape=jax.ShapeDtypeStruct((LEN, D), bf16),
        scratch_shapes=[pltpu.SemaphoreType.DMA((4,))],
        compiler_params=pltpu.CompilerParams(vmem_limit_bytes=MIB),
        cost_estimate=pl.CostEstimate(flops=0, bytes_accessed=2_000_000, transcendentals=0),
        name=name,
    )(where, own, oth, *parts)


def on_device(section_rows, kv_weight, cotangent, gain, section_map):
    rows, cot, weight, gain = section_rows[0], cotangent[0], kv_weight[0], gain[None]
    quarter = bf16_rows(QUARTER)

    def select(step, own, got):
        outs = [quarter, quarter] if step == 0 else quarter
        kernel = functools.partial(select_kernel, step)
        return small_call(kernel, outs, (own, got), "select", limit=3, where=section_map)

    keep, give, token = copy_call(
        columns_kernel,
        [bf16_rows(SLOT // 2), bf16_rows(SLOT // 2), jax.ShapeDtypeStruct((8, 128), f32)],
        (weight,), "columns", 4,
    )
    order = Order(token)
    got = other_core(give)
    hidden = other_y(copy_call(half_kernel, bf16_rows(2 * QUARTER), (rows,), "half", 1), 2)
    a, b = {0: copy_call(unit_kernel, bf16_rows(SLOT), (keep, got), "unit", 2)}, {}
    up, down, across = from_above(a[0]), from_below(a[0]), other_column(a[0])
    qg_oth = other_core(copy_call(give_kernel, bf16_rows(LEN), (rows, cot, a[0]), "give", 2))

    a[1], qg_oth = order.take(up, qg_oth)
    up, across_1 = from_above(a[1]), other_column(a[1])
    a[-1] = order.take(down)
    down = from_below(a[-1])
    hidden = order.take(hidden)
    mine, send = select(0, rows, hidden)
    hidden = other_y(send, 1)
    b[0] = order.take(across)
    hidden = order.take(hidden)
    mine = select(1, mine, hidden)
    hidden = other_high(mine)

    a[2] = order.take(up)
    up = from_above(a[2])
    a[-2] = order.take(down)
    down, across_2 = from_below(a[-2]), other_column(a[-2])
    b[1] = order.take(across_1)
    hidden = order.take(hidden)
    mine = select(2, mine, hidden)
    hidden = other_y(mine, 1)

    a[3] = order.take(up)
    up = from_above(b[1])
    a[-3] = order.take(down)
    down, across_3 = from_below(a[-3]), other_column(a[-3])
    b[-2] = order.take(across_2)
    hidden = order.take(hidden)
    own_a = small_call(stack_kernel, bf16_rows(PIECE), (mine, hidden), "stack", limit=3)
    hidden = other_y(own_a, 2)

    a[4] = order.take(down)
    down, across_4 = from_below(b[0]), other_column(a[4])
    b[2] = order.take(up)
    up = from_above(b[2])
    b[-3] = order.take(across_3)
    own_b = order.take(hidden)
    late_a = small_call(late_kernel, bf16_rows(PIECE), (own_a, order.token), "late", limit=3)
    oth_a, oth_b = other_core(late_a), other_core(own_b)
    b[3] = order.take(up)
    b[-1] = order.take(down)
    b[4] = order.take(across_4)
    oth_a, oth_b = order.take(oth_a, oth_b)
    units = [(a, b)[column][offset] for column, offset in SLOTS]

    def normalise(*pieces):
        outs = [bf16_rows(PIECE), jax.ShapeDtypeStruct((PIECE, 128), f32)] * len(pieces)
        return small_call(norm_kernel, outs, (gain, *pieces), "norm")

    enc_0, inv_0, enc_1, inv_1 = normalise(own_a, own_b)
    enc_2, inv_2, enc_3, inv_3 = normalise(oth_a, oth_b)
    dh_enc, gp_enc, enc_out, flag = small_call(
        encoder_kernel, [bf16_rows(LEN), LINE, bf16_rows(LEN), jax.ShapeDtypeStruct((8, 128), f32)], (gain, cot, own_a, own_b), "encoder",
        where=section_map,
    )
    pieces = (enc_0, enc_1, enc_2, enc_3, own_a, own_b, oth_a, oth_b, inv_0, inv_1, inv_2, inv_3)
    own_out, oth_out, dh_own, dh_oth, gp = attend(
        units, pieces, section_map, rows, cot, qg_oth, gain, dh_enc, gp_enc
    )

    def butterfly(part, *moves):
        return small_call(butterfly_kernel, LINE, (part, *[move(part) for move in moves]), "add", limit=1)

    def z_move(bits):
        return lambda v: dp_swap(v, lambda c, z, k: (c, z ^ bits, k))

    kept, gain_part, *parts = small_call(
        split_kernel, [ROWS32, LINE, quarter, quarter, quarter], (dh_own, gp, other_core(dh_oth)), "split"
    )
    far, near, other = other_y(parts[1], 2), other_y(parts[0], 1), other_y(parts[2], 3)
    gain_part, got_out = order.take(gain_part, other_core(oth_out))
    gain_part = butterfly(gain_part, *[z_move(bits) for bits in range(1, 8)])
    near, far, other, gain_part = order.take(near, far, other, gain_part)
    kept, sent, gain_part = small_call(
        sum_kernel, [ROWS32, quarter, LINE], (kept, gain_part, near, far, other), "sum"
    )
    crossed = other_high(sent)
    gain_part = butterfly(gain_part, *[lambda v, bits=bits: other_y(v, bits) for bits in (1, 2, 3)])
    dh, gain_part = small_call(last_kernel, [quarter, LINE], (kept, crossed, gain_part), "last")
    far, near, other = other_y(dh, 2), other_y(dh, 1), other_y(dh, 3)
    gain_part = butterfly(butterfly(gain_part, other_column), other_high)
    dhs = [dh, near, far, other]
    section_out = put_out(0, flag, own_out, got_out, [enc_out], "rows")
    section_grad = put_out(F, flag, own_out, got_out, dhs, "grads")
    return (section_out[None], section_grad[None], gain_part.reshape(D))


def solution(mesh):
    return jax.shard_map(
        on_device,
        mesh=mesh,
        in_specs=(
            P("section", "dp", None),
            P("section", "dp", None),
            P("section", "dp", None),
            P(),
            P(),
        ),
        out_specs=(P("section", "dp", None), P("section", "dp", None), P()),
        check_vma=False,
    )
```

```python
import functools
import math

import jax
import jax.numpy as jnp
from jax import lax
from jax.experimental import pallas as pl
from jax.experimental.pallas import tpu as pltpu
from jax.sharding import PartitionSpec as P

HEAD = 256
LEN = 256
D = 2048
HALF = 4
F = HALF * HEAD
QUARTER = LEN // 4
PIECE = LEN // 2

eps = 1e-06
bf16 = jnp.bfloat16
f32 = jnp.float32

SLOTS = (
    (0, 0), (0, 1), (0, -1), (1, 0), (0, 2), (0, -2), (1, 1), (0, 3),
    (0, -3), (1, -2), (0, 4), (1, 2), (1, -3), (1, 3), (1, -1), (1, 4),
)
N_SLOT = len(SLOTS)
SLOT = D // N_SLOT

ANY = pl.BlockSpec(memory_space=pl.ANY)
VMEM = pl.BlockSpec(memory_space=pltpu.VMEM)
SMEM = pl.BlockSpec(memory_space=pltpu.SMEM)
MIB = 1024 * 1024


def dp_swap(x, move):
    pairs = []
    for index in range(32):
        column, place, core = index // 16, (index // 2) % 8, index % 2
        column, place, core = move(column, place, core)
        pairs.append((index, (column % 2) * 16 + (place % 8) * 2 + core % 2))
    return lax.ppermute(x, "dp", pairs)


def section_swap(x, move):
    pairs = []
    for index in range(8):
        high, y = move(index // 4, index % 4)
        pairs.append((index, (high % 2) * 4 + y % 4))
    return lax.ppermute(x, "section", pairs)


def other_core(x):
    return dp_swap(x, lambda c, z, k: (c, z, k + 1))


def other_column(x):
    return dp_swap(x, lambda c, z, k: (c + 1, z, k))


def from_above(x):
    return dp_swap(x, lambda c, z, k: (c, z - 1, k))


def from_below(x):
    return dp_swap(x, lambda c, z, k: (c, z + 1, k))


def other_high(x):
    return section_swap(x, lambda h, y: (h + 1, y))


def other_y(x, bits):
    return section_swap(x, lambda h, y: (h, y ^ bits))


def join_kernel(*refs):
    del refs


class Order:
    def __init__(self, token):
        self.token = token

    def take(self, *arrays):
        arrays = arrays + (self.token,)
        count = len(arrays)
        *arrays, self.token = pl.pallas_call(
            join_kernel,
            in_specs=[ANY] * count,
            out_specs=[ANY] * count,
            out_shape=[jax.ShapeDtypeStruct(x.shape, x.dtype) for x in arrays],
            input_output_aliases={i: i for i in range(count)},
            compiler_params=pltpu.CompilerParams(vmem_limit_bytes=MIB),
            cost_estimate=pl.CostEstimate(flops=0, bytes_accessed=1024, transcendentals=0),
            name="join",
        )(*arrays)
        return arrays[0] if count == 2 else arrays


def core_index():
    return lax.axis_index("dp") % 2


def y_index():
    return lax.axis_index("section") % 4


def root_of(map_ref):
    root = jnp.int32(0)
    for index in range(8):
        root = jnp.where(map_ref[index] == 0, index, root)
    return root


def is_encoder(map_ref):
    return root_of(map_ref) == lax.axis_index("section")


def row_block(index, size):
    return pl.ds(pl.multiple_of(index * size, size), size)


def copy_all(pairs, sems):
    copies = [pltpu.make_async_copy(source, target, sems.at[i]) for i, (source, target) in enumerate(pairs)]
    for copy in copies:
        copy.start()
    for copy in copies:
        copy.wait()


def columns_kernel(w_ref, keep_ref, give_ref, token_ref, sems):
    core = core_index()
    token_ref[...] = jnp.zeros_like(token_ref)
    copy_all([
        (w_ref.at[:, row_block(side * 2 + which, F)], ref.at[:, pl.ds(side * F, F)])
        for ref, which in ((give_ref, 1 - core), (keep_ref, core))
        for side in range(2)
    ], sems)


def unit_kernel(keep_ref, got_ref, unit_ref, sems):
    core = core_index()
    copy_all([
        (keep_ref, unit_ref.at[row_block(core, SLOT // 2), :]),
        (got_ref, unit_ref.at[row_block(1 - core, SLOT // 2), :]),
    ], sems)


def half_kernel(rows_ref, half_ref, sems):
    copy_all([(rows_ref.at[row_block((y_index() // 2) ^ 1, 2 * QUARTER), :], half_ref)], sems)


def give_kernel(rows_ref, cot_ref, token_ref, give_ref, sems):
    del token_ref
    cols = row_block(1 - core_index(), F)
    copy_all([
        (rows_ref.at[:, cols], give_ref.at[:, pl.ds(0, F)]),
        (cot_ref.at[:, cols], give_ref.at[:, pl.ds(F, F)]),
    ], sems)


def butterfly_kernel(a_ref, b_ref, c_ref, d_ref, out_ref):
    out_ref[...] = (a_ref[...] + b_ref[...]) + (c_ref[...] + d_ref[...])


def select_kernel(step, map_ref, own_ref, got_ref, *outs):
    y, root = y_index(), root_of(map_ref)
    if step == 0:
        mine = y // 2 == root % 4 // 2
        keep_ref, send_ref = outs
        for ref, quarter in ((keep_ref, y), (send_ref, y ^ 1)):
            ref[...] = jnp.where(mine, own_ref[row_block(quarter, QUARTER), :], got_ref[row_block(quarter % 2, QUARTER), :])
    elif step == 1:
        outs[0][...] = jnp.where(y % 2 == root % 2, own_ref[...], got_ref[...])
    else:
        outs[0][...] = jnp.where(lax.axis_index("section") // 4 == root // 4, own_ref[...], got_ref[...])


def stack_kernel(*refs):
    *parts, out_ref = refs
    rows = out_ref.shape[0] // len(parts)
    for index, part in enumerate(parts):
        out_ref[index * rows:(index + 1) * rows, :] = part[...]


def late_kernel(a_ref, token_ref, out_ref):
    del token_ref
    out_ref[...] = a_ref[...]


def add_kernel(a_ref, b_ref, out_ref):
    out_ref[...] = a_ref[...] + b_ref[...]


def slot_column(column, offset):
    dp = lax.axis_index("dp")
    column = (dp // 16 + column) % 2
    place = ((dp // 2) % 8 + offset + 8) % 8
    return pl.multiple_of((column * 8 + place) * SLOT, SLOT)


def norm_block(ref, gain_ref, enc_ref, inv_ref):
    @pl.loop(0, PIECE // QUARTER)
    def _(block):
        rows = row_block(block, QUARTER)
        hidden = ref[rows, :].astype(f32)
        inv = lax.rsqrt(jnp.mean(hidden * hidden, axis=1, keepdims=True) + eps)
        inv_ref[rows, :] = jnp.broadcast_to(inv, (QUARTER, 128))
        for slot in range(N_SLOT):
            cols = pl.ds(slot_column(*SLOTS[slot]), SLOT)
            part = ref[rows, cols].astype(f32)
            enc_ref[rows, slot * SLOT:(slot + 1) * SLOT] = (part * inv * gain_ref[:, cols]).astype(bf16)


def norm_kernel(gain_ref, *refs):
    count = len(refs) // 3
    for index in range(count):
        norm_block(refs[index], gain_ref, refs[count + 2 * index], refs[count + 2 * index + 1])


def encoder_kernel(map_ref, gain_ref, cot_ref, a_ref, b_ref, dh_ref, gp_ref, full_ref, flag_ref):
    flag_ref[...] = jnp.where(is_encoder(map_ref), 1.0, 0.0) * jnp.ones_like(flag_ref)

    @pl.when(is_encoder(map_ref))
    def _():
        y = y_index()
        gain = gain_ref[...]
        gp_ref[...] = jnp.zeros_like(gp_ref)
        for index, ref in enumerate((a_ref, b_ref)):

            @pl.loop(0, PIECE // QUARTER)
            def _(block):
                quarter = index * (PIECE // QUARTER) + block
                rows = row_block(quarter, QUARTER)
                place = row_block(y ^ quarter, QUARTER)
                g = cot_ref[place, :].astype(f32)
                hidden = ref[row_block(block, QUARTER), :].astype(f32)
                inv = lax.rsqrt(jnp.mean(hidden * hidden, axis=1, keepdims=True) + eps)
                full_ref[place, :] = (hidden * inv * gain).astype(bf16)
                mean = jnp.mean(hidden * gain * g, axis=1, keepdims=True)
                dh_ref[rows, :] = (inv * gain * g - hidden * (inv * inv * inv * mean)).astype(bf16)
                gp_ref[...] += jnp.sum(g * hidden * inv, axis=0, keepdims=True)


NT = (((1,), (1,)), ((), ()))
TN = (((0,), (0,)), ((), ()))
SCALE = 1.0 / math.sqrt(HEAD)


def main_kernel(*refs):
    units = refs[:N_SLOT]
    encs, hids, invs = refs[N_SLOT:N_SLOT + 4], refs[N_SLOT + 4:N_SLOT + 8], refs[N_SLOT + 8:N_SLOT + 12]
    (map_ref, rows_ref, cot_ref, qg_oth, gain_ref, dh_enc, gp_enc,
     own_out, oth_out, dh_own, dh_oth, gp_ref, dkv, mean_ref) = refs[N_SLOT + 12:]
    mean_ref[...] = jnp.zeros_like(mean_ref)

    @pl.loop(0, HALF)
    def _(head):
        cols, vcols = row_block(head, HEAD), row_block(HALF + head, HEAD)
        mine = row_block(core_index() * HALF + head, HEAD)
        both = []
        for at in (cols, vcols):
            w = jnp.concatenate([unit[:, at] for unit in units], axis=0)
            enc = jnp.concatenate([ref[...] for ref in encs], axis=0)
            both.append(jnp.dot(enc, w, preferred_element_type=f32).astype(bf16))
        rows = (slice(0, LEN), slice(LEN, 2 * LEN))
        k = [both[0][at] for at in rows]
        v = [both[1][at] for at in rows]
        q = (rows_ref[:, mine], qg_oth[:, cols])
        g = (cot_ref[:, mine], qg_oth[:, vcols])
        two = range(2)
        scores = [lax.dot_general(k[i], q[i], NT, preferred_element_type=f32) * SCALE for i in two]
        dprobs = [lax.dot_general(v[i], g[i], NT, preferred_element_type=f32) for i in two]
        e = [jnp.exp(x - jnp.max(x, axis=0, keepdims=True)) for x in scores]
        probs = [x * (1.0 / jnp.sum(x, axis=0, keepdims=True)) for x in e]
        rounded = [x.astype(bf16) for x in probs]
        delta = [jnp.sum(rounded[i].astype(f32) * dprobs[i], axis=0, keepdims=True) for i in two]
        dscores = [(probs[i] * (dprobs[i] - delta[i])).astype(bf16) for i in two]
        context = [lax.dot_general(rounded[i], v[i], TN, preferred_element_type=f32) for i in two]
        dv = [jnp.dot(rounded[i], g[i], preferred_element_type=f32).astype(bf16) for i in two]
        dk = [(jnp.dot(dscores[i], q[i], preferred_element_type=f32) * SCALE).astype(bf16) for i in two]
        dq = [lax.dot_general(dscores[i], k[i], TN, preferred_element_type=f32) * SCALE for i in two]
        for i, out in enumerate((own_out, oth_out)):
            out[:, cols] = context[i].astype(bf16)
            out[:, vcols] = dq[i].astype(bf16)
            dkv[rows[i], cols] = dk[i]
            dkv[rows[i], vcols] = dv[i]
            term = dk[i].astype(f32) * k[i].astype(f32) + dv[i].astype(f32) * v[i].astype(f32)
            mean_ref[rows[i], :] += term[:, :128] + term[:, 128:]

    inv = jnp.concatenate([ref[:, :1] for ref in invs], axis=0)
    factor = inv * inv * (jnp.sum(mean_ref[...], axis=1, keepdims=True) * (1.0 / D))

    @pl.when(jnp.logical_not(is_encoder(map_ref)))
    def _():
        for block in range(N_SLOT // 2):
            w = jnp.concatenate([units[2 * block][...], units[2 * block + 1][...]], axis=0)
            denc = lax.dot_general(dkv[...], w, NT, preferred_element_type=f32)
            for side in range(2):
                cols = pl.ds(slot_column(*SLOTS[2 * block + side]), SLOT)
                total = jnp.zeros((1, SLOT), f32)
                for index, hid in enumerate(hids):
                    rows = slice(index * PIECE, (index + 1) * PIECE)
                    at = slice(index % 2 * PIECE, (index % 2 + 1) * PIECE)
                    out = (dh_own, dh_oth)[index // 2]
                    hidden = hid[:, cols].astype(f32)
                    scaled = inv[rows] * denc[rows, side * SLOT:(side + 1) * SLOT]
                    out[at, cols] = (gain_ref[:, cols] * scaled - hidden * factor[rows]).astype(bf16)
                    total = total + jnp.sum(scaled * hidden, axis=0, keepdims=True)
                gp_ref[:, cols] = total

    @pl.when(is_encoder(map_ref))
    def _():
        dh_oth[...] = jnp.zeros_like(dh_oth)
        dh_own[...] = dh_enc[...]
        gp_ref[...] = gp_enc[...]

    dh_oth[LEN:, :] = two_rows(gp_ref[...])


def two_rows(x):
    high = x.astype(bf16).astype(f32)
    index = lax.broadcasted_iota(jnp.int32, (16, x.shape[1]), 0)
    rows = jnp.where(index == 0, high, jnp.where(index == 1, x - high, 0.0))
    return rows.astype(bf16)


def one_row(rows):
    return rows[0:1, :].astype(f32) + rows[1:2, :].astype(f32)


def attend(units, pieces, where, *args):
    whole = jax.ShapeDtypeStruct((LEN, D), bf16)
    return pl.pallas_call(
        main_kernel,
        in_specs=[VMEM] * (N_SLOT + 12) + [SMEM] + [VMEM] * 6,
        out_specs=[VMEM] * 5,
        out_shape=[
            whole, whole, whole, jax.ShapeDtypeStruct((LEN + 16, D), bf16), jax.ShapeDtypeStruct((1, D), f32)
        ],
        scratch_shapes=[
            pltpu.VMEM((2 * LEN, 2 * F), bf16),
            pltpu.VMEM((2 * LEN, 128), f32),
        ],
        compiler_params=pltpu.CompilerParams(vmem_limit_bytes=16 * MIB),
        cost_estimate=pl.CostEstimate(flops=10_000_000_000, bytes_accessed=20_000_000, transcendentals=600_000),
        name="attend",
    )(*units, *pieces, where, *args)


def small_call(kernel, out_shape, args, name, limit=6, where=None):
    first = () if where is None else (where,)
    return pl.pallas_call(
        kernel,
        in_specs=[SMEM] * len(first) + [VMEM] * len(args),
        out_specs=jax.tree.map(lambda _: VMEM, out_shape),
        out_shape=out_shape,
        compiler_params=pltpu.CompilerParams(vmem_limit_bytes=limit * MIB),
        cost_estimate=pl.CostEstimate(flops=0, bytes_accessed=1024, transcendentals=0),
        name=name,
    )(*first, *args)


def copy_call(kernel, out_shape, args, name, count):
    return pl.pallas_call(
        kernel,
        in_specs=[ANY] * len(args),
        out_specs=jax.tree.map(lambda x: VMEM if x.dtype == f32 else ANY, out_shape),
        out_shape=out_shape,
        scratch_shapes=[pltpu.SemaphoreType.DMA((count,))],
        compiler_params=pltpu.CompilerParams(vmem_limit_bytes=MIB),
        cost_estimate=pl.CostEstimate(flops=0, bytes_accessed=1024, transcendentals=0),
        name=name,
    )(*args)


def bf16_rows(rows):
    return jax.ShapeDtypeStruct((rows, D), bf16)


ROWS32 = jax.ShapeDtypeStruct((QUARTER, D), f32)
LINE = jax.ShapeDtypeStruct((1, D), f32)


def split_kernel(own_ref, gp_ref, got_ref, kept_ref, gain_ref, *sent):
    gain_ref[...] = one_row(two_rows(gp_ref[...])) + one_row(got_ref[LEN:, :])
    for step in range(4):
        at = slice(step * QUARTER, (step + 1) * QUARTER)
        part = own_ref[at, :].astype(f32) + got_ref[at, :].astype(f32)
        if step == 0:
            kept_ref[...] = part
        else:
            sent[step - 1][...] = part.astype(bf16)


def sum_kernel(kept_ref, gain_ref, a_ref, b_ref, c_ref, sum_ref, sent_ref, gain_out):
    total = kept_ref[...] + (a_ref[...].astype(f32) + b_ref[...].astype(f32) + c_ref[...].astype(f32))
    sum_ref[...] = total
    sent_ref[...] = total.astype(bf16)
    gain_out[...] = gain_ref[...]


def last_kernel(sum_ref, got_ref, gain_ref, dh_ref, gain_out):
    gain_out[...] = gain_ref[...]
    dh_ref[...] = (sum_ref[...] + got_ref[...].astype(f32)).astype(bf16)


def out_kernel(offset, flag_ref, own_ref, oth_ref, *refs):
    *parts, out_ref, sems = refs
    core, y = core_index(), y_index()
    rows = LEN // len(parts)

    encoder = jnp.max(flag_ref[...]) > 0.5

    @pl.when(jnp.logical_not(encoder))
    def _():
        copies = [
            pltpu.make_async_copy(
                ref.at[:, pl.ds(offset, F)],
                out_ref.at[:, pl.ds(pl.multiple_of(place * F, F), F)],
                sems.at[index],
            )
            for index, (ref, place) in enumerate(((own_ref, core), (oth_ref, 1 - core)))
        ]
        for copy in copies:
            copy.start()
        for copy in copies:
            copy.wait()

    @pl.when(encoder)
    def _():
        copies = []
        for index, part in enumerate(parts):
            start = 0 if len(parts) == 1 else pl.multiple_of((y ^ index) * rows, rows)
            copies.append(
                pltpu.make_async_copy(part, out_ref.at[pl.ds(start, rows), :], sems.at[index])
            )
        for copy in copies:
            copy.start()
        for copy in copies:
            copy.wait()


def put_out(offset, where, own, oth, parts, name):
    return pl.pallas_call(
        functools.partial(out_kernel, offset),
        in_specs=[VMEM] + [ANY] * (2 + len(parts)),
        out_specs=ANY,
        out_shape=jax.ShapeDtypeStruct((LEN, D), bf16),
        scratch_shapes=[pltpu.SemaphoreType.DMA((4,))],
        compiler_params=pltpu.CompilerParams(vmem_limit_bytes=MIB),
        cost_estimate=pl.CostEstimate(flops=0, bytes_accessed=2_000_000, transcendentals=0),
        name=name,
    )(where, own, oth, *parts)


def on_device(section_rows, kv_weight, cotangent, gain, section_map):
    rows, cot, weight, gain = section_rows[0], cotangent[0], kv_weight[0], gain[None]
    quarter = bf16_rows(QUARTER)

    def select(step, own, got):
        outs = [quarter, quarter] if step == 0 else quarter
        kernel = functools.partial(select_kernel, step)
        return small_call(kernel, outs, (own, got), "select", limit=3, where=section_map)

    keep, give, token = copy_call(
        columns_kernel,
        [bf16_rows(SLOT // 2), bf16_rows(SLOT // 2), jax.ShapeDtypeStruct((8, 128), f32)],
        (weight,), "columns", 4,
    )
    order = Order(token)
    got = other_core(give)
    hidden = other_y(copy_call(half_kernel, bf16_rows(2 * QUARTER), (rows,), "half", 1), 2)
    a, b = {0: copy_call(unit_kernel, bf16_rows(SLOT), (keep, got), "unit", 2)}, {}
    up, down, across = from_above(a[0]), from_below(a[0]), other_column(a[0])
    qg_oth = other_core(copy_call(give_kernel, bf16_rows(LEN), (rows, cot, a[0]), "give", 2))

    a[1], qg_oth = order.take(up, qg_oth)
    up, across_1 = from_above(a[1]), other_column(a[1])
    a[-1] = order.take(down)
    down = from_below(a[-1])
    hidden = order.take(hidden)
    mine, send = select(0, rows, hidden)
    hidden = other_y(send, 1)
    b[0] = order.take(across)
    hidden = order.take(hidden)
    mine = select(1, mine, hidden)
    hidden = other_high(mine)

    a[2] = order.take(up)
    up = from_above(a[2])
    a[-2] = order.take(down)
    down, across_2 = from_below(a[-2]), other_column(a[-2])
    b[1] = order.take(across_1)
    hidden = order.take(hidden)
    mine = select(2, mine, hidden)
    hidden = other_y(mine, 1)

    a[3] = order.take(up)
    up = from_above(b[1])
    a[-3] = order.take(down)
    down, across_3 = from_below(a[-3]), other_column(a[-3])
    b[-2] = order.take(across_2)
    hidden = order.take(hidden)
    own_a = small_call(stack_kernel, bf16_rows(PIECE), (mine, hidden), "stack", limit=3)
    hidden = other_y(own_a, 2)

    a[4] = order.take(down)
    down, across_4 = from_below(b[0]), other_column(a[4])
    b[2] = order.take(up)
    up = from_above(b[2])
    b[-3] = order.take(across_3)
    own_b = order.take(hidden)
    late_a = small_call(late_kernel, bf16_rows(PIECE), (own_a, order.token), "late", limit=3)
    oth_a, oth_b = other_core(late_a), other_core(own_b)
    b[3] = order.take(up)
    b[-1] = order.take(down)
    b[4] = order.take(across_4)
    oth_a, oth_b = order.take(oth_a, oth_b)
    units = [(a, b)[column][offset] for column, offset in SLOTS]

    def normalise(*pieces):
        outs = [bf16_rows(PIECE), jax.ShapeDtypeStruct((PIECE, 128), f32)] * len(pieces)
        return small_call(norm_kernel, outs, (gain, *pieces), "norm")

    enc_0, inv_0, enc_1, inv_1 = normalise(own_a, own_b)
    enc_2, inv_2, enc_3, inv_3 = normalise(oth_a, oth_b)
    dh_enc, gp_enc, enc_out, flag = small_call(
        encoder_kernel, [bf16_rows(LEN), LINE, bf16_rows(LEN), jax.ShapeDtypeStruct((8, 128), f32)],
        (gain, cot, own_a, own_b), "encoder", where=section_map,
    )
    pieces = (enc_0, enc_1, enc_2, enc_3, own_a, own_b, oth_a, oth_b, inv_0, inv_1, inv_2, inv_3)
    own_out, oth_out, dh_own, dh_oth, gp = attend(
        units, pieces, section_map, rows, cot, qg_oth, gain, dh_enc, gp_enc
    )

    def add_from(part, *moves):
        for move in moves:
            part = small_call(add_kernel, LINE, (part, move(part)), "add", limit=1)
        return part

    def butterfly(part, *moves):
        return small_call(butterfly_kernel, LINE, (part, *[move(part) for move in moves]), "add", limit=1)

    def z_move(bits):
        return lambda v: dp_swap(v, lambda c, z, k: (c, z ^ bits, k))

    kept, gain_part, *parts = small_call(
        split_kernel, [ROWS32, LINE, quarter, quarter, quarter], (dh_own, gp, other_core(dh_oth)), "split"
    )
    far, near, other = other_y(parts[1], 2), other_y(parts[0], 1), other_y(parts[2], 3)
    gain_part, got_out = order.take(gain_part, other_core(oth_out))
    gain_part = butterfly(gain_part, *[z_move(bits) for bits in (1, 2, 3)])
    gain_part = add_from(gain_part, z_move(4))
    near, far, other, gain_part = order.take(near, far, other, gain_part)
    kept, sent, gain_part = small_call(
        sum_kernel, [ROWS32, quarter, LINE], (kept, gain_part, near, far, other), "sum"
    )
    crossed = other_high(sent)
    gain_part = butterfly(gain_part, *[lambda v, bits=bits: other_y(v, bits) for bits in (1, 2, 3)])
    dh, gain_part = small_call(last_kernel, [quarter, LINE], (kept, crossed, gain_part), "last")
    far, near, other = other_y(dh, 2), other_y(dh, 1), other_y(dh, 3)
    gain_part = add_from(gain_part, other_column)
    gain_part = add_from(gain_part, other_high)
    dhs = [dh, near, far, other]
    section_out = put_out(0, flag, own_out, got_out, [enc_out], "rows")
    section_grad = put_out(F, flag, own_out, got_out, dhs, "grads")
    return (section_out[None], section_grad[None], gain_part.reshape(D))


def solution(mesh):
    return jax.shard_map(
        on_device,
        mesh=mesh,
        in_specs=(
            P("section", "dp", None),
            P("section", "dp", None),
            P("section", "dp", None),
            P(),
            P(),
        ),
        out_specs=(P("section", "dp", None), P("section", "dp", None), P()),
        check_vma=False,
    )
```

```python
import functools
import math

import jax
import jax.numpy as jnp
from jax import lax
from jax.experimental import pallas as pl
from jax.experimental.pallas import tpu as pltpu
from jax.sharding import PartitionSpec as P

HEAD = 256
LEN = 256
D = 2048
HALF = 4
F = HALF * HEAD
QUARTER = LEN // 4
PIECE = LEN // 2

eps = 1e-06
bf16 = jnp.bfloat16
f32 = jnp.float32

SLOTS = (
    (0, 0), (0, 1), (0, -1), (1, 0), (0, 2), (0, -2), (1, 1), (0, 3),
    (0, -3), (1, -2), (0, 4), (1, 2), (1, -3), (1, 3), (1, -1), (1, 4),
)
N_SLOT = len(SLOTS)
SLOT = D // N_SLOT

ANY = pl.BlockSpec(memory_space=pl.ANY)
VMEM = pl.BlockSpec(memory_space=pltpu.VMEM)
SMEM = pl.BlockSpec(memory_space=pltpu.SMEM)
MIB = 1024 * 1024


def dp_swap(x, move):
    pairs = []
    for index in range(32):
        column, place, core = index // 16, (index // 2) % 8, index % 2
        column, place, core = move(column, place, core)
        pairs.append((index, (column % 2) * 16 + (place % 8) * 2 + core % 2))
    return lax.ppermute(x, "dp", pairs)


def section_swap(x, move):
    pairs = []
    for index in range(8):
        high, y = move(index // 4, index % 4)
        pairs.append((index, (high % 2) * 4 + y % 4))
    return lax.ppermute(x, "section", pairs)


def other_core(x):
    return dp_swap(x, lambda c, z, k: (c, z, k + 1))


def other_column(x):
    return dp_swap(x, lambda c, z, k: (c + 1, z, k))


def from_above(x):
    return dp_swap(x, lambda c, z, k: (c, z - 1, k))


def from_below(x):
    return dp_swap(x, lambda c, z, k: (c, z + 1, k))


def other_high(x):
    return section_swap(x, lambda h, y: (h + 1, y))


def other_y(x, bits):
    return section_swap(x, lambda h, y: (h, y ^ bits))


def join_kernel(*refs):
    del refs


class Order:
    def __init__(self, token):
        self.token = token

    def take(self, *arrays):
        arrays = arrays + (self.token,)
        count = len(arrays)
        *arrays, self.token = pl.pallas_call(
            join_kernel,
            in_specs=[ANY] * count,
            out_specs=[ANY] * count,
            out_shape=[jax.ShapeDtypeStruct(x.shape, x.dtype) for x in arrays],
            input_output_aliases={i: i for i in range(count)},
            compiler_params=pltpu.CompilerParams(vmem_limit_bytes=MIB),
            cost_estimate=pl.CostEstimate(flops=0, bytes_accessed=1024, transcendentals=0),
            name="join",
        )(*arrays)
        return arrays[0] if count == 2 else arrays


def core_index():
    return lax.axis_index("dp") % 2


def y_index():
    return lax.axis_index("section") % 4


def root_of(map_ref):
    root = jnp.int32(0)
    for index in range(8):
        root = jnp.where(map_ref[index] == 0, index, root)
    return root


def is_encoder(map_ref):
    return root_of(map_ref) == lax.axis_index("section")


def row_block(index, size):
    return pl.ds(pl.multiple_of(index * size, size), size)


def copy_all(pairs, sems):
    copies = [pltpu.make_async_copy(source, target, sems.at[i]) for i, (source, target) in enumerate(pairs)]
    for copy in copies:
        copy.start()
    for copy in copies:
        copy.wait()


def columns_kernel(w_ref, keep_ref, give_ref, token_ref, sems):
    core = core_index()
    token_ref[...] = jnp.zeros_like(token_ref)
    copy_all([
        (w_ref.at[:, row_block(side * 2 + which, F)], ref.at[:, pl.ds(side * F, F)])
        for ref, which in ((give_ref, 1 - core), (keep_ref, core))
        for side in range(2)
    ], sems)


def unit_kernel(keep_ref, got_ref, unit_ref, sems):
    core = core_index()
    copy_all([
        (keep_ref, unit_ref.at[row_block(core, SLOT // 2), :]),
        (got_ref, unit_ref.at[row_block(1 - core, SLOT // 2), :]),
    ], sems)


def half_kernel(rows_ref, half_ref, sems):
    copy_all([(rows_ref.at[row_block((y_index() // 2) ^ 1, 2 * QUARTER), :], half_ref)], sems)


def give_kernel(rows_ref, cot_ref, token_ref, give_ref, sems):
    del token_ref
    cols = row_block(1 - core_index(), F)
    copy_all([
        (rows_ref.at[:, cols], give_ref.at[:, pl.ds(0, F)]),
        (cot_ref.at[:, cols], give_ref.at[:, pl.ds(F, F)]),
    ], sems)


def butterfly_kernel(a_ref, b_ref, c_ref, d_ref, out_ref):
    out_ref[...] = (a_ref[...] + b_ref[...]) + (c_ref[...] + d_ref[...])


def select_kernel(step, map_ref, own_ref, got_ref, *outs):
    y, root = y_index(), root_of(map_ref)
    if step == 0:
        mine = y // 2 == root % 4 // 2
        keep_ref, send_ref = outs
        for ref, quarter in ((keep_ref, y), (send_ref, y ^ 1)):
            ref[...] = jnp.where(mine, own_ref[row_block(quarter, QUARTER), :], got_ref[row_block(quarter % 2, QUARTER), :])
    elif step == 1:
        outs[0][...] = jnp.where(y % 2 == root % 2, own_ref[...], got_ref[...])
    else:
        outs[0][...] = jnp.where(lax.axis_index("section") // 4 == root // 4, own_ref[...], got_ref[...])


def stack_kernel(*refs):
    *parts, out_ref = refs
    rows = out_ref.shape[0] // len(parts)
    for index, part in enumerate(parts):
        out_ref[index * rows:(index + 1) * rows, :] = part[...]


def late_kernel(a_ref, token_ref, out_ref):
    del token_ref
    out_ref[...] = a_ref[...]


def add_kernel(a_ref, b_ref, out_ref):
    out_ref[...] = a_ref[...] + b_ref[...]


def slot_column(column, offset):
    dp = lax.axis_index("dp")
    column = (dp // 16 + column) % 2
    place = ((dp // 2) % 8 + offset + 8) % 8
    return pl.multiple_of((column * 8 + place) * SLOT, SLOT)


def norm_block(ref, gain_ref, enc_ref, inv_ref):
    @pl.loop(0, PIECE // QUARTER)
    def _(block):
        rows = row_block(block, QUARTER)
        hidden = ref[rows, :].astype(f32)
        inv = lax.rsqrt(jnp.mean(hidden * hidden, axis=1, keepdims=True) + eps)
        inv_ref[rows, :] = jnp.broadcast_to(inv, (QUARTER, 128))
        for slot in range(N_SLOT):
            cols = pl.ds(slot_column(*SLOTS[slot]), SLOT)
            part = ref[rows, cols].astype(f32)
            enc_ref[rows, slot * SLOT:(slot + 1) * SLOT] = (part * inv * gain_ref[:, cols]).astype(bf16)


def norm_kernel(gain_ref, *refs):
    count = len(refs) // 3
    for index in range(count):
        norm_block(refs[index], gain_ref, refs[count + 2 * index], refs[count + 2 * index + 1])


def encoder_kernel(map_ref, gain_ref, cot_ref, a_ref, b_ref, dh_ref, gp_ref, full_ref, flag_ref):
    flag_ref[...] = jnp.where(is_encoder(map_ref), 1.0, 0.0) * jnp.ones_like(flag_ref)

    @pl.when(is_encoder(map_ref))
    def _():
        y = y_index()
        gain = gain_ref[...]
        gp_ref[...] = jnp.zeros_like(gp_ref)
        for index, ref in enumerate((a_ref, b_ref)):

            @pl.loop(0, PIECE // QUARTER)
            def _(block):
                quarter = index * (PIECE // QUARTER) + block
                rows = row_block(quarter, QUARTER)
                place = row_block(y ^ quarter, QUARTER)
                g = cot_ref[place, :].astype(f32)
                hidden = ref[row_block(block, QUARTER), :].astype(f32)
                inv = lax.rsqrt(jnp.mean(hidden * hidden, axis=1, keepdims=True) + eps)
                full_ref[place, :] = (hidden * inv * gain).astype(bf16)
                mean = jnp.mean(hidden * gain * g, axis=1, keepdims=True)
                dh_ref[rows, :] = (inv * gain * g - hidden * (inv * inv * inv * mean)).astype(bf16)
                gp_ref[...] += jnp.sum(g * hidden * inv, axis=0, keepdims=True)


NT = (((1,), (1,)), ((), ()))
TN = (((0,), (0,)), ((), ()))
SCALE = 1.0 / math.sqrt(HEAD)


def main_kernel(*refs):
    units = refs[:N_SLOT]
    encs, hids, invs = refs[N_SLOT:N_SLOT + 4], refs[N_SLOT + 4:N_SLOT + 8], refs[N_SLOT + 8:N_SLOT + 12]
    (flag_ref, rows_ref, cot_ref, qg_oth, gain_ref, dh_enc, gp_enc,
     own_out, oth_out, dh_own, dh_oth, gp_ref, dkv, mean_ref) = refs[N_SLOT + 12:]
    mean_ref[...] = jnp.zeros_like(mean_ref)

    @pl.loop(0, HALF)
    def _(head):
        cols, vcols = row_block(head, HEAD), row_block(HALF + head, HEAD)
        mine = row_block(core_index() * HALF + head, HEAD)
        both = []
        for at in (cols, vcols):
            w = jnp.concatenate([unit[:, at] for unit in units], axis=0)
            enc = jnp.concatenate([ref[...] for ref in encs], axis=0)
            both.append(jnp.dot(enc, w, preferred_element_type=f32).astype(bf16))
        rows = (slice(0, LEN), slice(LEN, 2 * LEN))
        k = [both[0][at] for at in rows]
        v = [both[1][at] for at in rows]
        q = (rows_ref[:, mine], qg_oth[:, cols])
        g = (cot_ref[:, mine], qg_oth[:, vcols])
        two = range(2)
        scores = [lax.dot_general(k[i], q[i], NT, preferred_element_type=f32) * SCALE for i in two]
        dprobs = [lax.dot_general(v[i], g[i], NT, preferred_element_type=f32) for i in two]
        e = [jnp.exp(x - jnp.max(x, axis=0, keepdims=True)) for x in scores]
        probs = [x * (1.0 / jnp.sum(x, axis=0, keepdims=True)) for x in e]
        rounded = [x.astype(bf16) for x in probs]
        delta = [jnp.sum(rounded[i].astype(f32) * dprobs[i], axis=0, keepdims=True) for i in two]
        dscores = [(probs[i] * (dprobs[i] - delta[i])).astype(bf16) for i in two]
        context = [lax.dot_general(rounded[i], v[i], TN, preferred_element_type=f32) for i in two]
        dv = [jnp.dot(rounded[i], g[i], preferred_element_type=f32).astype(bf16) for i in two]
        dk = [(jnp.dot(dscores[i], q[i], preferred_element_type=f32) * SCALE).astype(bf16) for i in two]
        dq = [lax.dot_general(dscores[i], k[i], TN, preferred_element_type=f32) * SCALE for i in two]
        for i, out in enumerate((own_out, oth_out)):
            out[:, cols] = context[i].astype(bf16)
            out[:, vcols] = dq[i].astype(bf16)
            dkv[rows[i], cols] = dk[i]
            dkv[rows[i], vcols] = dv[i]
            term = dk[i].astype(f32) * k[i].astype(f32) + dv[i].astype(f32) * v[i].astype(f32)
            mean_ref[rows[i], :] += term[:, :128] + term[:, 128:]

    inv = jnp.concatenate([ref[:, :1] for ref in invs], axis=0)
    factor = inv * inv * (jnp.sum(mean_ref[...], axis=1, keepdims=True) * (1.0 / D))

    encoder = jnp.max(flag_ref[...]) > 0.5

    @pl.when(jnp.logical_not(encoder))
    def _():
        for block in range(N_SLOT // 2):
            w = jnp.concatenate([units[2 * block][...], units[2 * block + 1][...]], axis=0)
            denc = lax.dot_general(dkv[...], w, NT, preferred_element_type=f32)
            for side in range(2):
                cols = pl.ds(slot_column(*SLOTS[2 * block + side]), SLOT)
                total = jnp.zeros((1, SLOT), f32)
                for index, hid in enumerate(hids):
                    rows = slice(index * PIECE, (index + 1) * PIECE)
                    at = slice(index % 2 * PIECE, (index % 2 + 1) * PIECE)
                    out = (dh_own, dh_oth)[index // 2]
                    hidden = hid[:, cols].astype(f32)
                    scaled = inv[rows] * denc[rows, side * SLOT:(side + 1) * SLOT]
                    out[at, cols] = (gain_ref[:, cols] * scaled - hidden * factor[rows]).astype(bf16)
                    total = total + jnp.sum(scaled * hidden, axis=0, keepdims=True)
                gp_ref[:, cols] = total

    @pl.when(encoder)
    def _():
        dh_oth[...] = jnp.zeros_like(dh_oth)
        dh_own[...] = dh_enc[...]
        gp_ref[...] = gp_enc[...]

    dh_oth[LEN:, :] = two_rows(gp_ref[...])


def two_rows(x):
    high = x.astype(bf16).astype(f32)
    index = lax.broadcasted_iota(jnp.int32, (16, x.shape[1]), 0)
    rows = jnp.where(index == 0, high, jnp.where(index == 1, x - high, 0.0))
    return rows.astype(bf16)


def one_row(rows):
    return rows[0:1, :].astype(f32) + rows[1:2, :].astype(f32)


def attend(units, pieces, where, *args):
    whole = jax.ShapeDtypeStruct((LEN, D), bf16)
    return pl.pallas_call(
        main_kernel,
        in_specs=[VMEM] * (N_SLOT + 19),
        out_specs=[VMEM] * 5,
        out_shape=[
            whole, whole, whole, jax.ShapeDtypeStruct((LEN + 16, D), bf16), jax.ShapeDtypeStruct((1, D), f32)
        ],
        scratch_shapes=[
            pltpu.VMEM((2 * LEN, 2 * F), bf16),
            pltpu.VMEM((2 * LEN, 128), f32),
        ],
        compiler_params=pltpu.CompilerParams(vmem_limit_bytes=16 * MIB),
        cost_estimate=pl.CostEstimate(flops=10_000_000_000, bytes_accessed=20_000_000, transcendentals=600_000),
        name="attend",
    )(*units, *pieces, where, *args)


def small_call(kernel, out_shape, args, name, limit=6, where=None):
    first = () if where is None else (where,)
    return pl.pallas_call(
        kernel,
        in_specs=[SMEM] * len(first) + [VMEM] * len(args),
        out_specs=jax.tree.map(lambda _: VMEM, out_shape),
        out_shape=out_shape,
        compiler_params=pltpu.CompilerParams(vmem_limit_bytes=limit * MIB),
        cost_estimate=pl.CostEstimate(flops=0, bytes_accessed=1024, transcendentals=0),
        name=name,
    )(*first, *args)


def copy_call(kernel, out_shape, args, name, count):
    return pl.pallas_call(
        kernel,
        in_specs=[ANY] * len(args),
        out_specs=jax.tree.map(lambda x: VMEM if x.dtype == f32 else ANY, out_shape),
        out_shape=out_shape,
        scratch_shapes=[pltpu.SemaphoreType.DMA((count,))],
        compiler_params=pltpu.CompilerParams(vmem_limit_bytes=MIB),
        cost_estimate=pl.CostEstimate(flops=0, bytes_accessed=1024, transcendentals=0),
        name=name,
    )(*args)


def bf16_rows(rows):
    return jax.ShapeDtypeStruct((rows, D), bf16)


ROWS32 = jax.ShapeDtypeStruct((QUARTER, D), f32)
LINE = jax.ShapeDtypeStruct((1, D), f32)


def split_kernel(own_ref, gp_ref, got_ref, kept_ref, gain_ref, *sent):
    gain_ref[...] = one_row(two_rows(gp_ref[...])) + one_row(got_ref[LEN:, :])
    for step in range(4):
        at = slice(step * QUARTER, (step + 1) * QUARTER)
        part = own_ref[at, :].astype(f32) + got_ref[at, :].astype(f32)
        if step == 0:
            kept_ref[...] = part
        else:
            sent[step - 1][...] = part.astype(bf16)


def sum_kernel(kept_ref, gain_ref, a_ref, b_ref, c_ref, sum_ref, sent_ref, gain_out):
    total = kept_ref[...] + (a_ref[...].astype(f32) + b_ref[...].astype(f32) + c_ref[...].astype(f32))
    sum_ref[...] = total
    sent_ref[...] = total.astype(bf16)
    gain_out[...] = gain_ref[...]


def last_kernel(sum_ref, got_ref, gain_ref, dh_ref, gain_out):
    gain_out[...] = gain_ref[...]
    dh_ref[...] = (sum_ref[...] + got_ref[...].astype(f32)).astype(bf16)


def out_kernel(offset, flag_ref, own_ref, oth_ref, *refs):
    *parts, out_ref, sems = refs
    core, y = core_index(), y_index()
    rows = LEN // len(parts)

    encoder = jnp.max(flag_ref[...]) > 0.5

    @pl.when(jnp.logical_not(encoder))
    def _():
        copies = [
            pltpu.make_async_copy(
                ref.at[:, pl.ds(offset, F)],
                out_ref.at[:, pl.ds(pl.multiple_of(place * F, F), F)],
                sems.at[index],
            )
            for index, (ref, place) in enumerate(((own_ref, core), (oth_ref, 1 - core)))
        ]
        for copy in copies:
            copy.start()
        for copy in copies:
            copy.wait()

    @pl.when(encoder)
    def _():
        copies = []
        for index, part in enumerate(parts):
            start = 0 if len(parts) == 1 else pl.multiple_of((y ^ index) * rows, rows)
            copies.append(
                pltpu.make_async_copy(part, out_ref.at[pl.ds(start, rows), :], sems.at[index])
            )
        for copy in copies:
            copy.start()
        for copy in copies:
            copy.wait()


def put_out(offset, where, own, oth, parts, name):
    return pl.pallas_call(
        functools.partial(out_kernel, offset),
        in_specs=[VMEM] + [ANY] * (2 + len(parts)),
        out_specs=ANY,
        out_shape=jax.ShapeDtypeStruct((LEN, D), bf16),
        scratch_shapes=[pltpu.SemaphoreType.DMA((4,))],
        compiler_params=pltpu.CompilerParams(vmem_limit_bytes=MIB),
        cost_estimate=pl.CostEstimate(flops=0, bytes_accessed=2_000_000, transcendentals=0),
        name=name,
    )(where, own, oth, *parts)


def on_device(section_rows, kv_weight, cotangent, gain, section_map):
    rows, cot, weight, gain = section_rows[0], cotangent[0], kv_weight[0], gain[None]
    quarter = bf16_rows(QUARTER)

    def select(step, own, got):
        outs = [quarter, quarter] if step == 0 else quarter
        kernel = functools.partial(select_kernel, step)
        return small_call(kernel, outs, (own, got), "select", limit=3, where=section_map)

    keep, give, token = copy_call(
        columns_kernel,
        [bf16_rows(SLOT // 2), bf16_rows(SLOT // 2), jax.ShapeDtypeStruct((8, 128), f32)],
        (weight,), "columns", 4,
    )
    order = Order(token)
    got = other_core(give)
    hidden = other_y(copy_call(half_kernel, bf16_rows(2 * QUARTER), (rows,), "half", 1), 2)
    a, b = {0: copy_call(unit_kernel, bf16_rows(SLOT), (keep, got), "unit", 2)}, {}
    up, down, across = from_above(a[0]), from_below(a[0]), other_column(a[0])
    qg_oth = other_core(copy_call(give_kernel, bf16_rows(LEN), (rows, cot, a[0]), "give", 2))

    a[1], qg_oth = order.take(up, qg_oth)
    up, across_1 = from_above(a[1]), other_column(a[1])
    a[-1] = order.take(down)
    down = from_below(a[-1])
    hidden = order.take(hidden)
    mine, send = select(0, rows, hidden)
    hidden = other_y(send, 1)
    b[0] = order.take(across)
    hidden = order.take(hidden)
    mine = select(1, mine, hidden)
    hidden = other_high(mine)

    a[2] = order.take(up)
    up = from_above(a[2])
    a[-2] = order.take(down)
    down, across_2 = from_below(a[-2]), other_column(a[-2])
    b[1] = order.take(across_1)
    hidden = order.take(hidden)
    mine = select(2, mine, hidden)
    hidden = other_y(mine, 1)

    a[3] = order.take(up)
    up = from_above(b[1])
    a[-3] = order.take(down)
    down, across_3 = from_below(a[-3]), other_column(a[-3])
    b[-2] = order.take(across_2)
    hidden = order.take(hidden)
    own_a = small_call(stack_kernel, bf16_rows(PIECE), (mine, hidden), "stack", limit=3)
    hidden = other_y(own_a, 2)

    a[4] = order.take(down)
    down, across_4 = from_below(b[0]), other_column(a[4])
    b[2] = order.take(up)
    up = from_above(b[2])
    b[-3] = order.take(across_3)
    own_b = order.take(hidden)
    late_a = small_call(late_kernel, bf16_rows(PIECE), (own_a, order.token), "late", limit=3)
    oth_a, oth_b = other_core(late_a), other_core(own_b)
    b[3] = order.take(up)
    b[-1] = order.take(down)
    b[4] = order.take(across_4)
    oth_a, oth_b = order.take(oth_a, oth_b)
    units = [(a, b)[column][offset] for column, offset in SLOTS]

    def normalise(*pieces):
        outs = [bf16_rows(PIECE), jax.ShapeDtypeStruct((PIECE, 128), f32)] * len(pieces)
        return small_call(norm_kernel, outs, (gain, *pieces), "norm")

    enc_0, inv_0, enc_1, inv_1 = normalise(own_a, own_b)
    enc_2, inv_2, enc_3, inv_3 = normalise(oth_a, oth_b)
    dh_enc, gp_enc, enc_out, flag = small_call(
        encoder_kernel, [bf16_rows(LEN), LINE, bf16_rows(LEN), jax.ShapeDtypeStruct((8, 128), f32)],
        (gain, cot, own_a, own_b), "encoder", where=section_map,
    )
    pieces = (enc_0, enc_1, enc_2, enc_3, own_a, own_b, oth_a, oth_b, inv_0, inv_1, inv_2, inv_3)
    own_out, oth_out, dh_own, dh_oth, gp = attend(
        units, pieces, flag, rows, cot, qg_oth, gain, dh_enc, gp_enc
    )

    def add_from(part, *moves):
        for move in moves:
            part = small_call(add_kernel, LINE, (part, move(part)), "add", limit=1)
        return part

    def butterfly(part, *moves):
        return small_call(butterfly_kernel, LINE, (part, *[move(part) for move in moves]), "add", limit=1)

    def z_move(bits):
        return lambda v: dp_swap(v, lambda c, z, k: (c, z ^ bits, k))

    kept, gain_part, *parts = small_call(
        split_kernel, [ROWS32, LINE, quarter, quarter, quarter], (dh_own, gp, other_core(dh_oth)), "split"
    )
    far, near, other = other_y(parts[1], 2), other_y(parts[0], 1), other_y(parts[2], 3)
    gain_part, got_out = order.take(gain_part, other_core(oth_out))
    gain_part = butterfly(gain_part, *[z_move(bits) for bits in (1, 2, 3)])
    gain_part = add_from(gain_part, z_move(4))
    near, far, other, gain_part = order.take(near, far, other, gain_part)
    kept, sent, gain_part = small_call(
        sum_kernel, [ROWS32, quarter, LINE], (kept, gain_part, near, far, other), "sum"
    )
    crossed = other_high(sent)
    gain_part = butterfly(gain_part, *[lambda v, bits=bits: other_y(v, bits) for bits in (1, 2, 3)])
    dh, gain_part = small_call(last_kernel, [quarter, LINE], (kept, crossed, gain_part), "last")
    far, near, other = other_y(dh, 2), other_y(dh, 1), other_y(dh, 3)
    gain_part = add_from(gain_part, other_column)
    gain_part = add_from(gain_part, other_high)
    dhs = [dh, near, far, other]
    section_out = put_out(0, flag, own_out, got_out, [enc_out], "rows")
    section_grad = put_out(F, flag, own_out, got_out, dhs, "grads")
    return (section_out[None], section_grad[None], gain_part.reshape(D))


def solution(mesh):
    return jax.shard_map(
        on_device,
        mesh=mesh,
        in_specs=(
            P("section", "dp", None),
            P("section", "dp", None),
            P("section", "dp", None),
            P(),
            P(),
        ),
        out_specs=(P("section", "dp", None), P("section", "dp", None), P()),
        check_vma=False,
    )
```
